512 devices in a mesh: ctx: 32 (over z, y_hi), tp: 16 (over x, y_lo, core).
Axes of the slice: x: 4, y: 4 (y_hi: 2, y_lo: 2; y = y_hi * 2 + y_lo), z: 16, core: 2. Of those that a mesh axis runs over, the one named last changes fastest.
Arguments:
- queries: bfloat16 [192, 8192], P('ctx', 'tp')
- cache_keys: bfloat16 [16, 98304, 128], P('tp', 'ctx'), as said below
- cache_values: bfloat16 [16, 98304, 128], P('tp', 'ctx')
- seg_keys: bfloat16 [192, 2048], P('ctx', 'tp')
- seg_values: bfloat16 [192, 2048], P('ctx', 'tp')
- lengths: int32 [32], P('ctx'), may hold values from 1 to 3072, as said below
- residual_stream: bfloat16 [192, 8192], P('tp', 'ctx')
- out_weight: bfloat16 [8192, 8192], P('tp', 'ctx'), may hold values from -0.0625 to 0.0625
- norm_gain: float32 [8192], P('ctx'), may hold values from 0.1 to 1.9
- gate_weight: bfloat16 [8192, 29568], P('ctx', 'tp'), may hold values from -0.0625 to 0.0625
- up_weight: bfloat16 [8192, 29568], P('ctx', 'tp'), may hold values from -0.0625 to 0.0625
- down_weight: bfloat16 [29568, 8192], P('tp', 'ctx'), may hold values from -0.03125 to 0.03125
Outputs:
- attention: bfloat16 [192, 8192], P('ctx', 'tp')
- layer_out: bfloat16 [192, 8192], P('tp', 'ctx')
The draws below stay inside these ranges and needn't reach their ends.
Inputs may be any that keep to these rules, and one draw needn't show every extreme that they name: Block c of the cache holds live entries at its first lengths[c] positions; the rest are unused. The last block is at most half live and at least one block is fully live. `cache_keys`: slots hold the 8 key-value heads in order, each repeated 16 / 8 times in a row; the same holds for the segment's keys and values.
All inputs are finite; a program needn't handle non-finite values.
Results may differ from the reference program's by a relative error of at most 0.02.
Values may be sent and summed in bfloat16 or wider, within the bound.
No kernel may reach another device: no remote copies, remote signals or barrier semaphores. Data moves between devices by JAX's collectives and lax.ppermute only.
A program may use at most 64 MiB of HBM per device.

```python
import math
import jax
import jax.numpy as jnp
from jax import lax

D = 8192
QUERY_HEADS = 64
KEY_VALUE_HEADS = 8
HEAD_SIZE = 128
FF = 29568
SEGMENT_TOKENS = 192
STRETCH = 3072
STORED_HEADS = 16
CACHED_POSITIONS = 98304


def cache_base(key):
    key = jax.random.fold_in(key, 101)
    noise_level = jax.random.normal(key, (KEY_VALUE_HEADS, CACHED_POSITIONS, HEAD_SIZE), jnp.float32)
    return 2.5 * noise_level


def block_lengths(key):
    key = jax.random.fold_in(key, 202)
    first, second, third = jax.random.split(key, 3)
    count = CACHED_POSITIONS // STRETCH
    spots = jnp.arange(count)
    base_offset = jax.random.randint(first, (count,), STRETCH // 4, STRETCH + 1)
    full = jax.random.randint(second, (), 0, count - 1)
    base_offset = jnp.where(spots == full, STRETCH, base_offset)
    final = jax.random.randint(third, (), 1, STRETCH // 2 + 1)
    return jnp.where(spots == count - 1, final, base_offset).astype(jnp.int32)


def draw_lengths(key, part):
    return block_lengths(key)


def draw_cache_keys(key, part):
    base_offset = cache_base(key)
    return jnp.repeat(base_offset, STORED_HEADS // KEY_VALUE_HEADS, axis=0).astype(jnp.bfloat16)


def draw_cache_values(key, part):
    key = jax.random.fold_in(key, 303)
    base_offset = 3.0 * jax.random.normal(key, (KEY_VALUE_HEADS, CACHED_POSITIONS, HEAD_SIZE), jnp.float32)
    return jnp.repeat(base_offset, STORED_HEADS // KEY_VALUE_HEADS, axis=0).astype(jnp.bfloat16)


def segment_table(key, spread_factor):
    base_offset = spread_factor * jax.random.normal(key, (SEGMENT_TOKENS, KEY_VALUE_HEADS, HEAD_SIZE), jnp.float32)
    return jnp.repeat(base_offset, STORED_HEADS // KEY_VALUE_HEADS, axis=1).reshape(SEGMENT_TOKENS, STORED_HEADS * HEAD_SIZE)


def draw_seg_keys(key, part):
    key = jax.random.fold_in(key, 404)
    return segment_table(key, 2.5).astype(jnp.bfloat16)


def draw_seg_values(key, part):
    key = jax.random.fold_in(key, 505)
    return segment_table(key, 3.0).astype(jnp.bfloat16)


def draw_queries(key, part):
    own = jax.random.fold_in(key, 606)
    parts = jax.random.split(own, 1)
    drawn = jax.random.normal(parts[0], (SEGMENT_TOKENS, QUERY_HEADS, HEAD_SIZE), jnp.float32)
    return drawn.reshape(SEGMENT_TOKENS, QUERY_HEADS * HEAD_SIZE).astype(jnp.bfloat16)


def draw_residual_stream(key, part):
    key = jax.random.fold_in(key, 707)
    first = jax.random.fold_in(key, 0)
    noise_level = jax.random.normal(first, (SEGMENT_TOKENS, D), jnp.float32)
    ramp = jnp.arange(D, dtype=jnp.float32) / D
    return (0.6 * noise_level * jnp.exp(ramp * math.log(3.0))[None, :]).astype(jnp.bfloat16)


def steps_of(key, shape, cuts, least, high):
    def one(position, blocks):
        steps = jax.random.uniform(jax.random.fold_in(jax.random.fold_in(key, 6), position), (blocks,), jnp.float32, least / len(cuts), high / len(cuts))
        return jnp.repeat(jnp.exp(steps), shape[position] // blocks).reshape((-1,) + (1,) * (len(shape) - position - 1))

    level = one(*cuts[0])
    for cut in cuts[1:]:
        level = level * one(*cut)
    return level


def normal_values(own_key, extent, spread, limit, shards=(), kind=jnp.bfloat16):
    gain = steps_of(own_key, extent, shards, -0.22, 0.18) if shards else 1.0
    result = jax.random.normal(own_key, extent, jnp.float32) * spread * gain
    return jnp.minimum(jnp.maximum(result, -limit), limit).astype(kind)


def setup_inputs(seed: int = 0) -> dict:
    arg_keys = jax.random.split(jax.random.key(seed), 13)
    return {
        "queries": draw_queries(jax.random.fold_in(arg_keys[12], 71), 0),
        "cache_keys": draw_cache_keys(jax.random.fold_in(arg_keys[12], 71), 0),
        "cache_values": draw_cache_values(jax.random.fold_in(arg_keys[12], 71), 0),
        "seg_keys": draw_seg_keys(jax.random.fold_in(arg_keys[12], 71), 0),
        "seg_values": draw_seg_values(jax.random.fold_in(arg_keys[12], 71), 0),
        "lengths": draw_lengths(jax.random.fold_in(arg_keys[12], 71), 0),
        "residual_stream": draw_residual_stream(jax.random.fold_in(arg_keys[12], 71), 0),
        "out_weight": normal_values(arg_keys[7], (QUERY_HEADS * HEAD_SIZE, D), (QUERY_HEADS * HEAD_SIZE) ** -0.5, 0.0625, ((0, 16), (1, 32))),
        "norm_gain": jnp.clip(1.0 + 0.18 * jax.random.normal(arg_keys[8], (D,), jnp.float32), 0.1, 1.9),
        "gate_weight": normal_values(arg_keys[9], (D, FF), D ** -0.5, 0.0625, ((0, 32), (1, 16))),
        "up_weight": normal_values(arg_keys[10], (D, FF), D ** -0.5, 0.0625, ((0, 32), (1, 16))),
        "down_weight": normal_values(arg_keys[11], (FF, D), FF ** -0.5, 0.03125, ((0, 16), (1, 32))),
    }


def reference(queries, cache_keys, cache_values, seg_keys, seg_values, lengths, residual_stream, out_weight, norm_gain, gate_weight, up_weight, down_weight):
    scale = 1.0 / math.sqrt(HEAD_SIZE)
    heads_q = queries.reshape(SEGMENT_TOKENS, QUERY_HEADS, HEAD_SIZE).transpose(1, 0, 2)
    heads_k = seg_keys.reshape(SEGMENT_TOKENS, STORED_HEADS, HEAD_SIZE).transpose(1, 0, 2)
    heads_v = seg_values.reshape(SEGMENT_TOKENS, STORED_HEADS, HEAD_SIZE).transpose(1, 0, 2)
    slot_of = (jnp.arange(QUERY_HEADS) // (QUERY_HEADS // STORED_HEADS)).astype(jnp.int32)
    places = jnp.arange(CACHED_POSITIONS)
    live = places % STRETCH < lengths[(places // STRETCH).astype(jnp.int32)]
    causal = jnp.arange(SEGMENT_TOKENS)[:, None] >= jnp.arange(SEGMENT_TOKENS)[None, :]

    def one_head(pair):
        query, slot = pair
        keys_c = cache_keys[slot]
        vals_c = cache_values[slot]
        keys_s = heads_k[slot]
        vals_s = heads_v[slot]
        score_c = jnp.dot(query, keys_c.T, preferred_element_type=jnp.float32) * scale
        score_c = jnp.where(live[None, :], score_c, -jnp.inf)
        score_s = jnp.dot(query, keys_s.T, preferred_element_type=jnp.float32) * scale
        score_s = jnp.where(causal, score_s, -jnp.inf)
        top = jnp.maximum(score_c.max(axis=1), score_s.max(axis=1))
        weight_c = jnp.exp(score_c - top[:, None])
        weight_s = jnp.exp(score_s - top[:, None])
        total = weight_c.sum(axis=1) + weight_s.sum(axis=1)
        numer = jnp.dot(weight_c.astype(jnp.bfloat16), vals_c, preferred_element_type=jnp.float32)
        numer = numer + jnp.dot(weight_s.astype(jnp.bfloat16), vals_s, preferred_element_type=jnp.float32)
        return (numer / total[:, None]).astype(jnp.bfloat16)
    heads_out = lax.map(one_head, (heads_q, slot_of))
    attention = heads_out.transpose(1, 0, 2).reshape(SEGMENT_TOKENS, QUERY_HEADS * HEAD_SIZE)
    mixed = jnp.dot(attention, out_weight, preferred_element_type=jnp.float32)
    stream = (residual_stream.astype(jnp.float32) + mixed).astype(jnp.bfloat16)
    wide = stream.astype(jnp.float32)
    power = lax.optimization_barrier(jnp.mean(wide * wide, axis=1))
    normed = (wide * lax.rsqrt(power + 1e-06)[:, None] * norm_gain).astype(jnp.bfloat16)
    gate = jnp.dot(normed, gate_weight, preferred_element_type=jnp.float32)
    upper = jnp.dot(normed, up_weight, preferred_element_type=jnp.float32)
    hidden = (jax.nn.silu(gate) * upper).astype(jnp.bfloat16)
    lowered = jnp.dot(hidden, down_weight, preferred_element_type=jnp.float32)
    layer_out = (wide + lowered).astype(jnp.bfloat16)
    return (attention, layer_out)
```

```python
import functools
import math

import jax
import jax.numpy as jnp
from jax import lax
from jax.experimental import pallas as pl
from jax.experimental.pallas import tpu as pltpu
from jax.sharding import PartitionSpec as P

D = 8192
F32 = jnp.float32
BF16 = jnp.bfloat16
LOW = -1e30
SPAN = 512


def three_parts(x):
    one = x.astype(BF16).astype(F32)
    rest = x - one
    two = rest.astype(BF16).astype(F32)
    return one, two, (rest - two).astype(BF16).astype(F32)


def attend_kernel(where, q_ref, k_ref, v_ref, sk_ref, sv_ref, out_ref, *, tokens, group, head, scale):
    length = where[0]
    first = where[1]
    rows = tokens * group
    own = sk_ref.shape[0]
    query = jnp.concatenate([q_ref[:, g * head : (g + 1) * head] for g in range(group)], axis=0)

    def scores(keys):
        return lax.dot_general(keys, query, (((1,), (1,)), ((), ())), preferred_element_type=F32) * scale

    def add(carry, s, values):
        top, total, numer = carry
        top_new = jnp.maximum(top, jnp.max(s, axis=0, keepdims=True))
        fade = jnp.exp(top - top_new)
        w = jnp.exp(s - top_new)
        total = total * fade + jnp.sum(w, axis=0, keepdims=True)
        numer = numer * fade + lax.dot_general(
            values, w.astype(BF16), (((0,), (0,)), ((), ())), preferred_element_type=F32
        )
        return top_new, total, numer

    s = scores(sk_ref[...])
    token = lax.broadcasted_iota(jnp.int32, (own, rows), 1) % tokens
    place = first + lax.broadcasted_iota(jnp.int32, (own, rows), 0)
    seen = place <= token
    s = jnp.where(seen, s, LOW)
    top = jnp.max(s, axis=0, keepdims=True)
    w = jnp.where(seen, jnp.exp(s - top), 0.0)
    total = jnp.sum(w, axis=0, keepdims=True)
    numer = lax.dot_general(sv_ref[...], w.astype(BF16), (((0,), (0,)), ((), ())), preferred_element_type=F32)

    def whole(step, carry):
        at = pl.ds(pl.multiple_of(step * SPAN, SPAN), SPAN)
        return add(carry, scores(k_ref[at, :]), v_ref[at, :])

    full = length // SPAN
    carry = lax.fori_loop(0, full, whole, (top, total, numer))

    def part(step, carry):
        at = pl.ds(pl.multiple_of(step * SPAN, SPAN), SPAN)
        s = scores(k_ref[at, :])
        live = step * SPAN + lax.broadcasted_iota(jnp.int32, s.shape, 0) < length
        return add(carry, jnp.where(live, s, LOW), v_ref[at, :])

    top, total, numer = lax.fori_loop(full, (length + SPAN - 1) // SPAN, part, carry)
    out = (numer / total).T
    stats = jnp.concatenate([*three_parts(top), *three_parts(total), jnp.zeros((2, rows), F32)], axis=0).T
    for g in range(group):
        mine = slice(g * tokens, (g + 1) * tokens)
        out_ref[:, g * head : (g + 1) * head] = out[mine].astype(BF16)
    tail = jnp.concatenate(
        [stats[g * tokens : (g + 1) * tokens] for g in range(group)] + [jnp.zeros((tokens, 128 - 8 * group), F32)],
        axis=1,
    )
    out_ref[:, group * head :] = tail.astype(BF16)


def merge_kernel(in_ref, out_ref, *, group, head):
    stats = in_ref[:, :, group * head :].astype(F32)
    for g in range(group):
        col = [stats[:, :, 8 * g + i : 8 * g + i + 1] for i in range(6)]
        top = col[0] + col[1] + col[2]
        total = col[3] + col[4] + col[5]
        best = jnp.max(top, axis=0, keepdims=True)
        w = jnp.exp(top - best) * total
        mine = slice(g * head, (g + 1) * head)
        numer = jnp.sum(in_ref[:, :, mine].astype(F32) * w, axis=0)
        out_ref[:, mine] = (numer / jnp.sum(w, axis=0)).astype(BF16)


def to_all(x, axis):
    n = lax.axis_size(axis)
    return lax.all_to_all(jnp.broadcast_to(x[None], (n, *x.shape)), axis, 0, 0, tiled=True)


def swap(x, axis, mask):
    n = lax.axis_size(axis)
    return lax.ppermute(x, axis, [(i, i ^ mask) for i in range(n)])


def per_device(
    queries,
    cache_keys,
    cache_values,
    seg_keys,
    seg_values,
    lengths,
    residual_stream,
    out_weight,
    norm_gain,
    gate_weight,
    up_weight,
    down_weight,
):
    rows, width = queries.shape
    _, stretch, head = cache_keys.shape
    group = width // head
    n_ctx, n_tp = lax.axis_size("ctx"), lax.axis_size("tp")
    tokens = rows * n_ctx
    c, t = lax.axis_index("ctx"), lax.axis_index("tp")
    trows = residual_stream.shape[0]
    feats = residual_stream.shape[1]
    units = gate_weight.shape[1]

    q_all = to_all(queries, "ctx").reshape(tokens, width)
    where = jnp.stack([lengths[0], c * rows])
    vmem = pl.BlockSpec(memory_space=pltpu.VMEM)
    partial = pl.pallas_call(
        functools.partial(attend_kernel, tokens=tokens, group=group, head=head, scale=1.0 / math.sqrt(head)),
        out_shape=jax.ShapeDtypeStruct((tokens, width + 128), BF16),
        in_specs=[pl.BlockSpec(memory_space=pltpu.SMEM)] + [vmem] * 5,
        out_specs=vmem,
        compiler_params=pltpu.CompilerParams(vmem_limit_bytes=40 * 2**20),
        cost_estimate=pl.CostEstimate(flops=4 * tokens * width * stretch, bytes_accessed=2**21, transcendentals=tokens * group * stretch),
        name="attend",
    )(where, q_all, cache_keys[0], cache_values[0], seg_keys, seg_values)
    parts = lax.all_to_all(partial.reshape(n_ctx, rows, width + 128), "ctx", 0, 0, tiled=True)
    attention = pl.pallas_call(
        functools.partial(merge_kernel, group=group, head=head),
        out_shape=jax.ShapeDtypeStruct((rows, width), BF16),
        in_specs=[vmem],
        out_specs=vmem,
        compiler_params=pltpu.CompilerParams(vmem_limit_bytes=40 * 2**20),
        name="merge",
    )(parts)

    heads_all = to_all(attention, "ctx").reshape(tokens, width)
    mixed = jnp.dot(heads_all, out_weight, preferred_element_type=F32)
    residual = jnp.where(
        (jnp.arange(n_tp) == t)[:, None, None], residual_stream.astype(F32)[None], 0.0
    ).reshape(tokens, feats)
    total = (mixed + residual).astype(BF16)
    for mask in (1, 2, 4, 8):
        got = swap(total, "tp", mask)
        total = (total.astype(F32) + got.astype(F32)).astype(BF16)
    stream = total
    wide = stream.astype(F32)
    squares = jnp.sum(wide * wide, axis=1, keepdims=True)
    scaled = (wide * norm_gain).astype(BF16)
    gate = jnp.dot(scaled, gate_weight, preferred_element_type=F32).astype(BF16)
    upper = jnp.dot(scaled, up_weight, preferred_element_type=F32).astype(BF16)
    pad = -(2 * units + 3) % 128
    sums = jnp.concatenate(
        [gate, upper] + [p.astype(BF16) for p in three_parts(squares)] + [jnp.zeros((tokens, pad), BF16)], axis=1
    )
    sums = lax.all_to_all(sums.reshape(n_ctx, rows, -1), "ctx", 0, 0, tiled=True)
    sums = jnp.sum(sums.astype(F32), axis=0)
    power = jnp.sum(sums[:, 2 * units : 2 * units + 3], axis=1, keepdims=True) / D
    inv = lax.rsqrt(power + 1e-06)
    gate, upper = sums[:, :units] * inv, sums[:, units : 2 * units] * inv
    hidden = (jax.nn.silu(gate) * upper).astype(BF16)
    hidden_all = to_all(hidden, "ctx").reshape(tokens, units)
    lowered = jnp.dot(hidden_all, down_weight, preferred_element_type=F32)

    keep = lowered.reshape(n_tp, trows, feats)
    for bit in range(4):
        both = keep.reshape(-1, 2, trows, feats)
        mine = (t >> bit) & 1
        send = lax.dynamic_index_in_dim(both, 1 - mine, 1, keepdims=False).astype(BF16)
        stay = lax.dynamic_index_in_dim(both, mine, 1, keepdims=False)
        keep = stay + swap(send, "tp", 1 << bit).astype(F32)
    own = lax.dynamic_slice_in_dim(wide, t * trows, trows, 0)
    layer_out = (own + keep[0]).astype(BF16)
    return (attention, layer_out)


def solution(mesh):
    return jax.shard_map(
        per_device,
        mesh=mesh,
        in_specs=(
            P("ctx", "tp"),
            P("tp", "ctx", None),
            P("tp", "ctx", None),
            P("ctx", "tp"),
            P("ctx", "tp"),
            P("ctx"),
            P("tp", "ctx"),
            P("tp", "ctx"),
            P("ctx"),
            P("ctx", "tp"),
            P("ctx", "tp"),
            P("tp", "ctx"),
        ),
        out_specs=(P("ctx", "tp"), P("tp", "ctx")),
        check_vma=False,
    )
```

```python
import functools
import math

import jax
import jax.numpy as jnp
from jax import lax
from jax.experimental import pallas as pl
from jax.experimental.pallas import tpu as pltpu
from jax.sharding import PartitionSpec as P

D = 8192
F32 = jnp.float32
BF16 = jnp.bfloat16
LOW = -1e30
SPAN = 512


def three_parts(x):
    one = x.astype(BF16).astype(F32)
    rest = x - one
    two = rest.astype(BF16).astype(F32)
    return one, two, (rest - two).astype(BF16).astype(F32)


def attend_kernel(
    where, q_ref, k_hbm, v_hbm, sk_ref, sv_ref, out_ref, k_ref, v_ref, sems, *, tokens, group, head, scale
):
    k_copy = pltpu.make_async_copy(k_hbm, k_ref, sems.at[0])
    v_copy = pltpu.make_async_copy(v_hbm, v_ref, sems.at[1])
    k_copy.start()
    v_copy.start()
    length = where[0]
    first = where[1]
    rows = tokens * group
    own = sk_ref.shape[0]
    query = jnp.concatenate([q_ref[:, g * head : (g + 1) * head] for g in range(group)], axis=0)

    def scores(keys):
        return lax.dot_general(keys, query, (((1,), (1,)), ((), ())), preferred_element_type=F32) * scale

    def add(carry, s, values):
        top, total, numer = carry
        top_new = jnp.maximum(top, jnp.max(s, axis=0, keepdims=True))
        fade = jnp.exp(top - top_new)
        w = jnp.exp(s - top_new)
        total = total * fade + jnp.sum(w, axis=0, keepdims=True)
        numer = numer * fade + lax.dot_general(
            values, w.astype(BF16), (((0,), (0,)), ((), ())), preferred_element_type=F32
        )
        return top_new, total, numer

    s = scores(sk_ref[...])
    token = lax.broadcasted_iota(jnp.int32, (own, rows), 1) % tokens
    place = first + lax.broadcasted_iota(jnp.int32, (own, rows), 0)
    seen = place <= token
    s = jnp.where(seen, s, LOW)
    top = jnp.max(s, axis=0, keepdims=True)
    w = jnp.where(seen, jnp.exp(s - top), 0.0)
    total = jnp.sum(w, axis=0, keepdims=True)
    numer = lax.dot_general(sv_ref[...], w.astype(BF16), (((0,), (0,)), ((), ())), preferred_element_type=F32)

    k_copy.wait()
    v_copy.wait()

    def whole(step, carry):
        at = pl.ds(pl.multiple_of(step * SPAN, SPAN), SPAN)
        return add(carry, scores(k_ref[at, :]), v_ref[at, :])

    full = length // SPAN
    carry = lax.fori_loop(0, full, whole, (top, total, numer))

    def part(step, carry):
        at = pl.ds(pl.multiple_of(step * SPAN, SPAN), SPAN)
        s = scores(k_ref[at, :])
        live = step * SPAN + lax.broadcasted_iota(jnp.int32, s.shape, 0) < length
        return add(carry, jnp.where(live, s, LOW), v_ref[at, :])

    top, total, numer = lax.fori_loop(full, (length + SPAN - 1) // SPAN, part, carry)
    out = (numer / total).T
    stats = jnp.concatenate([*three_parts(top), *three_parts(total), jnp.zeros((2, rows), F32)], axis=0).T
    for g in range(group):
        mine = slice(g * tokens, (g + 1) * tokens)
        out_ref[:, g * head : (g + 1) * head] = out[mine].astype(BF16)
    tail = jnp.concatenate(
        [stats[g * tokens : (g + 1) * tokens] for g in range(group)] + [jnp.zeros((tokens, 128 - 8 * group), F32)],
        axis=1,
    )
    out_ref[:, group * head :] = tail.astype(BF16)


def merge_kernel(in_ref, out_ref, *, group, head):
    stats = in_ref[:, :, group * head :].astype(F32)
    for g in range(group):
        col = [stats[:, :, 8 * g + i : 8 * g + i + 1] for i in range(6)]
        top = col[0] + col[1] + col[2]
        total = col[3] + col[4] + col[5]
        best = jnp.max(top, axis=0, keepdims=True)
        w = jnp.exp(top - best) * total
        mine = slice(g * head, (g + 1) * head)
        numer = jnp.sum(in_ref[:, :, mine].astype(F32) * w, axis=0)
        out_ref[:, mine] = (numer / jnp.sum(w, axis=0)).astype(BF16)


def project_kernel(sel, x_ref, gain_ref, w_ref, send_ref, stay_ref, *, bit, power):
    quarter = send_ref.shape[1]
    units = w_ref.shape[0]
    stride = (2, 1)[bit]
    mine = sel[bit]

    def rows(which, other):
        block = which * stride + other * (3 - stride)
        return x_ref[pl.ds(pl.multiple_of(block * quarter, quarter), quarter), :]

    x = jnp.concatenate([rows(1 - mine, 0), rows(1 - mine, 1), rows(mine, 0), rows(mine, 1)], axis=0).astype(F32)
    y = lax.dot_general(
        (x * gain_ref[...]).astype(BF16), w_ref[...], (((1,), (1,)), ((), ())), preferred_element_type=F32
    )
    if power:
        parts = three_parts(jnp.sum(x * x, axis=1, keepdims=True))
        cut = units // 128 * 128
        spare = jnp.zeros((x.shape[0], send_ref.shape[2] - units - 3), F32)
        y = jnp.concatenate([y[:, :cut], jnp.concatenate([y[:, cut:], *parts, spare], axis=1)], axis=1)
    for other in range(2):
        send_ref[other] = y[other * quarter : (other + 1) * quarter].astype(BF16)
        stay_ref[other] = y[(2 + other) * quarter : (3 + other) * quarter]


def resplit(x, units):
    cut = units // 128 * 128
    tail = x[:, cut:]
    at = units - cut
    one, two, three = three_parts(jnp.sum(tail[:, at : at + 3], axis=1, keepdims=True))
    column = lax.broadcasted_iota(jnp.int32, tail.shape, 1) - at
    tail = jnp.where(column == 0, one, jnp.where(column == 1, two, jnp.where(column == 2, three, tail)))
    return jnp.concatenate([x[:, :cut], tail], axis=1)


def halve_kernel(sel, stay_ref, got_ref, send_ref, keep_ref, *, bit, units):
    mine = sel[bit]
    send = stay_ref[1 - mine] + got_ref[1 - mine].astype(F32)
    send_ref[...] = (resplit(send, units) if units else send).astype(BF16)
    keep_ref[...] = stay_ref[mine] + got_ref[mine].astype(F32)


def join_kernel(g_ref, g_got_ref, u_ref, u_got_ref, out_ref, *, units):
    g = resplit(g_ref[...] + g_got_ref[...].astype(F32), units)
    u = u_ref[...] + u_got_ref[...].astype(F32)
    rows = out_ref.shape[1]
    width = g.shape[1]
    for i in range(out_ref.shape[0]):
        out_ref[i, :, :width] = g[i * rows : (i + 1) * rows].astype(BF16)
        out_ref[i, :, width:] = u[i * rows : (i + 1) * rows].astype(BF16)


def hidden_kernel(in_ref, out_ref, *, units, width):
    sums = jnp.sum(in_ref[...].astype(F32), axis=0)
    power = jnp.sum(sums[:, units : units + 3], axis=1, keepdims=True) / D
    inv = lax.rsqrt(power + 1e-06)
    gate, upper = sums[:, :units] * inv, sums[:, width:] * inv
    out_ref[...] = (gate / (1.0 + jnp.exp(-gate)) * upper).astype(BF16)


def swap(x, axis, mask):
    n = lax.axis_size(axis)
    return lax.ppermute(x, axis, [(i, i ^ mask) for i in range(n)])


def doubled(x, axis, bits):
    here = lax.axis_index(axis)
    for bit in bits:
        got = swap(x, axis, 1 << bit)
        first = ((here >> bit) & 1) == 0
        x = jnp.where(first, jnp.concatenate([x, got]), jnp.concatenate([got, x]))
    return x


def all_tokens(x, axis):
    x = doubled(x[None], axis, (4, 3, 2, 1, 0))
    x = x.reshape(2, 2, 2, 2, 2, *x.shape[1:]).transpose(4, 3, 2, 1, 0, 5, 6)
    return x.reshape(-1, x.shape[-1])


def per_device(
    queries,
    cache_keys,
    cache_values,
    seg_keys,
    seg_values,
    lengths,
    residual_stream,
    out_weight,
    norm_gain,
    gate_weight,
    up_weight,
    down_weight,
):
    rows, width = queries.shape
    _, stretch, head = cache_keys.shape
    group = width // head
    n_ctx, n_tp = lax.axis_size("ctx"), lax.axis_size("tp")
    tokens = rows * n_ctx
    c, t = lax.axis_index("ctx"), lax.axis_index("tp")
    trows = residual_stream.shape[0]
    feats = residual_stream.shape[1]
    units = gate_weight.shape[1]

    q_all = all_tokens(queries, "ctx")
    where = jnp.stack([lengths[0], c * rows])
    vmem = pl.BlockSpec(memory_space=pltpu.VMEM)
    smem = pl.BlockSpec(memory_space=pltpu.SMEM)
    anywhere = pl.BlockSpec(memory_space=pl.ANY)
    params = pltpu.CompilerParams(vmem_limit_bytes=60 * 2**20)
    small = pltpu.CompilerParams(vmem_limit_bytes=24 * 2**20)
    partial = pl.pallas_call(
        functools.partial(attend_kernel, tokens=tokens, group=group, head=head, scale=1.0 / math.sqrt(head)),
        out_shape=jax.ShapeDtypeStruct((tokens, width + 128), BF16),
        in_specs=[smem, vmem, anywhere, anywhere, vmem, vmem],
        out_specs=vmem,
        scratch_shapes=[
            pltpu.VMEM((stretch, head), BF16),
            pltpu.VMEM((stretch, head), BF16),
            pltpu.SemaphoreType.DMA((2,)),
        ],
        compiler_params=params,
        cost_estimate=pl.CostEstimate(
            flops=4 * tokens * width * stretch, bytes_accessed=2**21, transcendentals=tokens * group * stretch
        ),
        name="attend",
    )(where, q_all, cache_keys[0], cache_values[0], seg_keys, seg_values)
    parts = lax.all_to_all(partial.reshape(n_ctx, rows, width + 128), "ctx", 0, 0, tiled=True)
    attention = pl.pallas_call(
        functools.partial(merge_kernel, group=group, head=head),
        out_shape=jax.ShapeDtypeStruct((rows, width), BF16),
        in_specs=[vmem],
        out_specs=vmem,
        compiler_params=small,
        name="merge",
    )(parts)

    heads_all = all_tokens(attention, "ctx")
    mixed = jnp.dot(heads_all, out_weight, preferred_element_type=F32)
    residual = jnp.where(
        (jnp.arange(n_tp) == t)[:, None, None], residual_stream.astype(F32)[None], 0.0
    ).reshape(tokens, feats)
    total = (mixed + residual).astype(BF16)
    for mask in (1, 2, 4, 8):
        got = swap(total, "tp", mask)
        total = (total.astype(F32) + got.astype(F32)).astype(BF16)
    stream = total

    y_hi, z_lo = c & 1, (c >> 1) & 1
    sel = jnp.stack([y_hi, z_lo])
    quarter = tokens // 4
    wide_units = -(-(units + 3) // 128) * 128

    def project(weight, bit, power):
        out = wide_units if power else units
        return pl.pallas_call(
            functools.partial(project_kernel, bit=bit, power=power),
            out_shape=(
                jax.ShapeDtypeStruct((2, quarter, out), BF16),
                jax.ShapeDtypeStruct((2, quarter, out), F32),
            ),
            in_specs=[smem, vmem, vmem, vmem],
            out_specs=(vmem, vmem),
            compiler_params=small,
            cost_estimate=pl.CostEstimate(flops=2 * tokens * feats * units, bytes_accessed=2**21, transcendentals=0),
            name="gate" if power else "up",
        )(sel, stream, norm_gain[None], weight.T)

    def halve(stay, got, bit, power):
        out = stay.shape[2]
        return pl.pallas_call(
            functools.partial(halve_kernel, bit=bit, units=units if power else 0),
            out_shape=(jax.ShapeDtypeStruct((quarter, out), BF16), jax.ShapeDtypeStruct((quarter, out), F32)),
            in_specs=[smem, vmem, vmem],
            out_specs=(vmem, vmem),
            compiler_params=small,
            name="halve_gate" if power else "halve_up",
        )(sel, stay, got)

    g_send, g_stay = project(gate_weight, 1, True)
    g_got = swap(g_send, "ctx", 2)
    u_send, u_stay = project(up_weight, 0, False)
    u_got = swap(u_send, "ctx", 1)
    g_send, g_stay = halve(g_stay, g_got, 0, True)
    g_got = swap(g_send, "ctx", 1)
    u_send, u_stay = halve(u_stay, u_got, 1, False)
    u_got = swap(u_send, "ctx", 2)
    far = n_ctx // 4
    sums = pl.pallas_call(
        functools.partial(join_kernel, units=units),
        out_shape=jax.ShapeDtypeStruct((far, rows, wide_units + units), BF16),
        in_specs=[vmem] * 4,
        out_specs=vmem,
        compiler_params=small,
        name="join",
    )(g_stay, g_got, u_stay, u_got)
    turned = [sum(((i >> k) & 1) << (2 - k) for k in range(3)) for i in range(far)]
    groups = [[j * 4 + q for j in turned] for q in range(4)]
    sums = lax.all_to_all(sums, "ctx", 0, 0, axis_index_groups=groups, tiled=True)
    hidden = pl.pallas_call(
        functools.partial(hidden_kernel, units=units, width=wide_units),
        out_shape=jax.ShapeDtypeStruct((rows, units), BF16),
        in_specs=[vmem],
        out_specs=vmem,
        compiler_params=small,
        name="hidden",
    )(sums)
    hidden = doubled(hidden[None], "ctx", (4, 3, 2)).reshape(quarter, units)
    hidden = doubled(hidden, "ctx", (1, 0))
    keep = jnp.dot(hidden, down_weight, preferred_element_type=F32)

    for bit in (3, 2, 1, 0):
        half = keep.shape[0] // 2
        mine = (t >> bit) & 1
        send = lax.dynamic_slice_in_dim(keep, (1 - mine) * half, half, 0).astype(BF16)
        stay = lax.dynamic_slice_in_dim(keep, mine * half, half, 0)
        keep = stay + swap(send, "tp", 1 << bit).astype(F32)
    own = lax.dynamic_slice_in_dim(stream, t * trows, trows, 0).astype(F32)
    layer_out = (own + keep).astype(BF16)
    return (attention, layer_out)


def solution(mesh):
    return jax.shard_map(
        per_device,
        mesh=mesh,
        in_specs=(
            P("ctx", "tp"),
            P("tp", "ctx", None),
            P("tp", "ctx", None),
            P("ctx", "tp"),
            P("ctx", "tp"),
            P("ctx"),
            P("tp", "ctx"),
            P("tp", "ctx"),
            P("ctx"),
            P("ctx", "tp"),
            P("ctx", "tp"),
            P("tp", "ctx"),
        ),
        out_specs=(P("ctx", "tp"), P("tp", "ctx")),
        check_vma=False,
    )
```

```python
import functools
import math

import jax
import jax.numpy as jnp
from jax import lax
from jax.experimental import pallas as pl
from jax.experimental.pallas import tpu as pltpu
from jax.sharding import PartitionSpec as P

D = 8192
F32 = jnp.float32
BF16 = jnp.bfloat16
LOW = -1e30
SPAN = 512


def three_parts(x):
    one = x.astype(BF16).astype(F32)
    rest = x - one
    two = rest.astype(BF16).astype(F32)
    return one, two, (rest - two).astype(BF16).astype(F32)


def attend_kernel(
    where, q_ref, k_hbm, v_hbm, sk_ref, sv_ref, out_ref, k_ref, v_ref, sems, *, tokens, group, head, scale
):
    k_copy = pltpu.make_async_copy(k_hbm, k_ref, sems.at[0])
    v_copy = pltpu.make_async_copy(v_hbm, v_ref, sems.at[1])
    k_copy.start()
    v_copy.start()
    length = where[0]
    first = where[1]
    rows = tokens * group
    own = sk_ref.shape[0]
    query = q_ref[...].reshape(rows, head)
    unit = scale / math.log(2.0)

    def scores(keys):
        return lax.dot_general(keys, query, (((1,), (1,)), ((), ())), preferred_element_type=F32)

    def weigh(values, w):
        return lax.dot_general(values, w.astype(BF16), (((0,), (0,)), ((), ())), preferred_element_type=F32)

    def add(carry, s, values):
        top, total, numer = carry
        top_new = jnp.maximum(top, jnp.max(s, axis=0, keepdims=True))
        fade = jnp.exp2((top - top_new) * unit)
        w = jnp.exp2((s - top_new) * unit)
        return top_new, total * fade + jnp.sum(w, axis=0, keepdims=True), numer * fade + weigh(values, w)

    s = scores(sk_ref[...])
    token = lax.broadcasted_iota(jnp.int32, (own, rows), 1) // group
    place = first + lax.broadcasted_iota(jnp.int32, (own, rows), 0)
    seen = place <= token
    s = jnp.where(seen, s, LOW)
    top = jnp.max(s, axis=0, keepdims=True)
    w = jnp.where(seen, jnp.exp2((s - top) * unit), 0.0)
    total = jnp.sum(w, axis=0, keepdims=True)
    numer = weigh(sv_ref[...], w)
    k_copy.wait()
    v_copy.wait()

    def whole(step, carry):
        at = pl.ds(pl.multiple_of(step * SPAN, SPAN), SPAN)
        return add(carry, scores(k_ref[at, :]), v_ref[at, :])

    full = length // SPAN
    carry = lax.fori_loop(0, full, whole, (top, total, numer))

    def part(step, carry):
        at = pl.ds(pl.multiple_of(step * SPAN, SPAN), SPAN)
        s = scores(k_ref[at, :])
        live = step * SPAN + lax.broadcasted_iota(jnp.int32, s.shape, 0) < length
        return add(carry, jnp.where(live, s, LOW), v_ref[at, :])

    top, total, numer = lax.fori_loop(full, (length + SPAN - 1) // SPAN, part, carry)
    blocks = out_ref.shape[0]
    each = rows // blocks
    out_ref[:, :each, :] = (numer / total).T.astype(BF16).reshape(blocks, each, head)
    stats = jnp.concatenate([*three_parts(top * unit), *three_parts(total), jnp.zeros((2, rows), F32)], axis=0)
    stats = jnp.concatenate([stats, jnp.zeros((8, rows), F32)], axis=0)
    spare = jnp.zeros((out_ref.shape[1] - each, head - each), F32)
    for i in range(blocks):
        tail = stats[: out_ref.shape[1] - each, i * each : (i + 1) * each]
        out_ref[i, each:, :] = jnp.concatenate([tail, spare], axis=1).astype(BF16)


def merge_kernel(in_ref, out_ref, copies_ref):
    blocks, rows, head = copies_ref.shape
    stat = [in_ref[:, rows + i, :].astype(F32) for i in range(6)]
    top = stat[0] + stat[1] + stat[2]
    total = stat[3] + stat[4] + stat[5]
    w = jnp.exp2(top - jnp.max(top, axis=0, keepdims=True)) * total
    w = (w / jnp.sum(w, axis=0, keepdims=True)).T
    out = jnp.zeros((rows, head), F32)
    for i in range(blocks):
        out = out + in_ref[i, :rows, :].astype(F32) * w[:rows, i : i + 1]
    out = out.astype(BF16)
    out_ref[...] = out
    for i in range(blocks):
        copies_ref[i] = out


def project_kernel(sel, x_ref, gain_ref, w_ref, send_ref, stay_ref, *, bit, power):
    quarter = send_ref.shape[1]
    units = w_ref.shape[0]
    stride = (2, 1)[bit]
    mine = sel[bit]

    def rows(which, other):
        block = which * stride + other * (3 - stride)
        return x_ref[pl.ds(pl.multiple_of(block * quarter, quarter), quarter), :]

    x = jnp.concatenate([rows(1 - mine, 0), rows(1 - mine, 1), rows(mine, 0), rows(mine, 1)], axis=0).astype(F32)
    y = lax.dot_general(
        (x * gain_ref[...]).astype(BF16), w_ref[...], (((1,), (1,)), ((), ())), preferred_element_type=F32
    )
    if power:
        parts = three_parts(jnp.sum(x * x, axis=1, keepdims=True))
        cut = units // 128 * 128
        spare = jnp.zeros((x.shape[0], send_ref.shape[2] - units - 3), F32)
        y = jnp.concatenate([y[:, :cut], jnp.concatenate([y[:, cut:], *parts, spare], axis=1)], axis=1)
    for other in range(2):
        send_ref[other] = y[other * quarter : (other + 1) * quarter].astype(BF16)
        stay_ref[other] = y[(2 + other) * quarter : (3 + other) * quarter]


def resplit(x, units):
    cut = units // 128 * 128
    tail = x[:, cut:]
    at = units - cut
    one, two, three = three_parts(jnp.sum(tail[:, at : at + 3], axis=1, keepdims=True))
    column = lax.broadcasted_iota(jnp.int32, tail.shape, 1) - at
    tail = jnp.where(column == 0, one, jnp.where(column == 1, two, jnp.where(column == 2, three, tail)))
    return jnp.concatenate([x[:, :cut], tail], axis=1)


def halve_kernel(sel, stay_ref, got_ref, send_ref, keep_ref, *, bit, units):
    mine = sel[bit]
    send = stay_ref[1 - mine] + got_ref[1 - mine].astype(F32)
    send_ref[...] = (resplit(send, units) if units else send).astype(BF16)
    keep_ref[...] = stay_ref[mine] + got_ref[mine].astype(F32)


def join_kernel(g_ref, g_got_ref, u_ref, u_got_ref, out_ref, *, units):
    g = resplit(g_ref[...] + g_got_ref[...].astype(F32), units)
    u = u_ref[...] + u_got_ref[...].astype(F32)
    rows = out_ref.shape[1]
    width = g.shape[1]
    for i in range(out_ref.shape[0]):
        out_ref[i, :, :width] = g[i * rows : (i + 1) * rows].astype(BF16)
        out_ref[i, :, width:] = u[i * rows : (i + 1) * rows].astype(BF16)


def hidden_kernel(in_ref, out_ref, *, units, width):
    sums = jnp.sum(in_ref[...].astype(F32), axis=0)
    power = jnp.sum(sums[:, units : units + 3], axis=1, keepdims=True) / D
    inv = lax.rsqrt(power + 1e-06)
    gate, upper = sums[:, :units] * inv, sums[:, width:] * inv
    out = (gate / (1.0 + jnp.exp(-gate)) * upper).astype(BF16)
    for i in range(out_ref.shape[0]):
        out_ref[i] = out


def swap(x, axis, mask):
    n = lax.axis_size(axis)
    return lax.ppermute(x, axis, [(i, i ^ mask) for i in range(n)])


def doubled(x, axis, bits):
    here = lax.axis_index(axis)
    for bit in bits:
        got = swap(x, axis, 1 << bit)
        first = ((here >> bit) & 1) == 0
        x = jnp.where(first, jnp.concatenate([x, got]), jnp.concatenate([got, x]))
    return x


def per_device(
    queries,
    cache_keys,
    cache_values,
    seg_keys,
    seg_values,
    lengths,
    residual_stream,
    out_weight,
    norm_gain,
    gate_weight,
    up_weight,
    down_weight,
):
    rows, width = queries.shape
    _, stretch, head = cache_keys.shape
    group = width // head
    n_ctx, n_tp = lax.axis_size("ctx"), lax.axis_size("tp")
    tokens = rows * n_ctx
    c, t = lax.axis_index("ctx"), lax.axis_index("tp")
    trows = residual_stream.shape[0]
    feats = residual_stream.shape[1]
    units = gate_weight.shape[1]

    each = rows * group
    q_all = jnp.broadcast_to(queries.reshape(1, each, head), (n_ctx, each, head))
    q_all = lax.all_to_all(q_all, "ctx", 0, 0, tiled=True)
    where = jnp.stack([lengths[0], c * rows])
    vmem = pl.BlockSpec(memory_space=pltpu.VMEM)
    smem = pl.BlockSpec(memory_space=pltpu.SMEM)
    anywhere = pl.BlockSpec(memory_space=pl.ANY)
    params = pltpu.CompilerParams(vmem_limit_bytes=60 * 2**20)
    small = pltpu.CompilerParams(vmem_limit_bytes=24 * 2**20)
    partial = pl.pallas_call(
        functools.partial(attend_kernel, tokens=tokens, group=group, head=head, scale=1.0 / math.sqrt(head)),
        out_shape=jax.ShapeDtypeStruct((n_ctx, each + 8, head), BF16),
        in_specs=[smem, vmem, anywhere, anywhere, vmem, vmem],
        out_specs=vmem,
        scratch_shapes=[
            pltpu.VMEM((stretch, head), BF16),
            pltpu.VMEM((stretch, head), BF16),
            pltpu.SemaphoreType.DMA((2,)),
        ],
        compiler_params=params,
        cost_estimate=pl.CostEstimate(
            flops=4 * tokens * width * stretch, bytes_accessed=2**21, transcendentals=tokens * group * stretch
        ),
        name="attend",
    )(where, q_all, cache_keys[0], cache_values[0], seg_keys, seg_values)
    parts = lax.all_to_all(partial, "ctx", 0, 0, tiled=True)
    attention, copies = pl.pallas_call(
        merge_kernel,
        out_shape=(jax.ShapeDtypeStruct((each, head), BF16), jax.ShapeDtypeStruct((n_ctx, each, head), BF16)),
        in_specs=[vmem],
        out_specs=(vmem, vmem),
        compiler_params=small,
        name="merge",
    )(parts)
    attention = attention.reshape(rows, width)
    heads_all = lax.all_to_all(copies, "ctx", 0, 0, tiled=True).reshape(tokens, width)
    mixed = jnp.dot(heads_all, out_weight, preferred_element_type=F32)
    residual = jnp.where(
        (jnp.arange(n_tp) == t)[:, None, None], residual_stream.astype(F32)[None], 0.0
    ).reshape(tokens, feats)
    total = (mixed + residual).astype(BF16)
    for mask in (1, 2, 4, 8):
        got = swap(total, "tp", mask)
        total = (total.astype(F32) + got.astype(F32)).astype(BF16)
    stream = total

    y_hi, z_lo = c & 1, (c >> 1) & 1
    sel = jnp.stack([y_hi, z_lo])
    quarter = tokens // 4
    wide_units = -(-(units + 3) // 128) * 128

    def project(weight, bit, power):
        out = wide_units if power else units
        return pl.pallas_call(
            functools.partial(project_kernel, bit=bit, power=power),
            out_shape=(
                jax.ShapeDtypeStruct((2, quarter, out), BF16),
                jax.ShapeDtypeStruct((2, quarter, out), F32),
            ),
            in_specs=[smem, vmem, vmem, vmem],
            out_specs=(vmem, vmem),
            compiler_params=small,
            cost_estimate=pl.CostEstimate(flops=2 * tokens * feats * units, bytes_accessed=2**21, transcendentals=0),
            name="gate" if power else "up",
        )(sel, stream, norm_gain[None], weight.T)

    def halve(stay, got, bit, power):
        out = stay.shape[2]
        return pl.pallas_call(
            functools.partial(halve_kernel, bit=bit, units=units if power else 0),
            out_shape=(jax.ShapeDtypeStruct((quarter, out), BF16), jax.ShapeDtypeStruct((quarter, out), F32)),
            in_specs=[smem, vmem, vmem],
            out_specs=(vmem, vmem),
            compiler_params=small,
            name="halve_gate" if power else "halve_up",
        )(sel, stay, got)

    g_send, g_stay = project(gate_weight, 1, True)
    g_got = swap(g_send, "ctx", 2)
    u_send, u_stay = project(up_weight, 0, False)
    u_got = swap(u_send, "ctx", 1)
    g_send, g_stay = halve(g_stay, g_got, 0, True)
    g_got = swap(g_send, "ctx", 1)
    u_send, u_stay = halve(u_stay, u_got, 1, False)
    u_got = swap(u_send, "ctx", 2)
    far = n_ctx // 4
    sums = pl.pallas_call(
        functools.partial(join_kernel, units=units),
        out_shape=jax.ShapeDtypeStruct((far, rows, wide_units + units), BF16),
        in_specs=[vmem] * 4,
        out_specs=vmem,
        compiler_params=small,
        name="join",
    )(g_stay, g_got, u_stay, u_got)
    groups = [[j * 4 + q for j in range(far)] for q in range(4)]
    sums = lax.all_to_all(sums, "ctx", 0, 0, axis_index_groups=groups, tiled=True)
    hidden = pl.pallas_call(
        functools.partial(hidden_kernel, units=units, width=wide_units),
        out_shape=jax.ShapeDtypeStruct((far, rows, units), BF16),
        in_specs=[vmem],
        out_specs=vmem,
        compiler_params=small,
        name="hidden",
    )(sums)
    hidden = lax.all_to_all(hidden, "ctx", 0, 0, axis_index_groups=groups, tiled=True).reshape(quarter, units)
    hidden = doubled(hidden, "ctx", (1, 0))
    keep = jnp.dot(hidden, down_weight, preferred_element_type=F32)

    for bit in (3, 2, 1, 0):
        half = keep.shape[0] // 2
        mine = (t >> bit) & 1
        send = lax.dynamic_slice_in_dim(keep, (1 - mine) * half, half, 0).astype(BF16)
        stay = lax.dynamic_slice_in_dim(keep, mine * half, half, 0)
        keep = stay + swap(send, "tp", 1 << bit).astype(F32)
    own = lax.dynamic_slice_in_dim(stream, t * trows, trows, 0).astype(F32)
    layer_out = (own + keep).astype(BF16)
    return (attention, layer_out)


def solution(mesh):
    return jax.shard_map(
        per_device,
        mesh=mesh,
        in_specs=(
            P("ctx", "tp"),
            P("tp", "ctx", None),
            P("tp", "ctx", None),
            P("ctx", "tp"),
            P("ctx", "tp"),
            P("ctx"),
            P("tp", "ctx"),
            P("tp", "ctx"),
            P("ctx"),
            P("ctx", "tp"),
            P("ctx", "tp"),
            P("tp", "ctx"),
        ),
        out_specs=(P("ctx", "tp"), P("tp", "ctx")),
        check_vma=False,
    )
```

```python
import functools
import math

import jax
import jax.numpy as jnp
from jax import lax
from jax.experimental import pallas as pl
from jax.experimental.pallas import tpu as pltpu
from jax.sharding import PartitionSpec as P

D = 8192
F32 = jnp.float32
BF16 = jnp.bfloat16
LOW = -1e30
SPAN = 512


def three_parts(x):
    one = x.astype(BF16).astype(F32)
    rest = x - one
    two = rest.astype(BF16).astype(F32)
    return one, two, (rest - two).astype(BF16).astype(F32)


def attend_kernel(
    where, q_ref, k_hbm, v_hbm, sk_ref, sv_ref, out_ref, k_ref, v_ref, sems, *, tokens, group, head, scale
):
    k_copy = pltpu.make_async_copy(k_hbm, k_ref, sems.at[0])
    v_copy = pltpu.make_async_copy(v_hbm, v_ref, sems.at[1])
    k_copy.start()
    v_copy.start()
    length = where[0]
    first = where[1]
    rows = tokens * group
    own = sk_ref.shape[0]
    query = q_ref[...].reshape(rows, head)
    unit = scale / math.log(2.0)

    def scores(keys):
        return lax.dot_general(keys, query, (((1,), (1,)), ((), ())), preferred_element_type=F32)

    def weigh(values, w):
        return lax.dot_general(values, w.astype(BF16), (((0,), (0,)), ((), ())), preferred_element_type=F32)

    def add(carry, s, values):
        top, total, numer = carry
        top_new = jnp.maximum(top, jnp.max(s, axis=0, keepdims=True))
        fade = jnp.exp2((top - top_new) * unit)
        w = jnp.exp2((s - top_new) * unit)
        return top_new, total * fade + jnp.sum(w, axis=0, keepdims=True), numer * fade + weigh(values, w)

    s = scores(sk_ref[...])
    token = lax.broadcasted_iota(jnp.int32, (own, rows), 1) // group
    place = first + lax.broadcasted_iota(jnp.int32, (own, rows), 0)
    seen = place <= token
    s = jnp.where(seen, s, LOW)
    top = jnp.max(s, axis=0, keepdims=True)
    w = jnp.where(seen, jnp.exp2((s - top) * unit), 0.0)
    total = jnp.sum(w, axis=0, keepdims=True)
    numer = weigh(sv_ref[...], w)
    k_copy.wait()
    v_copy.wait()

    def whole(step, carry):
        at = pl.ds(pl.multiple_of(step * SPAN, SPAN), SPAN)
        return add(carry, scores(k_ref[at, :]), v_ref[at, :])

    full = length // SPAN
    carry = lax.fori_loop(0, full, whole, (top, total, numer))

    def part(step, carry):
        at = pl.ds(pl.multiple_of(step * SPAN, SPAN), SPAN)
        s = scores(k_ref[at, :])
        live = step * SPAN + lax.broadcasted_iota(jnp.int32, s.shape, 0) < length
        return add(carry, jnp.where(live, s, LOW), v_ref[at, :])

    top, total, numer = lax.fori_loop(full, (length + SPAN - 1) // SPAN, part, carry)
    blocks = out_ref.shape[0]
    each = rows // blocks
    out_ref[:, :each, :] = (numer / total).T.astype(BF16).reshape(blocks, each, head)
    stats = jnp.concatenate([*three_parts(top * unit), *three_parts(total), jnp.zeros((2, rows), F32)], axis=0)
    stats = jnp.concatenate([stats, jnp.zeros((8, rows), F32)], axis=0)
    spare = jnp.zeros((out_ref.shape[1] - each, head - each), F32)
    for i in range(blocks):
        tail = stats[: out_ref.shape[1] - each, i * each : (i + 1) * each]
        out_ref[i, each:, :] = jnp.concatenate([tail, spare], axis=1).astype(BF16)


def merge_kernel(in_ref, out_ref, copies_ref):
    blocks, rows, head = copies_ref.shape
    stat = [in_ref[:, rows + i, :].astype(F32) for i in range(6)]
    top = stat[0] + stat[1] + stat[2]
    total = stat[3] + stat[4] + stat[5]
    w = jnp.exp2(top - jnp.max(top, axis=0, keepdims=True)) * total
    w = (w / jnp.sum(w, axis=0, keepdims=True)).T
    out = jnp.zeros((rows, head), F32)
    for i in range(blocks):
        out = out + in_ref[i, :rows, :].astype(F32) * w[:rows, i : i + 1]
    out = out.astype(BF16)
    out_ref[...] = out
    for i in range(blocks):
        copies_ref[i] = out


def project_kernel(sel, x_ref, gain_ref, w_ref, send_ref, stay_ref, *, bit, power):
    quarter = send_ref.shape[1]
    units = w_ref.shape[0]
    stride = (2, 1)[bit]
    mine = sel[bit]

    def rows(which, other):
        block = which * stride + other * (3 - stride)
        return x_ref[pl.ds(pl.multiple_of(block * quarter, quarter), quarter), :]

    x = jnp.concatenate([rows(1 - mine, 0), rows(1 - mine, 1), rows(mine, 0), rows(mine, 1)], axis=0).astype(F32)
    y = lax.dot_general(
        (x * gain_ref[...]).astype(BF16), w_ref[...], (((1,), (1,)), ((), ())), preferred_element_type=F32
    )
    if power:
        parts = three_parts(jnp.sum(x * x, axis=1, keepdims=True))
        cut = units // 128 * 128
        spare = jnp.zeros((x.shape[0], send_ref.shape[2] - units - 3), F32)
        y = jnp.concatenate([y[:, :cut], jnp.concatenate([y[:, cut:], *parts, spare], axis=1)], axis=1)
    for other in range(2):
        send_ref[other] = y[other * quarter : (other + 1) * quarter].astype(BF16)
        stay_ref[other] = y[(2 + other) * quarter : (3 + other) * quarter]


def resplit(x, units):
    cut = units // 128 * 128
    tail = x[:, cut:]
    at = units - cut
    one, two, three = three_parts(jnp.sum(tail[:, at : at + 3], axis=1, keepdims=True))
    column = lax.broadcasted_iota(jnp.int32, tail.shape, 1) - at
    tail = jnp.where(column == 0, one, jnp.where(column == 1, two, jnp.where(column == 2, three, tail)))
    return jnp.concatenate([x[:, :cut], tail], axis=1)


def halve_kernel(sel, stay_ref, got_ref, send_ref, keep_ref, *, bit, units):
    mine = sel[bit]
    send = stay_ref[1 - mine] + got_ref[1 - mine].astype(F32)
    send_ref[...] = (resplit(send, units) if units else send).astype(BF16)
    keep_ref[...] = stay_ref[mine] + got_ref[mine].astype(F32)


def join_kernel(g_ref, g_got_ref, u_ref, u_got_ref, out_ref, *, units):
    g = resplit(g_ref[...] + g_got_ref[...].astype(F32), units)
    u = u_ref[...] + u_got_ref[...].astype(F32)
    rows = out_ref.shape[1]
    width = g.shape[1]
    for i in range(out_ref.shape[0]):
        out_ref[i, :, :width] = g[i * rows : (i + 1) * rows].astype(BF16)
        out_ref[i, :, width:] = u[i * rows : (i + 1) * rows].astype(BF16)


def hidden_kernel(in_ref, out_ref, *, units, width):
    sums = jnp.sum(in_ref[...].astype(F32), axis=0)
    power = jnp.sum(sums[:, units : units + 3], axis=1, keepdims=True) / D
    inv = lax.rsqrt(power + 1e-06)
    gate, upper = sums[:, :units] * inv, sums[:, width:] * inv
    out = (gate / (1.0 + jnp.exp(-gate)) * upper).astype(BF16)
    for i in range(out_ref.shape[0]):
        out_ref[i] = out


def swap(x, axis, mask):
    n = lax.axis_size(axis)
    return lax.ppermute(x, axis, [(i, i ^ mask) for i in range(n)])


def doubled(x, axis, bits):
    here = lax.axis_index(axis)
    for bit in bits:
        got = swap(x, axis, 1 << bit)
        first = ((here >> bit) & 1) == 0
        x = jnp.where(first, jnp.concatenate([x, got]), jnp.concatenate([got, x]))
    return x


def per_device(
    queries,
    cache_keys,
    cache_values,
    seg_keys,
    seg_values,
    lengths,
    residual_stream,
    out_weight,
    norm_gain,
    gate_weight,
    up_weight,
    down_weight,
):
    rows, width = queries.shape
    _, stretch, head = cache_keys.shape
    group = width // head
    n_ctx, n_tp = lax.axis_size("ctx"), lax.axis_size("tp")
    tokens = rows * n_ctx
    c = lax.axis_index("ctx")
    trows = residual_stream.shape[0]
    feats = residual_stream.shape[1]
    units = gate_weight.shape[1]

    each = rows * group
    q_all = jnp.broadcast_to(queries.reshape(1, each, head), (n_ctx, each, head))
    q_all = lax.all_to_all(q_all, "ctx", 0, 0, tiled=True)
    where = jnp.stack([lengths[0], c * rows])
    vmem = pl.BlockSpec(memory_space=pltpu.VMEM)
    smem = pl.BlockSpec(memory_space=pltpu.SMEM)
    anywhere = pl.BlockSpec(memory_space=pl.ANY)
    params = pltpu.CompilerParams(vmem_limit_bytes=60 * 2**20)
    small = pltpu.CompilerParams(vmem_limit_bytes=24 * 2**20)
    partial = pl.pallas_call(
        functools.partial(attend_kernel, tokens=tokens, group=group, head=head, scale=1.0 / math.sqrt(head)),
        out_shape=jax.ShapeDtypeStruct((n_ctx, each + 8, head), BF16),
        in_specs=[smem, vmem, anywhere, anywhere, vmem, vmem],
        out_specs=vmem,
        scratch_shapes=[
            pltpu.VMEM((stretch, head), BF16),
            pltpu.VMEM((stretch, head), BF16),
            pltpu.SemaphoreType.DMA((2,)),
        ],
        compiler_params=params,
        cost_estimate=pl.CostEstimate(
            flops=4 * tokens * width * stretch, bytes_accessed=2**21, transcendentals=tokens * group * stretch
        ),
        name="attend",
    )(where, q_all, cache_keys[0], cache_values[0], seg_keys, seg_values)
    parts = lax.all_to_all(partial, "ctx", 0, 0, tiled=True)
    attention, copies = pl.pallas_call(
        merge_kernel,
        out_shape=(jax.ShapeDtypeStruct((each, head), BF16), jax.ShapeDtypeStruct((n_ctx, each, head), BF16)),
        in_specs=[vmem],
        out_specs=(vmem, vmem),
        compiler_params=small,
        name="merge",
    )(parts)
    attention = attention.reshape(rows, width)
    heads_all = lax.all_to_all(copies, "ctx", 0, 0, tiled=True).reshape(tokens, width)
    mixed = jnp.dot(heads_all, out_weight, preferred_element_type=F32)

    def sum_tp(x):
        x = x.astype(BF16).reshape(n_tp, trows, feats)
        return jnp.sum(lax.all_to_all(x, "tp", 0, 0, tiled=True).astype(F32), axis=0)

    own = (residual_stream.astype(F32) + sum_tp(mixed)).astype(BF16)
    stream = jnp.broadcast_to(own[None], (n_tp, trows, feats))
    stream = lax.all_to_all(stream, "tp", 0, 0, tiled=True).reshape(tokens, feats)

    y_hi, z_lo = c & 1, (c >> 1) & 1
    sel = jnp.stack([y_hi, z_lo])
    quarter = tokens // 4
    wide_units = -(-(units + 3) // 128) * 128

    def project(weight, bit, power):
        out = wide_units if power else units
        return pl.pallas_call(
            functools.partial(project_kernel, bit=bit, power=power),
            out_shape=(
                jax.ShapeDtypeStruct((2, quarter, out), BF16),
                jax.ShapeDtypeStruct((2, quarter, out), F32),
            ),
            in_specs=[smem, vmem, vmem, vmem],
            out_specs=(vmem, vmem),
            compiler_params=small,
            cost_estimate=pl.CostEstimate(flops=2 * tokens * feats * units, bytes_accessed=2**21, transcendentals=0),
            name="gate" if power else "up",
        )(sel, stream, norm_gain[None], weight.T)

    def halve(stay, got, bit, power):
        out = stay.shape[2]
        return pl.pallas_call(
            functools.partial(halve_kernel, bit=bit, units=units if power else 0),
            out_shape=(jax.ShapeDtypeStruct((quarter, out), BF16), jax.ShapeDtypeStruct((quarter, out), F32)),
            in_specs=[smem, vmem, vmem],
            out_specs=(vmem, vmem),
            compiler_params=small,
            name="halve_gate" if power else "halve_up",
        )(sel, stay, got)

    g_send, g_stay = project(gate_weight, 1, True)
    g_got = swap(g_send, "ctx", 2)
    u_send, u_stay = project(up_weight, 0, False)
    u_got = swap(u_send, "ctx", 1)
    g_send, g_stay = halve(g_stay, g_got, 0, True)
    g_got = swap(g_send, "ctx", 1)
    u_send, u_stay = halve(u_stay, u_got, 1, False)
    u_got = swap(u_send, "ctx", 2)
    far = n_ctx // 4
    sums = pl.pallas_call(
        functools.partial(join_kernel, units=units),
        out_shape=jax.ShapeDtypeStruct((far, rows, wide_units + units), BF16),
        in_specs=[vmem] * 4,
        out_specs=vmem,
        compiler_params=small,
        name="join",
    )(g_stay, g_got, u_stay, u_got)
    groups = [[j * 4 + q for j in range(far)] for q in range(4)]
    sums = lax.all_to_all(sums, "ctx", 0, 0, axis_index_groups=groups, tiled=True)
    hidden = pl.pallas_call(
        functools.partial(hidden_kernel, units=units, width=wide_units),
        out_shape=jax.ShapeDtypeStruct((far, rows, units), BF16),
        in_specs=[vmem],
        out_specs=vmem,
        compiler_params=small,
        name="hidden",
    )(sums)
    hidden = lax.all_to_all(hidden, "ctx", 0, 0, axis_index_groups=groups, tiled=True).reshape(quarter, units)
    hidden = doubled(hidden, "ctx", (1, 0))
    lowered = jnp.dot(hidden, down_weight, preferred_element_type=F32)
    layer_out = (own.astype(F32) + sum_tp(lowered)).astype(BF16)
    return (attention, layer_out)


def solution(mesh):
    return jax.shard_map(
        per_device,
        mesh=mesh,
        in_specs=(
            P("ctx", "tp"),
            P("tp", "ctx", None),
            P("tp", "ctx", None),
            P("ctx", "tp"),
            P("ctx", "tp"),
            P("ctx"),
            P("tp", "ctx"),
            P("tp", "ctx"),
            P("ctx"),
            P("ctx", "tp"),
            P("ctx", "tp"),
            P("tp", "ctx"),
        ),
        out_specs=(P("ctx", "tp"), P("tp", "ctx")),
        check_vma=False,
    )
```

```python
import functools
import math

import jax
import jax.numpy as jnp
from jax import lax
from jax.experimental import pallas as pl
from jax.experimental.pallas import tpu as pltpu
from jax.sharding import PartitionSpec as P

D = 8192
F32 = jnp.float32
BF16 = jnp.bfloat16
LOW = -1e30
SPAN = 512


def three_parts(x):
    one = x.astype(BF16).astype(F32)
    rest = x - one
    two = rest.astype(BF16).astype(F32)
    return one, two, (rest - two).astype(BF16).astype(F32)


def attend_kernel(
    where, q_ref, k_hbm, v_hbm, sk_ref, sv_ref, out_ref, k_ref, v_ref, sems, *, tokens, group, head, scale
):
    k_copy = pltpu.make_async_copy(k_hbm, k_ref, sems.at[0])
    v_copy = pltpu.make_async_copy(v_hbm, v_ref, sems.at[1])
    k_copy.start()
    v_copy.start()
    length = where[0]
    first = where[1]
    rows = tokens * group
    own = sk_ref.shape[0]
    query = q_ref[...].reshape(rows, head)
    unit = scale / math.log(2.0)

    def scores(keys):
        return lax.dot_general(keys, query, (((1,), (1,)), ((), ())), preferred_element_type=F32)

    def weigh(values, w):
        return lax.dot_general(values, w.astype(BF16), (((0,), (0,)), ((), ())), preferred_element_type=F32)

    def add(carry, s, values):
        top, total, numer = carry
        top_new = jnp.maximum(top, jnp.max(s, axis=0, keepdims=True))
        fade = jnp.exp2((top - top_new) * unit)
        w = jnp.exp2((s - top_new) * unit)
        return top_new, total * fade + jnp.sum(w, axis=0, keepdims=True), numer * fade + weigh(values, w)

    s = scores(sk_ref[...])
    token = lax.broadcasted_iota(jnp.int32, (own, rows), 1) // group
    place = first + lax.broadcasted_iota(jnp.int32, (own, rows), 0)
    seen = place <= token
    s = jnp.where(seen, s, LOW)
    top = jnp.max(s, axis=0, keepdims=True)
    w = jnp.where(seen, jnp.exp2((s - top) * unit), 0.0)
    total = jnp.sum(w, axis=0, keepdims=True)
    numer = weigh(sv_ref[...], w)
    k_copy.wait()
    v_copy.wait()

    def whole(step, carry):
        at = pl.ds(pl.multiple_of(step * SPAN, SPAN), SPAN)
        return add(carry, scores(k_ref[at, :]), v_ref[at, :])

    full = length // SPAN
    carry = lax.fori_loop(0, full, whole, (top, total, numer))

    def part(step, carry):
        at = pl.ds(pl.multiple_of(step * SPAN, SPAN), SPAN)
        s = scores(k_ref[at, :])
        live = step * SPAN + lax.broadcasted_iota(jnp.int32, s.shape, 0) < length
        return add(carry, jnp.where(live, s, LOW), v_ref[at, :])

    top, total, numer = lax.fori_loop(full, (length + SPAN - 1) // SPAN, part, carry)
    blocks = out_ref.shape[0]
    each = rows // blocks
    out_ref[:, :each, :] = (numer / total).T.astype(BF16).reshape(blocks, each, head)
    stats = jnp.concatenate([*three_parts(top * unit), *three_parts(total), jnp.zeros((2, rows), F32)], axis=0)
    stats = jnp.concatenate([stats, jnp.zeros((8, rows), F32)], axis=0)
    spare = jnp.zeros((out_ref.shape[1] - each, head - each), F32)
    for i in range(blocks):
        tail = stats[: out_ref.shape[1] - each, i * each : (i + 1) * each]
        out_ref[i, each:, :] = jnp.concatenate([tail, spare], axis=1).astype(BF16)


def merge_kernel(in_ref, out_ref, copies_ref):
    blocks, rows, head = copies_ref.shape
    stat = [in_ref[:, rows + i, :].astype(F32) for i in range(6)]
    top = stat[0] + stat[1] + stat[2]
    total = stat[3] + stat[4] + stat[5]
    w = jnp.exp2(top - jnp.max(top, axis=0, keepdims=True)) * total
    w = (w / jnp.sum(w, axis=0, keepdims=True)).T
    out = jnp.zeros((rows, head), F32)
    for i in range(blocks):
        out = out + in_ref[i, :rows, :].astype(F32) * w[:rows, i : i + 1]
    out = out.astype(BF16)
    out_ref[...] = out
    for i in range(blocks):
        copies_ref[i] = out


def project_kernel(place, x_ref, *refs):
    out_ref = refs[-1]
    w_refs = refs[:-1]
    _, units, _ = w_refs[0].shape
    blocks, rows, width = out_ref.shape
    half = width // 2
    near = place[0]

    def product(kind):
        y = 0.0
        for m, w_ref in enumerate(w_refs):
            y = y + lax.dot_general(x_ref[near ^ m], w_ref[kind], (((1,), (1,)), ((), ())), preferred_element_type=F32)
        return y

    squares = 0.0
    for i in range(x_ref.shape[0]):
        x = x_ref[i].astype(F32)
        squares = squares + jnp.sum(x * x, axis=1, keepdims=True)
    tokens = squares.shape[0]
    spare = jnp.zeros((tokens, half - units - 3), F32)
    gate = jnp.concatenate([product(0), *three_parts(squares), spare], axis=1).astype(BF16)
    up = product(1).astype(BF16)
    for i in range(blocks):
        out_ref[i, :, :half] = gate[i * rows : (i + 1) * rows]
        out_ref[i, :, half : half + units] = up[i * rows : (i + 1) * rows]
        out_ref[i, :, half + units :] = jnp.zeros((rows, half - units), BF16)


def hidden_kernel(in_ref, out_ref):
    blocks, _, units = out_ref.shape
    half = in_ref.shape[2] // 2
    sums = jnp.sum(in_ref[...].astype(F32), axis=0)
    power = jnp.sum(sums[:, units : units + 3], axis=1, keepdims=True) / D
    inv = lax.rsqrt(power + 1e-06)
    gate, upper = sums[:, :units] * inv, sums[:, half : half + units] * inv
    out = (gate / (1.0 + jnp.exp(-gate)) * upper).astype(BF16)
    for i in range(blocks):
        out_ref[i] = out


def down_kernel(place, h_ref, *refs):
    out_ref = refs[-1]
    w_refs = refs[:-1]
    rows = out_ref.shape[1]
    each = out_ref.shape[0] // len(w_refs)
    near = place[0]
    for m, w_ref in enumerate(w_refs):
        y = jnp.dot(h_ref[...], w_ref[2], preferred_element_type=F32)
        for k in range(each):
            out_ref[(near ^ m) * each + k] = y[k * rows : (k + 1) * rows].astype(BF16)


def per_device(
    queries,
    cache_keys,
    cache_values,
    seg_keys,
    seg_values,
    lengths,
    residual_stream,
    out_weight,
    norm_gain,
    gate_weight,
    up_weight,
    down_weight,
):
    rows, width = queries.shape
    _, stretch, head = cache_keys.shape
    group = width // head
    n_far, n_near, n_tp = lax.axis_size("far"), lax.axis_size("near"), lax.axis_size("tp")
    n_ctx = n_far * n_near
    ctx = ("far", "near")
    tokens = rows * n_ctx
    c = lax.axis_index(ctx)
    trows = residual_stream.shape[0]
    feats = residual_stream.shape[1]
    units = gate_weight.shape[1] // n_near

    near = lax.axis_index("near")

    def chunk(place):
        def part(w):
            return lax.dynamic_slice_in_dim(w, place * units, units, 0)

        gate, upper = part(gate_weight.T).astype(F32) * norm_gain, part(up_weight.T).astype(F32) * norm_gain
        return jnp.stack([gate.astype(BF16), upper.astype(BF16), part(down_weight)])

    def trade(m, place):
        return lax.ppermute(chunk(place ^ m), "near", [(i, i ^ m) for i in range(4)])

    weights = [chunk(near)]
    each = rows * group
    q_all = jnp.broadcast_to(queries.reshape(1, each, head), (n_ctx, each, head))
    q_all = lax.all_to_all(q_all, ctx, 0, 0, tiled=True)
    q_all, w, place = lax.optimization_barrier((q_all, trade(1, near), near))
    weights.append(w)
    where = jnp.stack([lengths[0], c * rows])
    vmem = pl.BlockSpec(memory_space=pltpu.VMEM)
    smem = pl.BlockSpec(memory_space=pltpu.SMEM)
    anywhere = pl.BlockSpec(memory_space=pl.ANY)
    params = pltpu.CompilerParams(vmem_limit_bytes=60 * 2**20)
    small = pltpu.CompilerParams(vmem_limit_bytes=24 * 2**20)
    partial = pl.pallas_call(
        functools.partial(attend_kernel, tokens=tokens, group=group, head=head, scale=1.0 / math.sqrt(head)),
        out_shape=jax.ShapeDtypeStruct((n_ctx, each + 8, head), BF16),
        in_specs=[smem, vmem, anywhere, anywhere, vmem, vmem],
        out_specs=vmem,
        scratch_shapes=[
            pltpu.VMEM((stretch, head), BF16),
            pltpu.VMEM((stretch, head), BF16),
            pltpu.SemaphoreType.DMA((2,)),
        ],
        compiler_params=params,
        cost_estimate=pl.CostEstimate(
            flops=4 * tokens * width * stretch, bytes_accessed=2**21, transcendentals=tokens * group * stretch
        ),
        name="attend",
    )(where, q_all, cache_keys[0], cache_values[0], seg_keys, seg_values)
    parts = lax.all_to_all(partial, ctx, 0, 0, tiled=True)
    parts, w, place = lax.optimization_barrier((parts, trade(2, place), place))
    weights.append(w)
    attention, copies = pl.pallas_call(
        merge_kernel,
        out_shape=(jax.ShapeDtypeStruct((each, head), BF16), jax.ShapeDtypeStruct((n_ctx, each, head), BF16)),
        in_specs=[vmem],
        out_specs=(vmem, vmem),
        compiler_params=small,
        name="merge",
    )(parts)
    attention = attention.reshape(rows, width)
    heads_all = lax.all_to_all(copies, ctx, 0, 0, tiled=True)
    heads_all, w = lax.optimization_barrier((heads_all, trade(3, place)))
    heads_all = heads_all.reshape(tokens, width)
    weights.append(w)
    mixed = jnp.dot(heads_all, out_weight, preferred_element_type=F32)

    mixed = mixed.astype(BF16).reshape(n_tp, trows, feats)
    mixed = jnp.sum(lax.all_to_all(mixed, "tp", 0, 0, tiled=True).astype(F32), axis=0)
    own = (residual_stream.astype(F32) + mixed).astype(BF16)
    stream = jnp.broadcast_to(own[None], (n_near * n_tp, trows, feats))
    stream = lax.all_to_all(stream, ("near", "tp"), 0, 0, tiled=True).reshape(n_near, tokens, feats)

    half = -(-(units + 3) // 128) * 128
    block = tokens // n_far
    sums = pl.pallas_call(
        project_kernel,
        out_shape=jax.ShapeDtypeStruct((n_far, block, 2 * half), BF16),
        in_specs=[smem] + [vmem] * 5,
        out_specs=vmem,
        compiler_params=small,
        name="project",
    )(near[None], stream, *weights)
    sums = lax.all_to_all(sums, "far", 0, 0, tiled=True)
    hidden = pl.pallas_call(
        hidden_kernel,
        out_shape=jax.ShapeDtypeStruct((n_far, block, units), BF16),
        in_specs=[vmem],
        out_specs=vmem,
        compiler_params=small,
        name="hidden",
    )(sums)
    hidden = lax.all_to_all(hidden, "far", 0, 0, tiled=True).reshape(tokens, units)
    lowered = pl.pallas_call(
        down_kernel,
        out_shape=jax.ShapeDtypeStruct((n_near * n_tp, trows, feats), BF16),
        in_specs=[smem] + [vmem] * 5,
        out_specs=vmem,
        compiler_params=small,
        name="down",
    )(near[None], hidden, *weights)
    lowered = lax.all_to_all(lowered, ("near", "tp"), 0, 0, tiled=True)
    layer_out = (own.astype(F32) + jnp.sum(lowered.astype(F32), axis=0)).astype(BF16)
    return (attention, layer_out)


def solution(mesh):
    fine = jax.sharding.Mesh(mesh.devices.reshape(-1, 4, mesh.shape["tp"]), ("far", "near", "tp"))
    ctx = ("far", "near")
    return jax.shard_map(
        per_device,
        mesh=fine,
        in_specs=(
            P(ctx, "tp"),
            P("tp", ctx, None),
            P("tp", ctx, None),
            P(ctx, "tp"),
            P(ctx, "tp"),
            P(ctx),
            P("tp", ctx),
            P("tp", ctx),
            P(ctx),
            P(ctx, "tp"),
            P(ctx, "tp"),
            P("tp", ctx),
        ),
        out_specs=(P(ctx, "tp"), P("tp", ctx)),
        check_vma=False,
    )
```

```python
import functools
import math

import jax
import jax.numpy as jnp
from jax import lax
from jax.experimental import pallas as pl
from jax.experimental.pallas import tpu as pltpu
from jax.sharding import PartitionSpec as P

D = 8192
F32 = jnp.float32
BF16 = jnp.bfloat16
LOW = -1e30
SPAN = 512


def three_parts(x):
    one = x.astype(BF16).astype(F32)
    rest = x - one
    two = rest.astype(BF16).astype(F32)
    return one, two, (rest - two).astype(BF16).astype(F32)


def attend_kernel(
    lengths, q_ref, k_hbm, v_hbm, sk_ref, sv_ref, out_ref, k_ref, v_ref, sems, *, tokens, group, head, scale
):
    k_copy = pltpu.make_async_copy(k_hbm, k_ref, sems.at[0])
    v_copy = pltpu.make_async_copy(v_hbm, v_ref, sems.at[1])
    k_copy.start()
    v_copy.start()
    length = lengths[0]
    rows = tokens * group
    own = sk_ref.shape[0]
    first = lax.axis_index(("far", "near")) * own
    query = q_ref[...].reshape(rows, head)
    unit = scale / math.log(2.0)

    def scores(keys):
        return lax.dot_general(keys, query, (((1,), (1,)), ((), ())), preferred_element_type=F32)

    def weigh(values, w):
        return lax.dot_general(values, w.astype(BF16), (((0,), (0,)), ((), ())), preferred_element_type=F32)

    def add(carry, s, values):
        top, total, numer = carry
        top_new = jnp.maximum(top, jnp.max(s, axis=0, keepdims=True))
        fade = jnp.exp2((top - top_new) * unit)
        w = jnp.exp2((s - top_new) * unit)
        return top_new, total * fade + jnp.sum(w, axis=0, keepdims=True), numer * fade + weigh(values, w)

    s = scores(sk_ref[...])
    token = lax.broadcasted_iota(jnp.int32, (own, rows), 1) // group
    place = first + lax.broadcasted_iota(jnp.int32, (own, rows), 0)
    seen = place <= token
    s = jnp.where(seen, s, LOW)
    top = jnp.max(s, axis=0, keepdims=True)
    w = jnp.where(seen, jnp.exp2((s - top) * unit), 0.0)
    total = jnp.sum(w, axis=0, keepdims=True)
    numer = weigh(sv_ref[...], w)
    k_copy.wait()
    v_copy.wait()

    def whole(step, carry):
        at = pl.ds(pl.multiple_of(step * SPAN, SPAN), SPAN)
        return add(carry, scores(k_ref[at, :]), v_ref[at, :])

    full = length // SPAN
    carry = lax.fori_loop(0, full, whole, (top, total, numer))

    def part(step, carry):
        at = pl.ds(pl.multiple_of(step * SPAN, SPAN), SPAN)
        s = scores(k_ref[at, :])
        live = step * SPAN + lax.broadcasted_iota(jnp.int32, s.shape, 0) < length
        return add(carry, jnp.where(live, s, LOW), v_ref[at, :])

    top, total, numer = lax.fori_loop(full, (length + SPAN - 1) // SPAN, part, carry)
    blocks = out_ref.shape[0]
    each = rows // blocks
    out_ref[:, :each, :] = (numer / total).T.astype(BF16).reshape(blocks, each, head)
    stats = jnp.concatenate([*three_parts(top * unit), *three_parts(total), jnp.zeros((2, rows), F32)], axis=0)
    stats = jnp.concatenate([stats, jnp.zeros((8, rows), F32)], axis=0)
    spare = jnp.zeros((out_ref.shape[1] - each, head - each), F32)
    for i in range(blocks):
        tail = stats[: out_ref.shape[1] - each, i * each : (i + 1) * each]
        out_ref[i, each:, :] = jnp.concatenate([tail, spare], axis=1).astype(BF16)


def merge_kernel(in_ref, out_ref, copies_ref):
    blocks, rows, head = copies_ref.shape
    stat = [in_ref[:, rows + i, :].astype(F32) for i in range(6)]
    top = stat[0] + stat[1] + stat[2]
    total = stat[3] + stat[4] + stat[5]
    w = jnp.exp2(top - jnp.max(top, axis=0, keepdims=True)) * total
    w = (w / jnp.sum(w, axis=0, keepdims=True)).T
    out = jnp.zeros((rows, head), F32)
    for i in range(blocks):
        out = out + in_ref[i, :rows, :].astype(F32) * w[:rows, i : i + 1]
    out = out.astype(BF16)
    out_ref[...] = out
    for i in range(blocks):
        copies_ref[i] = out


def out_kernel(h_ref, w_ref, out_ref, wide_ref):
    blocks, rows, _ = out_ref.shape
    tokens = blocks * rows
    head = h_ref.shape[2]
    group = w_ref.shape[0] // head
    wide_ref[...] = h_ref[...].astype(F32).reshape(tokens * group, head)
    y = 0.0
    for g in range(group):
        x = wide_ref[pl.ds(g, tokens, stride=group), :].astype(BF16)
        y = y + jnp.dot(x, w_ref[g * head : (g + 1) * head, :], preferred_element_type=F32)
    for i in range(blocks):
        out_ref[i] = y[i * rows : (i + 1) * rows].astype(BF16)


def stream_kernel(in_ref, residual_ref, own_ref, copies_ref):
    own = jnp.sum(in_ref[...].astype(F32), axis=0) + residual_ref[...].astype(F32)
    own = own.astype(BF16)
    own_ref[...] = own
    for i in range(copies_ref.shape[0]):
        copies_ref[i] = own


def last_kernel(in_ref, own_ref, out_ref):
    out_ref[...] = (own_ref[...].astype(F32) + jnp.sum(in_ref[...].astype(F32), axis=0)).astype(BF16)


def project_kernel(x_ref, *refs):
    out_ref = refs[-1]
    gates, ups = refs[: len(refs) // 2], refs[len(refs) // 2 : -1]
    units = gates[0].shape[0]
    slices = len(gates)
    each = x_ref.shape[0] // slices
    blocks, rows, width = out_ref.shape
    half = width // 2
    near = lax.axis_index("near")
    xs = []
    for m in range(slices):
        at = (near ^ m) * each
        xs.append(jnp.concatenate([x_ref[at + i].astype(F32) for i in range(each)], axis=0))

    def product(w_refs):
        y = 0.0
        for x, w_ref in zip(xs, w_refs):
            y = y + lax.dot_general(
                x.astype(BF16), w_ref[...], (((1,), (1,)), ((), ())), preferred_element_type=F32
            )
        return y

    squares = 0.0
    for x in xs:
        squares = squares + jnp.sum(x * x, axis=1, keepdims=True)
    tokens = squares.shape[0]
    spare = jnp.zeros((tokens, half - units - 3), F32)
    gate = jnp.concatenate([product(gates), *three_parts(squares), spare], axis=1).astype(BF16)
    up = product(ups).astype(BF16)
    for i in range(blocks):
        out_ref[i, :, :half] = gate[i * rows : (i + 1) * rows]
        out_ref[i, :, half : half + units] = up[i * rows : (i + 1) * rows]
        out_ref[i, :, half + units :] = jnp.zeros((rows, half - units), BF16)


def hidden_kernel(in_ref, out_ref):
    blocks, _, units = out_ref.shape
    half = in_ref.shape[2] // 2
    sums = jnp.sum(in_ref[...].astype(F32), axis=0)
    power = jnp.sum(sums[:, units : units + 3], axis=1, keepdims=True) / D
    inv = lax.rsqrt(power + 1e-06)
    gate, upper = sums[:, :units] * inv, sums[:, half : half + units] * inv
    out = (gate / (1.0 + jnp.exp(-gate)) * upper).astype(BF16)
    for i in range(blocks):
        out_ref[i] = out


def down_kernel(h_ref, *refs):
    out_ref = refs[-1]
    w_refs = refs[:-1]
    rows = out_ref.shape[1]
    each = out_ref.shape[0] // len(w_refs)
    near = lax.axis_index("near")
    for m, w_ref in enumerate(w_refs):
        y = jnp.dot(h_ref[...], w_ref[...], preferred_element_type=F32)
        for k in range(each):
            out_ref[(near ^ m) * each + k] = y[k * rows : (k + 1) * rows].astype(BF16)


def per_device(
    queries,
    cache_keys,
    cache_values,
    seg_keys,
    seg_values,
    lengths,
    residual_stream,
    out_weight,
    norm_gain,
    gate_weight,
    up_weight,
    down_weight,
):
    rows, width = queries.shape
    _, stretch, head = cache_keys.shape
    group = width // head
    n_far, n_near, n_tp = lax.axis_size("far"), lax.axis_size("near"), lax.axis_size("tp")
    n_ctx = n_far * n_near
    ctx = ("far", "near")
    tokens = rows * n_ctx
    trows = residual_stream.shape[0]
    feats = residual_stream.shape[1]
    units = gate_weight.shape[1] // n_near

    near = lax.axis_index("near")

    def chunk(kind, place):
        w = (gate_weight.T, up_weight.T, down_weight)[kind]
        w = lax.dynamic_slice_in_dim(w, place * units, units, 0)
        return w if kind == 2 else (w.astype(F32) * norm_gain).astype(BF16)

    weights = [[chunk(kind, near)] + [None] * 3 for kind in range(3)]
    place = near

    def beside(x, *trades):
        nonlocal place
        sent = [
            lax.ppermute(chunk(kind, place ^ m), "near", [(i, i ^ m) for i in range(4)]) for kind, m in trades
        ]
        x, place, *sent = lax.optimization_barrier((x, place, *sent))
        for (kind, m), w in zip(trades, sent):
            weights[kind][m] = w
        return x

    each = rows * group
    q_all = jnp.broadcast_to(queries.reshape(1, each, head), (n_ctx, each, head))
    q_all = lax.all_to_all(q_all, ctx, 0, 0, tiled=True)
    q_all = beside(q_all, (0, 1), (0, 2))
    vmem = pl.BlockSpec(memory_space=pltpu.VMEM)
    smem = pl.BlockSpec(memory_space=pltpu.SMEM)
    anywhere = pl.BlockSpec(memory_space=pl.ANY)
    params = pltpu.CompilerParams(vmem_limit_bytes=60 * 2**20)
    small = pltpu.CompilerParams(vmem_limit_bytes=24 * 2**20)
    partial = pl.pallas_call(
        functools.partial(attend_kernel, tokens=tokens, group=group, head=head, scale=1.0 / math.sqrt(head)),
        out_shape=jax.ShapeDtypeStruct((n_ctx, each + 8, head), BF16),
        in_specs=[smem, vmem, anywhere, anywhere, vmem, vmem],
        out_specs=vmem,
        scratch_shapes=[
            pltpu.VMEM((stretch, head), BF16),
            pltpu.VMEM((stretch, head), BF16),
            pltpu.SemaphoreType.DMA((2,)),
        ],
        compiler_params=params,
        cost_estimate=pl.CostEstimate(
            flops=4 * tokens * width * stretch, bytes_accessed=2**21, transcendentals=tokens * group * stretch
        ),
        name="attend",
    )(lengths, q_all, cache_keys[0], cache_values[0], seg_keys, seg_values)
    parts = lax.all_to_all(partial, ctx, 0, 0, tiled=True)
    parts = beside(parts, (1, 1), (1, 2))
    attention, copies = pl.pallas_call(
        merge_kernel,
        out_shape=(jax.ShapeDtypeStruct((each, head), BF16), jax.ShapeDtypeStruct((n_ctx, each, head), BF16)),
        in_specs=[vmem],
        out_specs=(vmem, vmem),
        compiler_params=small,
        name="merge",
    )(parts)
    attention = attention.reshape(rows, width)
    heads_all = lax.all_to_all(copies, ctx, 0, 0, tiled=True)
    heads_all = beside(heads_all, (0, 3), (1, 3))
    mixed = pl.pallas_call(
        out_kernel,
        out_shape=jax.ShapeDtypeStruct((n_tp, trows, feats), BF16),
        in_specs=[vmem] * 2,
        out_specs=vmem,
        scratch_shapes=[pltpu.VMEM((tokens * group, head), F32)],
        compiler_params=small,
        name="out",
    )(heads_all, out_weight)
    mixed = lax.all_to_all(mixed, "tp", 0, 0, tiled=True)
    own, stream = pl.pallas_call(
        stream_kernel,
        out_shape=(
            jax.ShapeDtypeStruct((trows, feats), BF16),
            jax.ShapeDtypeStruct((n_near * n_tp, trows, feats), BF16),
        ),
        in_specs=[vmem] * 2,
        out_specs=(vmem, vmem),
        compiler_params=small,
        name="stream",
    )(mixed, residual_stream)
    stream = lax.all_to_all(stream, ("near", "tp"), 0, 0, tiled=True)

    half = -(-(units + 3) // 128) * 128
    block = tokens // n_far
    sums = pl.pallas_call(
        project_kernel,
        out_shape=jax.ShapeDtypeStruct((n_far, block, 2 * half), BF16),
        in_specs=[vmem] * 9,
        out_specs=vmem,
        compiler_params=small,
        name="project",
    )(stream, *weights[0], *weights[1])
    sums = beside(lax.all_to_all(sums, "far", 0, 0, tiled=True), (2, 1), (2, 2))
    hidden = pl.pallas_call(
        hidden_kernel,
        out_shape=jax.ShapeDtypeStruct((n_far, block, units), BF16),
        in_specs=[vmem],
        out_specs=vmem,
        compiler_params=small,
        name="hidden",
    )(sums)
    hidden = beside(lax.all_to_all(hidden, "far", 0, 0, tiled=True), (2, 3)).reshape(tokens, units)
    lowered = pl.pallas_call(
        down_kernel,
        out_shape=jax.ShapeDtypeStruct((n_near * n_tp, trows, feats), BF16),
        in_specs=[vmem] * 5,
        out_specs=vmem,
        compiler_params=small,
        name="down",
    )(hidden, *weights[2])
    lowered = lax.all_to_all(lowered, ("near", "tp"), 0, 0, tiled=True)
    layer_out = pl.pallas_call(
        last_kernel,
        out_shape=jax.ShapeDtypeStruct((trows, feats), BF16),
        in_specs=[vmem] * 2,
        out_specs=vmem,
        compiler_params=small,
        name="last",
    )(lowered, own)
    return (attention, layer_out)


def solution(mesh):
    fine = jax.sharding.Mesh(mesh.devices.reshape(-1, 4, mesh.shape["tp"]), ("far", "near", "tp"))
    ctx = ("far", "near")
    return jax.shard_map(
        per_device,
        mesh=fine,
        in_specs=(
            P(ctx, "tp"),
            P("tp", ctx, None),
            P("tp", ctx, None),
            P(ctx, "tp"),
            P(ctx, "tp"),
            P(ctx),
            P("tp", ctx),
            P("tp", ctx),
            P(ctx),
            P(ctx, "tp"),
            P(ctx, "tp"),
            P("tp", ctx),
        ),
        out_specs=(P(ctx, "tp"), P("tp", ctx)),
        check_vma=False,
    )
```

```python
import functools
import math

import jax
import jax.numpy as jnp
from jax import lax
from jax.experimental import pallas as pl
from jax.experimental.pallas import tpu as pltpu
from jax.sharding import PartitionSpec as P

D = 8192
F32 = jnp.float32
BF16 = jnp.bfloat16
LOW = -1e30
SPAN = 512


def three_parts(x):
    one = x.astype(BF16).astype(F32)
    rest = x - one
    two = rest.astype(BF16).astype(F32)
    return one, two, (rest - two).astype(BF16).astype(F32)


def attend_kernel(
    lengths, q_ref, k_hbm, v_hbm, sk_hbm, sv_hbm, out_ref, k_ref, v_ref, sk_ref, sv_ref, sems,
    *, tokens, group, head, scale
):
    k_copy = pltpu.make_async_copy(k_hbm, k_ref, sems.at[0])
    v_copy = pltpu.make_async_copy(v_hbm, v_ref, sems.at[1])
    sk_copy = pltpu.make_async_copy(sk_hbm, sk_ref, sems.at[2])
    sv_copy = pltpu.make_async_copy(sv_hbm, sv_ref, sems.at[3])
    sk_copy.start()
    sv_copy.start()
    k_copy.start()
    v_copy.start()
    length = lengths[0]
    rows = tokens * group
    own = sk_ref.shape[0]
    first = lax.axis_index(("far", "lo", "hi")) * own
    query = q_ref[...].reshape(rows, head)
    unit = scale / math.log(2.0)

    def scores(keys):
        return lax.dot_general(keys, query, (((1,), (1,)), ((), ())), preferred_element_type=F32)

    def weigh(values, w):
        return lax.dot_general(values, w.astype(BF16), (((0,), (0,)), ((), ())), preferred_element_type=F32)

    def add(carry, s, values):
        top, total, numer = carry
        top_new = jnp.maximum(top, jnp.max(s, axis=0, keepdims=True))
        fade = jnp.exp2((top - top_new) * unit)
        w = jnp.exp2((s - top_new) * unit)
        return top_new, total * fade + jnp.sum(w, axis=0, keepdims=True), numer * fade + weigh(values, w)

    sk_copy.wait()
    sv_copy.wait()
    s = scores(sk_ref[...])
    token = lax.broadcasted_iota(jnp.int32, (own, rows), 1) // group
    place = first + lax.broadcasted_iota(jnp.int32, (own, rows), 0)
    seen = place <= token
    s = jnp.where(seen, s, LOW)
    top = jnp.max(s, axis=0, keepdims=True)
    w = jnp.where(seen, jnp.exp2((s - top) * unit), 0.0)
    total = jnp.sum(w, axis=0, keepdims=True)
    numer = weigh(sv_ref[...], w)
    k_copy.wait()
    v_copy.wait()

    def whole(step, carry):
        at = pl.ds(pl.multiple_of(step * SPAN, SPAN), SPAN)
        return add(carry, scores(k_ref[at, :]), v_ref[at, :])

    full = length // SPAN
    carry = lax.fori_loop(0, full, whole, (top, total, numer))

    def part(step, carry):
        at = pl.ds(pl.multiple_of(step * SPAN, SPAN), SPAN)
        s = scores(k_ref[at, :])
        live = step * SPAN + lax.broadcasted_iota(jnp.int32, s.shape, 0) < length
        return add(carry, jnp.where(live, s, LOW), v_ref[at, :])

    top, total, numer = lax.fori_loop(full, (length + SPAN - 1) // SPAN, part, carry)
    blocks = out_ref.shape[0]
    each = rows // blocks
    out_ref[:, :each, :] = (numer / total).T.astype(BF16).reshape(blocks, each, head)
    stats = jnp.concatenate([*three_parts(top * unit), *three_parts(total), jnp.zeros((2, rows), F32)], axis=0)
    stats = jnp.concatenate([stats, jnp.zeros((8, rows), F32)], axis=0)
    spare = jnp.zeros((out_ref.shape[1] - each, head - each), F32)
    for i in range(blocks):
        tail = stats[: out_ref.shape[1] - each, i * each : (i + 1) * each]
        out_ref[i, each:, :] = jnp.concatenate([tail, spare], axis=1).astype(BF16)


def merge_kernel(in_ref, out_ref, copies_ref):
    blocks, rows, head = copies_ref.shape
    stat = [in_ref[:, rows + i, :].astype(F32) for i in range(6)]
    top = stat[0] + stat[1] + stat[2]
    total = stat[3] + stat[4] + stat[5]
    w = jnp.exp2(top - jnp.max(top, axis=0, keepdims=True)) * total
    w = (w / jnp.sum(w, axis=0, keepdims=True)).T
    out = jnp.zeros((rows, head), F32)
    for i in range(blocks):
        out = out + in_ref[i, :rows, :].astype(F32) * w[:rows, i : i + 1]
    out = out.astype(BF16)
    out_ref[...] = out
    for i in range(blocks):
        copies_ref[i] = out


def out_kernel(h_ref, w_ref, out_ref, wide_ref):
    blocks, rows, _ = out_ref.shape
    tokens = blocks * rows
    head = h_ref.shape[2]
    group = w_ref.shape[0] // head
    wide_ref[...] = h_ref[...].astype(F32).reshape(tokens * group, head)
    y = 0.0
    for g in range(group):
        x = wide_ref[pl.ds(g, tokens, stride=group), :].astype(BF16)
        y = y + jnp.dot(x, w_ref[g * head : (g + 1) * head, :], preferred_element_type=F32)
    for i in range(blocks):
        out_ref[i] = y[i * rows : (i + 1) * rows].astype(BF16)


def stream_kernel(in_ref, residual_ref, own_ref, copies_ref):
    own = jnp.sum(in_ref[...].astype(F32), axis=0) + residual_ref[...].astype(F32)
    own = own.astype(BF16)
    own_ref[...] = own
    for i in range(copies_ref.shape[0]):
        copies_ref[i] = own


def last_kernel(in_ref, own_ref, out_ref):
    out_ref[...] = (own_ref[...].astype(F32) + jnp.sum(in_ref[...].astype(F32), axis=0)).astype(BF16)


def project_kernel(x_ref, *refs):
    out_ref = refs[-1]
    gates, ups = refs[: len(refs) // 2], refs[len(refs) // 2 : -1]
    units = gates[0].shape[0]
    slices = len(gates)
    each = x_ref.shape[0] // slices
    blocks, rows, width = out_ref.shape
    half = width // 2
    near = lax.axis_index(("lo", "hi"))
    xs = []
    for m in range(slices):
        at = (near ^ m) * each
        xs.append(jnp.concatenate([x_ref[at + i].astype(F32) for i in range(each)], axis=0))

    def product(w_refs):
        y = 0.0
        for x, w_ref in zip(xs, w_refs):
            y = y + lax.dot_general(
                x.astype(BF16), w_ref[...], (((1,), (1,)), ((), ())), preferred_element_type=F32
            )
        return y

    squares = 0.0
    for x in xs:
        squares = squares + jnp.sum(x * x, axis=1, keepdims=True)
    tokens = squares.shape[0]
    spare = jnp.zeros((tokens, half - units - 3), F32)
    gate = jnp.concatenate([product(gates), *three_parts(squares), spare], axis=1).astype(BF16)
    up = product(ups).astype(BF16)
    for i in range(blocks):
        out_ref[i, :, :half] = gate[i * rows : (i + 1) * rows]
        out_ref[i, :, half : half + units] = up[i * rows : (i + 1) * rows]
        out_ref[i, :, half + units :] = jnp.zeros((rows, half - units), BF16)


def hidden_kernel(in_ref, out_ref):
    blocks, _, units = out_ref.shape
    half = in_ref.shape[2] // 2
    sums = jnp.sum(in_ref[...].astype(F32), axis=0)
    power = jnp.sum(sums[:, units : units + 3], axis=1, keepdims=True) / D
    inv = lax.rsqrt(power + 1e-06)
    gate, upper = sums[:, :units] * inv, sums[:, half : half + units] * inv
    out = (gate / (1.0 + jnp.exp(-gate)) * upper).astype(BF16)
    for i in range(blocks):
        out_ref[i] = out


def down_kernel(mine_ref, other_ref, w_ref, wy_ref, out_ref):
    rows = out_ref.shape[1]
    each = out_ref.shape[0] // 2
    lo, hi = lax.axis_index("lo"), lax.axis_index("hi")
    for at, ref in ((hi, w_ref), (1 - hi, wy_ref)):
        y = jnp.dot(mine_ref[...], ref[lo], preferred_element_type=F32)
        y = y + jnp.dot(other_ref[...], ref[1 - lo], preferred_element_type=F32)
        for k in range(each):
            out_ref[at * each + k] = y[k * rows : (k + 1) * rows].astype(BF16)


def per_device(
    queries,
    cache_keys,
    cache_values,
    seg_keys,
    seg_values,
    lengths,
    residual_stream,
    out_weight,
    norm_gain,
    gate_weight,
    up_weight,
    down_weight,
):
    rows, width = queries.shape
    _, stretch, head = cache_keys.shape
    group = width // head
    near_axes = ("lo", "hi")
    n_far, n_near, n_tp = lax.axis_size("far"), lax.axis_size(near_axes), lax.axis_size("tp")
    n_ctx = n_far * n_near
    ctx = ("far", *near_axes)
    tokens = rows * n_ctx
    trows = residual_stream.shape[0]
    feats = residual_stream.shape[1]
    units = gate_weight.shape[1] // n_near

    near = lax.axis_index(near_axes)

    def chunk(w, place):
        w = lax.dynamic_slice_in_dim(w.T, place * units, units, 0)
        return (w.astype(F32) * norm_gain).astype(BF16)

    def trade(w, m):
        return lambda place: lax.ppermute(chunk(w, place ^ m), near_axes, [(i, i ^ m) for i in range(4)])

    def down_chunk(place):
        lows = [
            lax.dynamic_slice_in_dim(down_weight, (2 * lo + (place & 1)) * units, units, 0) for lo in range(2)
        ]
        return jnp.stack(lows)

    def down_trade(place):
        return lax.ppermute(down_chunk(place ^ 1), "hi", [(0, 1), (1, 0)])

    place = near

    def beside(x, *trades):
        nonlocal place
        x, place, *sent = lax.optimization_barrier((x, place, *[t(place) for t in trades]))
        return x, *sent

    each = rows * group
    q_all = jnp.broadcast_to(queries.reshape(1, each, head), (n_ctx, each, head))
    q_all = lax.all_to_all(q_all, ctx, 0, 0, tiled=True)
    q_all, gate_1, gate_2 = beside(q_all, trade(gate_weight, 1), trade(gate_weight, 2))
    vmem = pl.BlockSpec(memory_space=pltpu.VMEM)
    smem = pl.BlockSpec(memory_space=pltpu.SMEM)
    anywhere = pl.BlockSpec(memory_space=pl.ANY)
    params = pltpu.CompilerParams(vmem_limit_bytes=60 * 2**20)
    small = pltpu.CompilerParams(vmem_limit_bytes=24 * 2**20)
    partial = pl.pallas_call(
        functools.partial(attend_kernel, tokens=tokens, group=group, head=head, scale=1.0 / math.sqrt(head)),
        out_shape=jax.ShapeDtypeStruct((n_ctx, each + 8, head), BF16),
        in_specs=[smem, vmem] + [anywhere] * 4,
        out_specs=vmem,
        scratch_shapes=[
            pltpu.VMEM((stretch, head), BF16),
            pltpu.VMEM((stretch, head), BF16),
            pltpu.VMEM(seg_keys.shape, BF16),
            pltpu.VMEM(seg_values.shape, BF16),
            pltpu.SemaphoreType.DMA((4,)),
        ],
        compiler_params=params,
        cost_estimate=pl.CostEstimate(
            flops=4 * tokens * width * stretch, bytes_accessed=2**21, transcendentals=tokens * group * stretch
        ),
        name="attend",
    )(lengths, q_all, cache_keys[0], cache_values[0], seg_keys, seg_values)
    parts = lax.all_to_all(partial, ctx, 0, 0, tiled=True)
    parts, up_1, up_2 = beside(parts, trade(up_weight, 1), trade(up_weight, 2))
    attention, copies = pl.pallas_call(
        merge_kernel,
        out_shape=(jax.ShapeDtypeStruct((each, head), BF16), jax.ShapeDtypeStruct((n_ctx, each, head), BF16)),
        in_specs=[vmem],
        out_specs=(vmem, vmem),
        compiler_params=small,
        name="merge",
    )(parts)
    attention = attention.reshape(rows, width)
    heads_all = lax.all_to_all(copies, ctx, 0, 0, tiled=True)
    heads_all, gate_3 = beside(heads_all, trade(gate_weight, 3))
    mixed = pl.pallas_call(
        out_kernel,
        out_shape=jax.ShapeDtypeStruct((n_tp, trows, feats), BF16),
        in_specs=[vmem] * 2,
        out_specs=vmem,
        scratch_shapes=[pltpu.VMEM((tokens * group, head), F32)],
        compiler_params=small,
        name="out",
    )(heads_all, out_weight)
    mixed = lax.all_to_all(mixed, "tp", 0, 0, tiled=True)
    own, stream = pl.pallas_call(
        stream_kernel,
        out_shape=(
            jax.ShapeDtypeStruct((trows, feats), BF16),
            jax.ShapeDtypeStruct((n_near * n_tp, trows, feats), BF16),
        ),
        in_specs=[vmem] * 2,
        out_specs=(vmem, vmem),
        compiler_params=small,
        name="stream",
    )(mixed, residual_stream)
    stream = lax.all_to_all(stream, (*near_axes, "tp"), 0, 0, tiled=True)
    stream, up_3 = beside(stream, trade(up_weight, 3))

    half = -(-(units + 3) // 128) * 128
    block = tokens // n_far
    sums = pl.pallas_call(
        project_kernel,
        out_shape=jax.ShapeDtypeStruct((n_far, block, 2 * half), BF16),
        in_specs=[vmem] * 9,
        out_specs=vmem,
        compiler_params=small,
        name="project",
    )(stream, chunk(gate_weight, near), gate_1, gate_2, gate_3, chunk(up_weight, near), up_1, up_2, up_3)
    sums, down_y = beside(lax.all_to_all(sums, "far", 0, 0, tiled=True), down_trade)
    hidden = pl.pallas_call(
        hidden_kernel,
        out_shape=jax.ShapeDtypeStruct((n_far, block, units), BF16),
        in_specs=[vmem],
        out_specs=vmem,
        compiler_params=small,
        name="hidden",
    )(sums)
    hidden = lax.all_to_all(hidden, "far", 0, 0, tiled=True).reshape(tokens, units)
    other = lax.ppermute(hidden, "lo", [(0, 1), (1, 0)])
    lowered = pl.pallas_call(
        down_kernel,
        out_shape=jax.ShapeDtypeStruct((2 * n_tp, trows, feats), BF16),
        in_specs=[vmem] * 4,
        out_specs=vmem,
        compiler_params=small,
        name="down",
    )(hidden, other, down_chunk(near), down_y)
    lowered = lax.all_to_all(lowered, ("hi", "tp"), 0, 0, tiled=True)
    layer_out = pl.pallas_call(
        last_kernel,
        out_shape=jax.ShapeDtypeStruct((trows, feats), BF16),
        in_specs=[vmem] * 2,
        out_specs=vmem,
        compiler_params=small,
        name="last",
    )(lowered, own)
    return (attention, layer_out)


def solution(mesh):
    fine = jax.sharding.Mesh(mesh.devices.reshape(-1, 2, 2, mesh.shape["tp"]), ("far", "lo", "hi", "tp"))
    ctx = ("far", "lo", "hi")
    return jax.shard_map(
        per_device,
        mesh=fine,
        in_specs=(
            P(ctx, "tp"),
            P("tp", ctx, None),
            P("tp", ctx, None),
            P(ctx, "tp"),
            P(ctx, "tp"),
            P(ctx),
            P("tp", ctx),
            P("tp", ctx),
            P(ctx),
            P(ctx, "tp"),
            P(ctx, "tp"),
            P("tp", ctx),
        ),
        out_specs=(P(ctx, "tp"), P("tp", ctx)),
        check_vma=False,
    )
```

```python
import functools
import math

import jax
import jax.numpy as jnp
from jax import lax
from jax.experimental import pallas as pl
from jax.experimental.pallas import tpu as pltpu
from jax.sharding import PartitionSpec as P

D = 8192
F32 = jnp.float32
BF16 = jnp.bfloat16
LOW = -1e30
SPAN = 512


def three_parts(x):
    one = x.astype(BF16).astype(F32)
    rest = x - one
    two = rest.astype(BF16).astype(F32)
    return one, two, (rest - two).astype(BF16).astype(F32)


def attend_kernel(
    lengths, q_ref, k_hbm, v_hbm, sk_hbm, sv_hbm, out_ref, k_ref, v_ref, sk_ref, sv_ref, sems,
    *, tokens, group, head, scale
):
    k_copy = pltpu.make_async_copy(k_hbm, k_ref, sems.at[0])
    v_copy = pltpu.make_async_copy(v_hbm, v_ref, sems.at[1])
    sk_copy = pltpu.make_async_copy(sk_hbm, sk_ref, sems.at[2])
    sv_copy = pltpu.make_async_copy(sv_hbm, sv_ref, sems.at[3])
    sk_copy.start()
    sv_copy.start()
    k_copy.start()
    v_copy.start()
    length = lengths[0]
    rows = tokens * group
    own = sk_ref.shape[0]
    first = lax.axis_index(("far", "lo", "hi")) * own
    query = q_ref[...].reshape(rows, head)
    unit = scale / math.log(2.0)

    def scores(keys):
        return lax.dot_general(keys, query, (((1,), (1,)), ((), ())), preferred_element_type=F32)

    def weigh(values, w):
        return lax.dot_general(values, w.astype(BF16), (((0,), (0,)), ((), ())), preferred_element_type=F32)

    def add(carry, s, values):
        top, total, numer = carry
        top_new = jnp.maximum(top, jnp.max(s, axis=0, keepdims=True))
        fade = jnp.exp2((top - top_new) * unit)
        w = jnp.exp2((s - top_new) * unit)
        return top_new, total * fade + jnp.sum(w, axis=0, keepdims=True), numer * fade + weigh(values, w)

    sk_copy.wait()
    sv_copy.wait()
    s = scores(sk_ref[...])
    token = lax.broadcasted_iota(jnp.int32, (own, rows), 1) // group
    place = first + lax.broadcasted_iota(jnp.int32, (own, rows), 0)
    seen = place <= token
    s = jnp.where(seen, s, LOW)
    top = jnp.max(s, axis=0, keepdims=True)
    w = jnp.where(seen, jnp.exp2((s - top) * unit), 0.0)
    total = jnp.sum(w, axis=0, keepdims=True)
    numer = weigh(sv_ref[...], w)
    k_copy.wait()
    v_copy.wait()

    def whole(step, carry):
        at = pl.ds(pl.multiple_of(step * SPAN, SPAN), SPAN)
        return add(carry, scores(k_ref[at, :]), v_ref[at, :])

    full = length // SPAN
    carry = lax.fori_loop(0, full, whole, (top, total, numer))

    def part(step, carry):
        at = pl.ds(pl.multiple_of(step * SPAN, SPAN), SPAN)
        s = scores(k_ref[at, :])
        live = step * SPAN + lax.broadcasted_iota(jnp.int32, s.shape, 0) < length
        return add(carry, jnp.where(live, s, LOW), v_ref[at, :])

    top, total, numer = lax.fori_loop(full, (length + SPAN - 1) // SPAN, part, carry)
    blocks = out_ref.shape[0]
    each = rows // blocks
    out_ref[:, :each, :] = (numer / total).T.astype(BF16).reshape(blocks, each, head)
    stats = jnp.concatenate([*three_parts(top * unit), *three_parts(total), jnp.zeros((2, rows), F32)], axis=0)
    stats = jnp.concatenate([stats, jnp.zeros((8, rows), F32)], axis=0)
    spare = jnp.zeros((out_ref.shape[1] - each, head - each), F32)
    for i in range(blocks):
        tail = stats[: out_ref.shape[1] - each, i * each : (i + 1) * each]
        out_ref[i, each:, :] = jnp.concatenate([tail, spare], axis=1).astype(BF16)


def merge_kernel(in_ref, out_ref, copies_ref):
    blocks, rows, head = copies_ref.shape
    stat = [in_ref[:, rows + i, :].astype(F32) for i in range(6)]
    top = stat[0] + stat[1] + stat[2]
    total = stat[3] + stat[4] + stat[5]
    w = jnp.exp2(top - jnp.max(top, axis=0, keepdims=True)) * total
    w = (w / jnp.sum(w, axis=0, keepdims=True)).T
    out = jnp.zeros((rows, head), F32)
    for i in range(blocks):
        out = out + in_ref[i, :rows, :].astype(F32) * w[:rows, i : i + 1]
    out = out.astype(BF16)
    out_ref[...] = out
    for i in range(blocks):
        copies_ref[i] = out


def out_kernel(h_ref, w_ref, out_ref, wide_ref):
    blocks, rows, _ = out_ref.shape
    tokens = blocks * rows
    head = h_ref.shape[2]
    group = w_ref.shape[0] // head
    wide_ref[...] = h_ref[...].astype(F32).reshape(tokens * group, head)
    y = 0.0
    for g in range(group):
        x = wide_ref[pl.ds(g, tokens, stride=group), :].astype(BF16)
        y = y + jnp.dot(x, w_ref[g * head : (g + 1) * head, :], preferred_element_type=F32)
    for i in range(blocks):
        out_ref[i] = y[i * rows : (i + 1) * rows].astype(BF16)


def stream_kernel(in_ref, residual_ref, own_ref, copies_ref):
    own = jnp.sum(in_ref[...].astype(F32), axis=0) + residual_ref[...].astype(F32)
    own = own.astype(BF16)
    own_ref[...] = own
    for i in range(copies_ref.shape[0]):
        copies_ref[i] = own


def last_kernel(in_ref, own_ref, out_ref):
    out_ref[...] = (own_ref[...].astype(F32) + jnp.sum(in_ref[...].astype(F32), axis=0)).astype(BF16)


def project_kernel(x_ref, gate_ref, gate_y_ref, up_ref, up_y_ref, send_ref, keep_ref):
    units = gate_ref.shape[1]
    each = x_ref.shape[0] // 2
    half = keep_ref.shape[1] // 2
    lo, hi = lax.axis_index("lo"), lax.axis_index("hi")
    own, other = (
        jnp.concatenate([x_ref[at * each + i].astype(F32) for i in range(each)], axis=0) for at in (hi, 1 - hi)
    )
    squares = jnp.sum(own * own, axis=1, keepdims=True) + jnp.sum(other * other, axis=1, keepdims=True)
    parts = three_parts(squares)
    own, other = own.astype(BF16), other.astype(BF16)

    def product(w_ref, w_y_ref, at):
        y = lax.dot_general(own, w_ref[at], (((1,), (1,)), ((), ())), preferred_element_type=F32)
        return y + lax.dot_general(other, w_y_ref[at], (((1,), (1,)), ((), ())), preferred_element_type=F32)

    tokens = squares.shape[0]
    spare = half - units
    for at, ref in ((1 - lo, send_ref), (lo, keep_ref)):
        gate = product(gate_ref, gate_y_ref, at)
        up = product(up_ref, up_y_ref, at)
        ref[:, :half] = jnp.concatenate([gate, *parts, jnp.zeros((tokens, spare - 3), F32)], axis=1).astype(ref.dtype)
        ref[:, half:] = jnp.concatenate([up, jnp.zeros((tokens, spare), F32)], axis=1).astype(ref.dtype)


def join_kernel(keep_ref, got_ref, out_ref, *, units):
    total = keep_ref[...] + got_ref[...].astype(F32)
    cut = units // 128 * 128
    at = units - cut
    tail = total[:, cut : cut + 128]
    one, two, three = three_parts(jnp.sum(tail[:, at : at + 3], axis=1, keepdims=True))
    column = lax.broadcasted_iota(jnp.int32, tail.shape, 1) - at
    tail = jnp.where(column == 0, one, jnp.where(column == 1, two, jnp.where(column == 2, three, tail)))
    blocks, rows, _ = out_ref.shape
    for i in range(blocks):
        mine = slice(i * rows, (i + 1) * rows)
        out_ref[i] = total[mine].astype(BF16)
        out_ref[i, :, cut : cut + 128] = tail[mine].astype(BF16)


def hidden_kernel(in_ref, out_ref):
    blocks, _, units = out_ref.shape
    half = in_ref.shape[2] // 2
    sums = jnp.sum(in_ref[...].astype(F32), axis=0)
    power = jnp.sum(sums[:, units : units + 3], axis=1, keepdims=True) / D
    inv = lax.rsqrt(power + 1e-06)
    gate, upper = sums[:, :units] * inv, sums[:, half : half + units] * inv
    out = (gate / (1.0 + jnp.exp(-gate)) * upper).astype(BF16)
    for i in range(blocks):
        out_ref[i] = out


def down_kernel(mine_ref, other_ref, w_ref, wy_ref, out_ref):
    rows = out_ref.shape[1]
    each = out_ref.shape[0] // 2
    lo, hi = lax.axis_index("lo"), lax.axis_index("hi")
    for at, ref in ((hi, w_ref), (1 - hi, wy_ref)):
        y = jnp.dot(mine_ref[...], ref[lo], preferred_element_type=F32)
        y = y + jnp.dot(other_ref[...], ref[1 - lo], preferred_element_type=F32)
        for k in range(each):
            out_ref[at * each + k] = y[k * rows : (k + 1) * rows].astype(BF16)


def per_device(
    queries,
    cache_keys,
    cache_values,
    seg_keys,
    seg_values,
    lengths,
    residual_stream,
    out_weight,
    norm_gain,
    gate_weight,
    up_weight,
    down_weight,
):
    rows, width = queries.shape
    _, stretch, head = cache_keys.shape
    group = width // head
    near_axes = ("lo", "hi")
    n_far, n_near, n_tp = lax.axis_size("far"), lax.axis_size(near_axes), lax.axis_size("tp")
    n_ctx = n_far * n_near
    ctx = ("far", *near_axes)
    tokens = rows * n_ctx
    trows = residual_stream.shape[0]
    feats = residual_stream.shape[1]
    units = gate_weight.shape[1] // n_near

    near = lax.axis_index(near_axes)

    def chunk(w, place):
        lows = [lax.dynamic_slice_in_dim(w, (2 * lo + (place & 1)) * units, units, 0) for lo in range(2)]
        return jnp.stack(lows)

    def scaled(w):
        return lambda place: (chunk(w.T, place).astype(F32) * norm_gain).astype(BF16)

    gate_chunk, up_chunk = scaled(gate_weight), scaled(up_weight)

    def down_chunk(place):
        return chunk(down_weight, place)

    def trade(part):
        return lambda place: lax.ppermute(part(place ^ 1), "hi", [(0, 1), (1, 0)])

    place = near

    def beside(x, *trades):
        nonlocal place
        x, place, *sent = lax.optimization_barrier((x, place, *[t(place) for t in trades]))
        return x, *sent

    each = rows * group
    q_all = jnp.broadcast_to(queries.reshape(1, each, head), (n_ctx, each, head))
    q_all = lax.all_to_all(q_all, ctx, 0, 0, tiled=True)
    q_all, gate_y = beside(q_all, trade(gate_chunk))
    vmem = pl.BlockSpec(memory_space=pltpu.VMEM)
    smem = pl.BlockSpec(memory_space=pltpu.SMEM)
    anywhere = pl.BlockSpec(memory_space=pl.ANY)
    params = pltpu.CompilerParams(vmem_limit_bytes=60 * 2**20)
    small = pltpu.CompilerParams(vmem_limit_bytes=24 * 2**20)
    partial = pl.pallas_call(
        functools.partial(attend_kernel, tokens=tokens, group=group, head=head, scale=1.0 / math.sqrt(head)),
        out_shape=jax.ShapeDtypeStruct((n_ctx, each + 8, head), BF16),
        in_specs=[smem, vmem] + [anywhere] * 4,
        out_specs=vmem,
        scratch_shapes=[
            pltpu.VMEM((stretch, head), BF16),
            pltpu.VMEM((stretch, head), BF16),
            pltpu.VMEM(seg_keys.shape, BF16),
            pltpu.VMEM(seg_values.shape, BF16),
            pltpu.SemaphoreType.DMA((4,)),
        ],
        compiler_params=params,
        cost_estimate=pl.CostEstimate(
            flops=4 * tokens * width * stretch, bytes_accessed=2**21, transcendentals=tokens * group * stretch
        ),
        name="attend",
    )(lengths, q_all, cache_keys[0], cache_values[0], seg_keys, seg_values)
    parts = lax.all_to_all(partial, ctx, 0, 0, tiled=True)
    parts, up_y = beside(parts, trade(up_chunk))
    attention, copies = pl.pallas_call(
        merge_kernel,
        out_shape=(jax.ShapeDtypeStruct((each, head), BF16), jax.ShapeDtypeStruct((n_ctx, each, head), BF16)),
        in_specs=[vmem],
        out_specs=(vmem, vmem),
        compiler_params=small,
        name="merge",
    )(parts)
    attention = attention.reshape(rows, width)
    heads_all = lax.all_to_all(copies, ctx, 0, 0, tiled=True)
    heads_all, down_y = beside(heads_all, trade(down_chunk))
    mixed = pl.pallas_call(
        out_kernel,
        out_shape=jax.ShapeDtypeStruct((n_tp, trows, feats), BF16),
        in_specs=[vmem] * 2,
        out_specs=vmem,
        scratch_shapes=[pltpu.VMEM((tokens * group, head), F32)],
        compiler_params=small,
        name="out",
    )(heads_all, out_weight)
    mixed = lax.all_to_all(mixed, "tp", 0, 0, tiled=True)
    own, stream = pl.pallas_call(
        stream_kernel,
        out_shape=(
            jax.ShapeDtypeStruct((trows, feats), BF16),
            jax.ShapeDtypeStruct((2 * n_tp, trows, feats), BF16),
        ),
        in_specs=[vmem] * 2,
        out_specs=(vmem, vmem),
        compiler_params=small,
        name="stream",
    )(mixed, residual_stream)
    stream = lax.all_to_all(stream, ("hi", "tp"), 0, 0, tiled=True)

    half = -(-(units + 3) // 128) * 128
    block = tokens // n_far
    send, keep = pl.pallas_call(
        project_kernel,
        out_shape=(
            jax.ShapeDtypeStruct((tokens, 2 * half), BF16),
            jax.ShapeDtypeStruct((tokens, 2 * half), F32),
        ),
        in_specs=[vmem] * 5,
        out_specs=(vmem, vmem),
        compiler_params=small,
        name="project",
    )(stream, gate_chunk(near), gate_y, up_chunk(near), up_y)
    got = lax.ppermute(send, "lo", [(0, 1), (1, 0)])
    sums = pl.pallas_call(
        functools.partial(join_kernel, units=units),
        out_shape=jax.ShapeDtypeStruct((n_far, block, 2 * half), BF16),
        in_specs=[vmem] * 2,
        out_specs=vmem,
        compiler_params=small,
        name="join",
    )(keep, got)
    sums = lax.all_to_all(sums, "far", 0, 0, tiled=True)
    hidden = pl.pallas_call(
        hidden_kernel,
        out_shape=jax.ShapeDtypeStruct((n_far, block, units), BF16),
        in_specs=[vmem],
        out_specs=vmem,
        compiler_params=small,
        name="hidden",
    )(sums)
    hidden = lax.all_to_all(hidden, "far", 0, 0, tiled=True).reshape(tokens, units)
    other = lax.ppermute(hidden, "lo", [(0, 1), (1, 0)])
    lowered = pl.pallas_call(
        down_kernel,
        out_shape=jax.ShapeDtypeStruct((2 * n_tp, trows, feats), BF16),
        in_specs=[vmem] * 4,
        out_specs=vmem,
        compiler_params=small,
        name="down",
    )(hidden, other, down_chunk(near), down_y)
    lowered = lax.all_to_all(lowered, ("hi", "tp"), 0, 0, tiled=True)
    layer_out = pl.pallas_call(
        last_kernel,
        out_shape=jax.ShapeDtypeStruct((trows, feats), BF16),
        in_specs=[vmem] * 2,
        out_specs=vmem,
        compiler_params=small,
        name="last",
    )(lowered, own)
    return (attention, layer_out)


def solution(mesh):
    fine = jax.sharding.Mesh(mesh.devices.reshape(-1, 2, 2, mesh.shape["tp"]), ("far", "lo", "hi", "tp"))
    ctx = ("far", "lo", "hi")
    return jax.shard_map(
        per_device,
        mesh=fine,
        in_specs=(
            P(ctx, "tp"),
            P("tp", ctx, None),
            P("tp", ctx, None),
            P(ctx, "tp"),
            P(ctx, "tp"),
            P(ctx),
            P("tp", ctx),
            P("tp", ctx),
            P(ctx),
            P(ctx, "tp"),
            P(ctx, "tp"),
            P("tp", ctx),
        ),
        out_specs=(P(ctx, "tp"), P("tp", ctx)),
        check_vma=False,
    )
```

```python
import functools
import math

import jax
import jax.numpy as jnp
from jax import lax
from jax.experimental import pallas as pl
from jax.experimental.pallas import tpu as pltpu
from jax.sharding import PartitionSpec as P

D = 8192
F32 = jnp.float32
BF16 = jnp.bfloat16
LOW = -1e30
SPAN = 512


def three_parts(x):
    one = x.astype(BF16).astype(F32)
    rest = x - one
    two = rest.astype(BF16).astype(F32)
    return one, two, (rest - two).astype(BF16).astype(F32)


def attend_kernel(
    lengths, q_ref, k_hbm, v_hbm, sk_hbm, sv_hbm, out_ref, k_ref, v_ref, sk_ref, sv_ref, sems,
    *, tokens, group, head, scale
):
    k_copy = pltpu.make_async_copy(k_hbm, k_ref, sems.at[0])
    v_copy = pltpu.make_async_copy(v_hbm, v_ref, sems.at[1])
    sk_copy = pltpu.make_async_copy(sk_hbm, sk_ref, sems.at[2])
    sv_copy = pltpu.make_async_copy(sv_hbm, sv_ref, sems.at[3])
    sk_copy.start()
    sv_copy.start()
    k_copy.start()
    v_copy.start()
    length = lengths[0]
    rows = tokens * group
    own = sk_ref.shape[0]
    first = lax.axis_index(("far", "lo", "hi")) * own
    query = q_ref[...].reshape(rows, head)
    unit = scale / math.log(2.0)

    def scores(keys):
        return lax.dot_general(keys, query, (((1,), (1,)), ((), ())), preferred_element_type=F32)

    def weigh(values, w):
        return lax.dot_general(values, w.astype(BF16), (((0,), (0,)), ((), ())), preferred_element_type=F32)

    def add(carry, s, values):
        top, total, numer = carry
        top_new = jnp.maximum(top, jnp.max(s, axis=0, keepdims=True))
        fade = jnp.exp2((top - top_new) * unit)
        w = jnp.exp2((s - top_new) * unit)
        return top_new, total * fade + jnp.sum(w, axis=0, keepdims=True), numer * fade + weigh(values, w)

    sk_copy.wait()
    sv_copy.wait()
    s = scores(sk_ref[...])
    token = lax.broadcasted_iota(jnp.int32, (own, rows), 1) // group
    place = first + lax.broadcasted_iota(jnp.int32, (own, rows), 0)
    seen = place <= token
    s = jnp.where(seen, s, LOW)
    top = jnp.max(s, axis=0, keepdims=True)
    w = jnp.where(seen, jnp.exp2((s - top) * unit), 0.0)
    total = jnp.sum(w, axis=0, keepdims=True)
    numer = weigh(sv_ref[...], w)
    k_copy.wait()
    v_copy.wait()

    def whole(step, carry):
        at = pl.ds(pl.multiple_of(step * SPAN, SPAN), SPAN)
        return add(carry, scores(k_ref[at, :]), v_ref[at, :])

    full = length // SPAN
    carry = lax.fori_loop(0, full, whole, (top, total, numer))

    def part(step, carry):
        at = pl.ds(pl.multiple_of(step * SPAN, SPAN), SPAN)
        s = scores(k_ref[at, :])
        live = step * SPAN + lax.broadcasted_iota(jnp.int32, s.shape, 0) < length
        return add(carry, jnp.where(live, s, LOW), v_ref[at, :])

    top, total, numer = lax.fori_loop(full, (length + SPAN - 1) // SPAN, part, carry)
    blocks = out_ref.shape[0]
    each = rows // blocks
    out_ref[:, :each, :] = (numer / total).T.astype(BF16).reshape(blocks, each, head)
    stats = jnp.concatenate([*three_parts(top * unit), *three_parts(total), jnp.zeros((2, rows), F32)], axis=0)
    stats = jnp.concatenate([stats, jnp.zeros((8, rows), F32)], axis=0)
    spare = jnp.zeros((out_ref.shape[1] - each, head - each), F32)
    for i in range(blocks):
        tail = stats[: out_ref.shape[1] - each, i * each : (i + 1) * each]
        out_ref[i, each:, :] = jnp.concatenate([tail, spare], axis=1).astype(BF16)


def merge_kernel(in_ref, out_ref, copies_ref):
    blocks, rows, head = copies_ref.shape
    stat = [in_ref[:, rows + i, :].astype(F32) for i in range(6)]
    top = stat[0] + stat[1] + stat[2]
    total = stat[3] + stat[4] + stat[5]
    w = jnp.exp2(top - jnp.max(top, axis=0, keepdims=True)) * total
    w = (w / jnp.sum(w, axis=0, keepdims=True)).T
    out = jnp.zeros((rows, head), F32)
    for i in range(blocks):
        out = out + in_ref[i, :rows, :].astype(F32) * w[:rows, i : i + 1]
    out = out.astype(BF16)
    out_ref[...] = out
    for i in range(blocks):
        copies_ref[i] = out


def out_kernel(h_ref, w_ref, out_ref, wide_ref):
    blocks, rows, _ = out_ref.shape
    tokens = blocks * rows
    head = h_ref.shape[2]
    group = w_ref.shape[0] // head
    wide_ref[...] = h_ref[...].astype(F32).reshape(tokens * group, head)
    y = 0.0
    for g in range(group):
        x = wide_ref[pl.ds(g, tokens, stride=group), :].astype(BF16)
        y = y + jnp.dot(x, w_ref[g * head : (g + 1) * head, :], preferred_element_type=F32)
    for i in range(blocks):
        out_ref[i] = y[i * rows : (i + 1) * rows].astype(BF16)


def stream_kernel(in_ref, residual_ref, own_ref, copies_ref):
    own = jnp.sum(in_ref[...].astype(F32), axis=0) + residual_ref[...].astype(F32)
    own = own.astype(BF16)
    own_ref[...] = own
    for i in range(copies_ref.shape[0]):
        copies_ref[i] = own


def last_kernel(in_ref, own_ref, out_ref):
    out_ref[...] = (own_ref[...].astype(F32) + jnp.sum(in_ref[...].astype(F32), axis=0)).astype(BF16)


def project_kernel(x_ref, gate_ref, gate_y_ref, up_ref, up_y0_ref, up_y1_ref, send_ref, keep_ref):
    units = gate_ref.shape[1]
    each = x_ref.shape[0] // 2
    half = keep_ref.shape[1] // 2
    lo, hi = lax.axis_index("lo"), lax.axis_index("hi")
    own, other = (
        jnp.concatenate([x_ref[at * each + i].astype(F32) for i in range(each)], axis=0) for at in (hi, 1 - hi)
    )
    squares = jnp.sum(own * own, axis=1, keepdims=True) + jnp.sum(other * other, axis=1, keepdims=True)
    parts = three_parts(squares)
    own, other = own.astype(BF16), other.astype(BF16)

    def product(w, w_y):
        y = lax.dot_general(own, w, (((1,), (1,)), ((), ())), preferred_element_type=F32)
        return y + lax.dot_general(other, w_y, (((1,), (1,)), ((), ())), preferred_element_type=F32)

    tokens = squares.shape[0]
    spare = half - units
    for at, ref in ((1 - lo, send_ref), (lo, keep_ref)):
        gate = product(gate_ref[at], gate_y_ref[at])
        up = product(up_ref[at], jnp.where(at == 0, up_y0_ref[...], up_y1_ref[...]))
        ref[:, :half] = jnp.concatenate([gate, *parts, jnp.zeros((tokens, spare - 3), F32)], axis=1).astype(ref.dtype)
        ref[:, half:] = jnp.concatenate([up, jnp.zeros((tokens, spare), F32)], axis=1).astype(ref.dtype)


def join_kernel(keep_ref, got_ref, out_ref, *, units):
    total = keep_ref[...] + got_ref[...].astype(F32)
    cut = units // 128 * 128
    at = units - cut
    tail = total[:, cut : cut + 128]
    one, two, three = three_parts(jnp.sum(tail[:, at : at + 3], axis=1, keepdims=True))
    column = lax.broadcasted_iota(jnp.int32, tail.shape, 1) - at
    tail = jnp.where(column == 0, one, jnp.where(column == 1, two, jnp.where(column == 2, three, tail)))
    blocks, rows, _ = out_ref.shape
    for i in range(blocks):
        mine = slice(i * rows, (i + 1) * rows)
        out_ref[i] = total[mine].astype(BF16)
        out_ref[i, :, cut : cut + 128] = tail[mine].astype(BF16)


def hidden_kernel(in_ref, out_ref):
    blocks, _, units = out_ref.shape
    half = in_ref.shape[2] // 2
    sums = jnp.sum(in_ref[...].astype(F32), axis=0)
    power = jnp.sum(sums[:, units : units + 3], axis=1, keepdims=True) / D
    inv = lax.rsqrt(power + 1e-06)
    gate, upper = sums[:, :units] * inv, sums[:, half : half + units] * inv
    out = (gate / (1.0 + jnp.exp(-gate)) * upper).astype(BF16)
    for i in range(blocks):
        out_ref[i] = out


def down_kernel(h_ref, w_ref, wy_ref, out_ref):
    rows = out_ref.shape[1]
    each = out_ref.shape[0] // 2
    hi = lax.axis_index("hi")
    h = [jnp.concatenate([h_ref[i] for i in range(lo, h_ref.shape[0], 2)], axis=0) for lo in range(2)]
    for at, ref in ((hi, w_ref), (1 - hi, wy_ref)):
        y = jnp.dot(h[0], ref[0], preferred_element_type=F32) + jnp.dot(h[1], ref[1], preferred_element_type=F32)
        for k in range(each):
            out_ref[at * each + k] = y[k * rows : (k + 1) * rows].astype(BF16)


def per_device(
    queries,
    cache_keys,
    cache_values,
    seg_keys,
    seg_values,
    lengths,
    residual_stream,
    out_weight,
    norm_gain,
    gate_weight,
    up_weight,
    down_weight,
):
    rows, width = queries.shape
    _, stretch, head = cache_keys.shape
    group = width // head
    near_axes = ("lo", "hi")
    n_far, n_near, n_tp = lax.axis_size("far"), lax.axis_size(near_axes), lax.axis_size("tp")
    n_ctx = n_far * n_near
    ctx = ("far", *near_axes)
    tokens = rows * n_ctx
    trows = residual_stream.shape[0]
    feats = residual_stream.shape[1]
    units = gate_weight.shape[1] // n_near

    near = lax.axis_index(near_axes)

    def piece(w, lo, place):
        return lax.dynamic_slice_in_dim(w, (2 * lo + (place & 1)) * units, units, 0)

    def scaled(w, lo, place):
        return (piece(w.T, lo, place).astype(F32) * norm_gain).astype(BF16)

    def gate_chunk(place):
        return jnp.stack([scaled(gate_weight, lo, place) for lo in range(2)])

    def up_0(place):
        return scaled(up_weight, 0, place)

    def up_1(place):
        return scaled(up_weight, 1, place)

    def down_chunk(place):
        return jnp.stack([piece(down_weight, lo, place) for lo in range(2)])

    def trade(part):
        return lambda place: lax.ppermute(part(place ^ 1), "hi", [(0, 1), (1, 0)])

    place = near

    def beside(x, *trades):
        nonlocal place
        x, place, *sent = lax.optimization_barrier((x, place, *[t(place) for t in trades]))
        return x, *sent

    each = rows * group
    q_all = jnp.broadcast_to(queries.reshape(1, each, head), (n_ctx, each, head))
    q_all = lax.all_to_all(q_all, ctx, 0, 0, tiled=True)
    q_all, gate_y = beside(q_all, trade(gate_chunk))
    vmem = pl.BlockSpec(memory_space=pltpu.VMEM)
    smem = pl.BlockSpec(memory_space=pltpu.SMEM)
    anywhere = pl.BlockSpec(memory_space=pl.ANY)
    params = pltpu.CompilerParams(vmem_limit_bytes=60 * 2**20)
    small = pltpu.CompilerParams(vmem_limit_bytes=24 * 2**20)
    partial = pl.pallas_call(
        functools.partial(attend_kernel, tokens=tokens, group=group, head=head, scale=1.0 / math.sqrt(head)),
        out_shape=jax.ShapeDtypeStruct((n_ctx, each + 8, head), BF16),
        in_specs=[smem, vmem] + [anywhere] * 4,
        out_specs=vmem,
        scratch_shapes=[
            pltpu.VMEM((stretch, head), BF16),
            pltpu.VMEM((stretch, head), BF16),
            pltpu.VMEM(seg_keys.shape, BF16),
            pltpu.VMEM(seg_values.shape, BF16),
            pltpu.SemaphoreType.DMA((4,)),
        ],
        compiler_params=params,
        cost_estimate=pl.CostEstimate(
            flops=4 * tokens * width * stretch, bytes_accessed=2**21, transcendentals=tokens * group * stretch
        ),
        name="attend",
    )(lengths, q_all, cache_keys[0], cache_values[0], seg_keys, seg_values)
    parts = lax.all_to_all(partial, ctx, 0, 0, tiled=True)
    parts, up_y0 = beside(parts, trade(up_0))
    attention, copies = pl.pallas_call(
        merge_kernel,
        out_shape=(jax.ShapeDtypeStruct((each, head), BF16), jax.ShapeDtypeStruct((n_ctx, each, head), BF16)),
        in_specs=[vmem],
        out_specs=(vmem, vmem),
        compiler_params=small,
        name="merge",
    )(parts)
    attention = attention.reshape(rows, width)
    heads_all = lax.all_to_all(copies, ctx, 0, 0, tiled=True)
    heads_all, up_y1 = beside(heads_all, trade(up_1))
    mixed = pl.pallas_call(
        out_kernel,
        out_shape=jax.ShapeDtypeStruct((n_tp, trows, feats), BF16),
        in_specs=[vmem] * 2,
        out_specs=vmem,
        scratch_shapes=[pltpu.VMEM((tokens * group, head), F32)],
        compiler_params=small,
        name="out",
    )(heads_all, out_weight)
    mixed = lax.all_to_all(mixed, "tp", 0, 0, tiled=True)
    own, stream = pl.pallas_call(
        stream_kernel,
        out_shape=(
            jax.ShapeDtypeStruct((trows, feats), BF16),
            jax.ShapeDtypeStruct((2 * n_tp, trows, feats), BF16),
        ),
        in_specs=[vmem] * 2,
        out_specs=(vmem, vmem),
        compiler_params=small,
        name="stream",
    )(mixed, residual_stream)
    stream = lax.all_to_all(stream, ("hi", "tp"), 0, 0, tiled=True)

    half = -(-(units + 3) // 128) * 128
    block = tokens // n_far
    send, keep = pl.pallas_call(
        project_kernel,
        out_shape=(
            jax.ShapeDtypeStruct((tokens, 2 * half), BF16),
            jax.ShapeDtypeStruct((tokens, 2 * half), F32),
        ),
        in_specs=[vmem] * 6,
        out_specs=(vmem, vmem),
        compiler_params=small,
        name="project",
    )(stream, gate_chunk(near), gate_y, jnp.stack([up_0(near), up_1(near)]), up_y0, up_y1)
    got = lax.ppermute(send, "lo", [(0, 1), (1, 0)])
    sums = pl.pallas_call(
        functools.partial(join_kernel, units=units),
        out_shape=jax.ShapeDtypeStruct((n_far, block, 2 * half), BF16),
        in_specs=[vmem] * 2,
        out_specs=vmem,
        compiler_params=small,
        name="join",
    )(keep, got)
    sums, down_y = beside(lax.all_to_all(sums, "far", 0, 0, tiled=True), trade(down_chunk))
    hidden = pl.pallas_call(
        hidden_kernel,
        out_shape=jax.ShapeDtypeStruct((2 * n_far, block, units), BF16),
        in_specs=[vmem],
        out_specs=vmem,
        compiler_params=small,
        name="hidden",
    )(sums)
    hidden = lax.all_to_all(hidden, ("far", "lo"), 0, 0, tiled=True)
    lowered = pl.pallas_call(
        down_kernel,
        out_shape=jax.ShapeDtypeStruct((2 * n_tp, trows, feats), BF16),
        in_specs=[vmem] * 3,
        out_specs=vmem,
        compiler_params=small,
        name="down",
    )(hidden, down_chunk(near), down_y)
    lowered = lax.all_to_all(lowered, ("hi", "tp"), 0, 0, tiled=True)
    layer_out = pl.pallas_call(
        last_kernel,
        out_shape=jax.ShapeDtypeStruct((trows, feats), BF16),
        in_specs=[vmem] * 2,
        out_specs=vmem,
        compiler_params=small,
        name="last",
    )(lowered, own)
    return (attention, layer_out)


def solution(mesh):
    fine = jax.sharding.Mesh(mesh.devices.reshape(-1, 2, 2, mesh.shape["tp"]), ("far", "lo", "hi", "tp"))
    ctx = ("far", "lo", "hi")
    return jax.shard_map(
        per_device,
        mesh=fine,
        in_specs=(
            P(ctx, "tp"),
            P("tp", ctx, None),
            P("tp", ctx, None),
            P(ctx, "tp"),
            P(ctx, "tp"),
            P(ctx),
            P("tp", ctx),
            P("tp", ctx),
            P(ctx),
            P(ctx, "tp"),
            P(ctx, "tp"),
            P("tp", ctx),
        ),
        out_specs=(P(ctx, "tp"), P("tp", ctx)),
        check_vma=False,
    )
```

```python
import functools
import math

import jax
import jax.numpy as jnp
from jax import lax
from jax.experimental import pallas as pl
from jax.experimental.pallas import tpu as pltpu
from jax.sharding import PartitionSpec as P

D = 8192
F32 = jnp.float32
BF16 = jnp.bfloat16
LOW = -1e30
SPAN = 512


def three_parts(x):
    one = x.astype(BF16).astype(F32)
    rest = x - one
    two = rest.astype(BF16).astype(F32)
    return one, two, (rest - two).astype(BF16).astype(F32)


def attend_kernel(lengths, q_ref, k_ref, v_ref, sk_ref, sv_ref, out_ref, *, tokens, group, head, scale):
    length = lengths[0]
    rows = tokens * group
    own = sk_ref.shape[0]
    first = lax.axis_index(("far", "lo", "hi")) * own
    query = q_ref[...].reshape(rows, head)
    unit = scale / math.log(2.0)

    def scores(keys):
        return lax.dot_general(keys, query, (((1,), (1,)), ((), ())), preferred_element_type=F32)

    def weigh(values, w):
        return lax.dot_general(values, w.astype(BF16), (((0,), (0,)), ((), ())), preferred_element_type=F32)

    def add(carry, s, values):
        top, total, numer = carry
        top_new = jnp.maximum(top, jnp.max(s, axis=0, keepdims=True))
        fade = jnp.exp2((top - top_new) * unit)
        w = jnp.exp2((s - top_new) * unit)
        return top_new, total * fade + jnp.sum(w, axis=0, keepdims=True), numer * fade + weigh(values, w)

    s = scores(sk_ref[...])
    token = lax.broadcasted_iota(jnp.int32, (own, rows), 1) // group
    place = first + lax.broadcasted_iota(jnp.int32, (own, rows), 0)
    seen = place <= token
    s = jnp.where(seen, s, LOW)
    top = jnp.max(s, axis=0, keepdims=True)
    w = jnp.where(seen, jnp.exp2((s - top) * unit), 0.0)
    total = jnp.sum(w, axis=0, keepdims=True)
    numer = weigh(sv_ref[...], w)
    def whole(step, carry):
        at = pl.ds(pl.multiple_of(step * SPAN, SPAN), SPAN)
        return add(carry, scores(k_ref[at, :]), v_ref[at, :])

    full = length // SPAN
    carry = lax.fori_loop(0, full, whole, (top, total, numer))

    def part(step, carry):
        at = pl.ds(pl.multiple_of(step * SPAN, SPAN), SPAN)
        s = scores(k_ref[at, :])
        live = step * SPAN + lax.broadcasted_iota(jnp.int32, s.shape, 0) < length
        return add(carry, jnp.where(live, s, LOW), v_ref[at, :])

    top, total, numer = lax.fori_loop(full, (length + SPAN - 1) // SPAN, part, carry)
    blocks = out_ref.shape[0]
    each = rows // blocks
    out_ref[:, :each, :] = (numer / total).T.astype(BF16).reshape(blocks, each, head)
    stats = jnp.concatenate([*three_parts(top * unit), *three_parts(total), jnp.zeros((2, rows), F32)], axis=0)
    stats = jnp.concatenate([stats, jnp.zeros((8, rows), F32)], axis=0)
    spare = jnp.zeros((out_ref.shape[1] - each, head - each), F32)
    for i in range(blocks):
        tail = stats[: out_ref.shape[1] - each, i * each : (i + 1) * each]
        out_ref[i, each:, :] = jnp.concatenate([tail, spare], axis=1).astype(BF16)


def merge_kernel(in_ref, out_ref, copies_ref):
    blocks, rows, head = copies_ref.shape
    stat = [in_ref[:, rows + i, :].astype(F32) for i in range(6)]
    top = stat[0] + stat[1] + stat[2]
    total = stat[3] + stat[4] + stat[5]
    w = jnp.exp2(top - jnp.max(top, axis=0, keepdims=True)) * total
    w = (w / jnp.sum(w, axis=0, keepdims=True)).T
    out = jnp.zeros((rows, head), F32)
    for i in range(blocks):
        out = out + in_ref[i, :rows, :].astype(F32) * w[:rows, i : i + 1]
    out = out.astype(BF16)
    out_ref[...] = out
    for i in range(blocks):
        copies_ref[i] = out


def out_kernel(h_ref, w_ref, out_ref, wide_ref):
    blocks, rows, _ = out_ref.shape
    tokens = blocks * rows
    head = h_ref.shape[2]
    group = w_ref.shape[0] // head
    wide_ref[...] = h_ref[...].astype(F32).reshape(tokens * group, head)
    y = 0.0
    for g in range(group):
        x = wide_ref[pl.ds(g, tokens, stride=group), :].astype(BF16)
        y = y + jnp.dot(x, w_ref[g * head : (g + 1) * head, :], preferred_element_type=F32)
    for i in range(blocks):
        out_ref[i] = y[i * rows : (i + 1) * rows].astype(BF16)


def stream_kernel(in_ref, residual_ref, own_ref, copies_ref):
    own = jnp.sum(in_ref[...].astype(F32), axis=0) + residual_ref[...].astype(F32)
    own = own.astype(BF16)
    own_ref[...] = own
    for i in range(copies_ref.shape[0]):
        copies_ref[i] = own


def last_kernel(in_ref, own_ref, out_ref):
    out_ref[...] = (own_ref[...].astype(F32) + jnp.sum(in_ref[...].astype(F32), axis=0)).astype(BF16)


def project_kernel(x_ref, gate_ref, gate_y_ref, up_ref, up_y0_ref, up_y1_ref, send_ref, keep_ref):
    units = gate_ref.shape[1]
    each = x_ref.shape[0] // 2
    half = keep_ref.shape[1] // 2
    lo, hi = lax.axis_index("lo"), lax.axis_index("hi")
    own, other = (
        jnp.concatenate([x_ref[at * each + i].astype(F32) for i in range(each)], axis=0) for at in (hi, 1 - hi)
    )
    squares = jnp.sum(own * own, axis=1, keepdims=True) + jnp.sum(other * other, axis=1, keepdims=True)
    parts = three_parts(squares)
    own, other = own.astype(BF16), other.astype(BF16)

    def product(w, w_y):
        y = lax.dot_general(own, w, (((1,), (1,)), ((), ())), preferred_element_type=F32)
        return y + lax.dot_general(other, w_y, (((1,), (1,)), ((), ())), preferred_element_type=F32)

    tokens = squares.shape[0]
    spare = half - units
    for at, ref in ((1 - lo, send_ref), (lo, keep_ref)):
        gate = product(gate_ref[at], gate_y_ref[at])
        up = product(up_ref[at], jnp.where(at == 0, up_y0_ref[...], up_y1_ref[...]))
        ref[:, :half] = jnp.concatenate([gate, *parts, jnp.zeros((tokens, spare - 3), F32)], axis=1).astype(ref.dtype)
        ref[:, half:] = jnp.concatenate([up, jnp.zeros((tokens, spare), F32)], axis=1).astype(ref.dtype)


def join_kernel(keep_ref, got_ref, out_ref, *, units):
    total = keep_ref[...] + got_ref[...].astype(F32)
    cut = units // 128 * 128
    at = units - cut
    tail = total[:, cut : cut + 128]
    one, two, three = three_parts(jnp.sum(tail[:, at : at + 3], axis=1, keepdims=True))
    column = lax.broadcasted_iota(jnp.int32, tail.shape, 1) - at
    tail = jnp.where(column == 0, one, jnp.where(column == 1, two, jnp.where(column == 2, three, tail)))
    blocks, rows, _ = out_ref.shape
    for i in range(blocks):
        mine = slice(i * rows, (i + 1) * rows)
        out_ref[i] = total[mine].astype(BF16)
        out_ref[i, :, cut : cut + 128] = tail[mine].astype(BF16)


def hidden_kernel(in_ref, out_ref):
    blocks, _, units = out_ref.shape
    half = in_ref.shape[2] // 2
    sums = jnp.sum(in_ref[...].astype(F32), axis=0)
    power = jnp.sum(sums[:, units : units + 3], axis=1, keepdims=True) / D
    inv = lax.rsqrt(power + 1e-06)
    gate, upper = sums[:, :units] * inv, sums[:, half : half + units] * inv
    out = (gate / (1.0 + jnp.exp(-gate)) * upper).astype(BF16)
    for i in range(blocks):
        out_ref[i] = out


def down_kernel(h_ref, w_ref, wy_ref, out_ref):
    rows = out_ref.shape[1]
    each = out_ref.shape[0] // 2
    hi = lax.axis_index("hi")
    h = [jnp.concatenate([h_ref[i] for i in range(lo, h_ref.shape[0], 2)], axis=0) for lo in range(2)]
    for at, ref in ((hi, w_ref), (1 - hi, wy_ref)):
        y = jnp.dot(h[0], ref[0], preferred_element_type=F32) + jnp.dot(h[1], ref[1], preferred_element_type=F32)
        for k in range(each):
            out_ref[at * each + k] = y[k * rows : (k + 1) * rows].astype(BF16)


def per_device(
    queries,
    cache_keys,
    cache_values,
    seg_keys,
    seg_values,
    lengths,
    residual_stream,
    out_weight,
    norm_gain,
    gate_weight,
    up_weight,
    down_weight,
):
    rows, width = queries.shape
    _, stretch, head = cache_keys.shape
    group = width // head
    near_axes = ("lo", "hi")
    n_far, n_near, n_tp = lax.axis_size("far"), lax.axis_size(near_axes), lax.axis_size("tp")
    n_ctx = n_far * n_near
    ctx = ("far", *near_axes)
    tokens = rows * n_ctx
    trows = residual_stream.shape[0]
    feats = residual_stream.shape[1]
    units = gate_weight.shape[1] // n_near

    near = lax.axis_index(near_axes)

    def piece(w, lo, place):
        return lax.dynamic_slice_in_dim(w, (2 * lo + (place & 1)) * units, units, 0)

    def scaled(w, lo, place):
        return (piece(w.T, lo, place).astype(F32) * norm_gain).astype(BF16)

    def gate_chunk(place):
        return jnp.stack([scaled(gate_weight, lo, place) for lo in range(2)])

    def up_0(place):
        return scaled(up_weight, 0, place)

    def up_1(place):
        return scaled(up_weight, 1, place)

    def down_chunk(place):
        return jnp.stack([piece(down_weight, lo, place) for lo in range(2)])

    def trade(part):
        return lambda place: lax.ppermute(part(place ^ 1), "hi", [(0, 1), (1, 0)])

    place = near

    def beside(x, *trades):
        nonlocal place
        x, place, *sent = lax.optimization_barrier((x, place, *[t(place) for t in trades]))
        return x, *sent

    each = rows * group
    q_all = jnp.broadcast_to(queries.reshape(1, each, head), (n_ctx, each, head))
    q_all = lax.all_to_all(q_all, ctx, 0, 0, tiled=True)
    q_all, gate_y = beside(q_all, trade(gate_chunk))
    vmem = pl.BlockSpec(memory_space=pltpu.VMEM)
    smem = pl.BlockSpec(memory_space=pltpu.SMEM)
    params = pltpu.CompilerParams(vmem_limit_bytes=40 * 2**20)
    small = pltpu.CompilerParams(vmem_limit_bytes=24 * 2**20)
    partial = pl.pallas_call(
        functools.partial(attend_kernel, tokens=tokens, group=group, head=head, scale=1.0 / math.sqrt(head)),
        out_shape=jax.ShapeDtypeStruct((n_ctx, each + 8, head), BF16),
        in_specs=[smem] + [vmem] * 5,
        out_specs=vmem,
        compiler_params=params,
        cost_estimate=pl.CostEstimate(
            flops=4 * tokens * width * stretch, bytes_accessed=2**21, transcendentals=tokens * group * stretch
        ),
        name="attend",
    )(lengths, q_all, cache_keys[0], cache_values[0], seg_keys, seg_values)
    parts = lax.all_to_all(partial, ctx, 0, 0, tiled=True)
    (parts,) = beside(parts)
    attention, copies = pl.pallas_call(
        merge_kernel,
        out_shape=(jax.ShapeDtypeStruct((each, head), BF16), jax.ShapeDtypeStruct((n_ctx, each, head), BF16)),
        in_specs=[vmem],
        out_specs=(vmem, vmem),
        compiler_params=small,
        name="merge",
    )(parts)
    attention = attention.reshape(rows, width)
    heads_all = lax.all_to_all(copies, ctx, 0, 0, tiled=True)
    heads_all, up_y0 = beside(heads_all, trade(up_0))
    mixed = pl.pallas_call(
        out_kernel,
        out_shape=jax.ShapeDtypeStruct((n_tp, trows, feats), BF16),
        in_specs=[vmem] * 2,
        out_specs=vmem,
        scratch_shapes=[pltpu.VMEM((tokens * group, head), F32)],
        compiler_params=small,
        name="out",
    )(heads_all, out_weight)
    mixed = lax.all_to_all(mixed, "tp", 0, 0, tiled=True)
    own, stream = pl.pallas_call(
        stream_kernel,
        out_shape=(
            jax.ShapeDtypeStruct((trows, feats), BF16),
            jax.ShapeDtypeStruct((2 * n_tp, trows, feats), BF16),
        ),
        in_specs=[vmem] * 2,
        out_specs=(vmem, vmem),
        compiler_params=small,
        name="stream",
    )(mixed, residual_stream)
    stream = lax.all_to_all(stream, ("hi", "tp"), 0, 0, tiled=True)
    stream, up_y1 = beside(stream, trade(up_1))

    half = -(-(units + 3) // 128) * 128
    block = tokens // n_far
    send, keep = pl.pallas_call(
        project_kernel,
        out_shape=(
            jax.ShapeDtypeStruct((tokens, 2 * half), BF16),
            jax.ShapeDtypeStruct((tokens, 2 * half), F32),
        ),
        in_specs=[vmem] * 6,
        out_specs=(vmem, vmem),
        compiler_params=small,
        name="project",
    )(stream, gate_chunk(near), gate_y, jnp.stack([up_0(near), up_1(near)]), up_y0, up_y1)
    got = lax.ppermute(send, "lo", [(0, 1), (1, 0)])
    sums = pl.pallas_call(
        functools.partial(join_kernel, units=units),
        out_shape=jax.ShapeDtypeStruct((n_far, block, 2 * half), BF16),
        in_specs=[vmem] * 2,
        out_specs=vmem,
        compiler_params=small,
        name="join",
    )(keep, got)
    sums, down_y = beside(lax.all_to_all(sums, "far", 0, 0, tiled=True), trade(down_chunk))
    hidden = pl.pallas_call(
        hidden_kernel,
        out_shape=jax.ShapeDtypeStruct((2 * n_far, block, units), BF16),
        in_specs=[vmem],
        out_specs=vmem,
        compiler_params=small,
        name="hidden",
    )(sums)
    hidden = lax.all_to_all(hidden, ("far", "lo"), 0, 0, tiled=True)
    lowered = pl.pallas_call(
        down_kernel,
        out_shape=jax.ShapeDtypeStruct((2 * n_tp, trows, feats), BF16),
        in_specs=[vmem] * 3,
        out_specs=vmem,
        compiler_params=small,
        name="down",
    )(hidden, down_chunk(near), down_y)
    lowered = lax.all_to_all(lowered, ("hi", "tp"), 0, 0, tiled=True)
    layer_out = pl.pallas_call(
        last_kernel,
        out_shape=jax.ShapeDtypeStruct((trows, feats), BF16),
        in_specs=[vmem] * 2,
        out_specs=vmem,
        compiler_params=small,
        name="last",
    )(lowered, own)
    return (attention, layer_out)


def solution(mesh):
    fine = jax.sharding.Mesh(mesh.devices.reshape(-1, 2, 2, mesh.shape["tp"]), ("far", "lo", "hi", "tp"))
    ctx = ("far", "lo", "hi")
    return jax.shard_map(
        per_device,
        mesh=fine,
        in_specs=(
            P(ctx, "tp"),
            P("tp", ctx, None),
            P("tp", ctx, None),
            P(ctx, "tp"),
            P(ctx, "tp"),
            P(ctx),
            P("tp", ctx),
            P("tp", ctx),
            P(ctx),
            P(ctx, "tp"),
            P(ctx, "tp"),
            P("tp", ctx),
        ),
        out_specs=(P(ctx, "tp"), P("tp", ctx)),
        check_vma=False,
    )
```

```python
import functools
import math

import jax
import jax.numpy as jnp
from jax import lax
from jax.experimental import pallas as pl
from jax.experimental.pallas import tpu as pltpu
from jax.sharding import PartitionSpec as P

D = 8192
F32 = jnp.float32
BF16 = jnp.bfloat16
LOW = -1e30
SPAN = 512


def three_parts(x):
    one = x.astype(BF16).astype(F32)
    rest = x - one
    two = rest.astype(BF16).astype(F32)
    return one, two, (rest - two).astype(BF16).astype(F32)


def attend_kernel(lengths, q_ref, k_ref, v_ref, sk_ref, sv_ref, out_ref, *, tokens, group, head, scale):
    length = lengths[0]
    rows = tokens * group
    own = sk_ref.shape[0]
    first = lax.axis_index(("far", "lo", "hi")) * own
    query = q_ref[...].reshape(rows, head)
    unit = scale / math.log(2.0)

    def scores(keys):
        return lax.dot_general(keys, query, (((1,), (1,)), ((), ())), preferred_element_type=F32)

    def weigh(values, w):
        return lax.dot_general(values, w.astype(BF16), (((0,), (0,)), ((), ())), preferred_element_type=F32)

    def add(carry, s, values):
        top, total, numer = carry
        top_new = jnp.maximum(top, jnp.max(s, axis=0, keepdims=True))
        fade = jnp.exp2((top - top_new) * unit)
        w = jnp.exp2((s - top_new) * unit)
        return top_new, total * fade + jnp.sum(w, axis=0, keepdims=True), numer * fade + weigh(values, w)

    s = scores(sk_ref[...])
    token = lax.broadcasted_iota(jnp.int32, (own, rows), 1) // group
    place = first + lax.broadcasted_iota(jnp.int32, (own, rows), 0)
    seen = place <= token
    s = jnp.where(seen, s, LOW)
    top = jnp.max(s, axis=0, keepdims=True)
    w = jnp.where(seen, jnp.exp2((s - top) * unit), 0.0)
    total = jnp.sum(w, axis=0, keepdims=True)
    numer = weigh(sv_ref[...], w)
    def whole(step, carry):
        at = pl.ds(pl.multiple_of(step * SPAN, SPAN), SPAN)
        return add(carry, scores(k_ref[at, :]), v_ref[at, :])

    full = length // SPAN
    carry = lax.fori_loop(0, full, whole, (top, total, numer))

    def part(step, carry):
        at = pl.ds(pl.multiple_of(step * SPAN, SPAN), SPAN)
        s = scores(k_ref[at, :])
        live = step * SPAN + lax.broadcasted_iota(jnp.int32, s.shape, 0) < length
        return add(carry, jnp.where(live, s, LOW), v_ref[at, :])

    top, total, numer = lax.fori_loop(full, (length + SPAN - 1) // SPAN, part, carry)
    blocks = out_ref.shape[0]
    each = rows // blocks
    out_ref[:, :each, :] = (numer / total).T.astype(BF16).reshape(blocks, each, head)
    stats = jnp.concatenate([*three_parts(top * unit), *three_parts(total), jnp.zeros((2, rows), F32)], axis=0)
    stats = jnp.concatenate([stats, jnp.zeros((8, rows), F32)], axis=0)
    spare = jnp.zeros((out_ref.shape[1] - each, head - each), F32)
    for i in range(blocks):
        tail = stats[: out_ref.shape[1] - each, i * each : (i + 1) * each]
        out_ref[i, each:, :] = jnp.concatenate([tail, spare], axis=1).astype(BF16)


def merge_kernel(in_ref, out_ref, copies_ref):
    blocks, rows, head = copies_ref.shape
    stat = [in_ref[:, rows + i, :].astype(F32) for i in range(6)]
    top = stat[0] + stat[1] + stat[2]
    total = stat[3] + stat[4] + stat[5]
    w = jnp.exp2(top - jnp.max(top, axis=0, keepdims=True)) * total
    w = (w / jnp.sum(w, axis=0, keepdims=True)).T
    out = jnp.zeros((rows, head), F32)
    for i in range(blocks):
        out = out + in_ref[i, :rows, :].astype(F32) * w[:rows, i : i + 1]
    out = out.astype(BF16)
    out_ref[...] = out
    for i in range(blocks):
        copies_ref[i] = out


def out_kernel(h_ref, w_ref, out_ref, wide_ref):
    blocks, rows, _ = out_ref.shape
    tokens = blocks * rows
    head = h_ref.shape[2]
    group = w_ref.shape[0] // head
    wide_ref[...] = h_ref[...].astype(F32).reshape(tokens * group, head)
    y = 0.0
    for g in range(group):
        x = wide_ref[pl.ds(g, tokens, stride=group), :].astype(BF16)
        y = y + jnp.dot(x, w_ref[g * head : (g + 1) * head, :], preferred_element_type=F32)
    for i in range(blocks):
        out_ref[i] = y[i * rows : (i + 1) * rows].astype(BF16)


def stream_kernel(in_ref, residual_ref, own_ref, copies_ref):
    own = jnp.sum(in_ref[...].astype(F32), axis=0) + residual_ref[...].astype(F32)
    own = own.astype(BF16)
    own_ref[...] = own
    for i in range(copies_ref.shape[0]):
        copies_ref[i] = own


def last_kernel(in_ref, own_ref, out_ref):
    out_ref[...] = (own_ref[...].astype(F32) + jnp.sum(in_ref[...].astype(F32), axis=0)).astype(BF16)


def project_kernel(
    x_ref, gate_ref, gate_y0_ref, gate_y1_ref, up_ref, up_y0_ref, up_y1_ref, send_ref, keep_ref
):
    units = gate_ref.shape[1]
    each = x_ref.shape[0] // 2
    half = keep_ref.shape[1] // 2
    lo, hi = lax.axis_index("lo"), lax.axis_index("hi")
    own, other = (
        jnp.concatenate([x_ref[at * each + i].astype(F32) for i in range(each)], axis=0) for at in (hi, 1 - hi)
    )
    squares = jnp.sum(own * own, axis=1, keepdims=True) + jnp.sum(other * other, axis=1, keepdims=True)
    parts = three_parts(squares)
    own, other = own.astype(BF16), other.astype(BF16)

    def product(w, w_y):
        y = lax.dot_general(own, w, (((1,), (1,)), ((), ())), preferred_element_type=F32)
        return y + lax.dot_general(other, w_y, (((1,), (1,)), ((), ())), preferred_element_type=F32)

    tokens = squares.shape[0]
    spare = half - units
    for at, ref in ((1 - lo, send_ref), (lo, keep_ref)):
        gate = product(gate_ref[at], jnp.where(at == 0, gate_y0_ref[...], gate_y1_ref[...]))
        up = product(up_ref[at], jnp.where(at == 0, up_y0_ref[...], up_y1_ref[...]))
        ref[:, :half] = jnp.concatenate([gate, *parts, jnp.zeros((tokens, spare - 3), F32)], axis=1).astype(ref.dtype)
        ref[:, half:] = jnp.concatenate([up, jnp.zeros((tokens, spare), F32)], axis=1).astype(ref.dtype)


def join_kernel(keep_ref, got_ref, out_ref, *, units):
    total = keep_ref[...] + got_ref[...].astype(F32)
    cut = units // 128 * 128
    at = units - cut
    tail = total[:, cut : cut + 128]
    one, two, three = three_parts(jnp.sum(tail[:, at : at + 3], axis=1, keepdims=True))
    column = lax.broadcasted_iota(jnp.int32, tail.shape, 1) - at
    tail = jnp.where(column == 0, one, jnp.where(column == 1, two, jnp.where(column == 2, three, tail)))
    blocks, rows, _ = out_ref.shape
    for i in range(blocks):
        mine = slice(i * rows, (i + 1) * rows)
        out_ref[i] = total[mine].astype(BF16)
        out_ref[i, :, cut : cut + 128] = tail[mine].astype(BF16)


def hidden_kernel(in_ref, out_ref):
    blocks, _, units = out_ref.shape
    half = in_ref.shape[2] // 2
    sums = jnp.sum(in_ref[...].astype(F32), axis=0)
    power = jnp.sum(sums[:, units : units + 3], axis=1, keepdims=True) / D
    inv = lax.rsqrt(power + 1e-06)
    gate, upper = sums[:, :units] * inv, sums[:, half : half + units] * inv
    out = (gate / (1.0 + jnp.exp(-gate)) * upper).astype(BF16)
    for i in range(blocks):
        out_ref[i] = out


def down_kernel(h_ref, w_ref, wy_ref, out_ref):
    rows = out_ref.shape[1]
    each = out_ref.shape[0] // 2
    hi = lax.axis_index("hi")
    h = [jnp.concatenate([h_ref[i] for i in range(lo, h_ref.shape[0], 2)], axis=0) for lo in range(2)]
    for at, ref in ((hi, w_ref), (1 - hi, wy_ref)):
        y = jnp.dot(h[0], ref[0], preferred_element_type=F32) + jnp.dot(h[1], ref[1], preferred_element_type=F32)
        for k in range(each):
            out_ref[at * each + k] = y[k * rows : (k + 1) * rows].astype(BF16)


def per_device(
    queries,
    cache_keys,
    cache_values,
    seg_keys,
    seg_values,
    lengths,
    residual_stream,
    out_weight,
    norm_gain,
    gate_weight,
    up_weight,
    down_weight,
):
    rows, width = queries.shape
    _, stretch, head = cache_keys.shape
    group = width // head
    near_axes = ("lo", "hi")
    n_far, n_near, n_tp = lax.axis_size("far"), lax.axis_size(near_axes), lax.axis_size("tp")
    n_ctx = n_far * n_near
    ctx = ("far", *near_axes)
    tokens = rows * n_ctx
    trows = residual_stream.shape[0]
    feats = residual_stream.shape[1]
    units = gate_weight.shape[1] // n_near

    near = lax.axis_index(near_axes)

    def piece(w, lo, place):
        return lax.dynamic_slice_in_dim(w, (2 * lo + (place & 1)) * units, units, 0)

    def scaled(w, lo, place):
        return (piece(w.T, lo, place).astype(F32) * norm_gain).astype(BF16)

    def gate_0(place):
        return scaled(gate_weight, 0, place)

    def gate_1(place):
        return scaled(gate_weight, 1, place)

    def up_0(place):
        return scaled(up_weight, 0, place)

    def up_1(place):
        return scaled(up_weight, 1, place)

    def down_chunk(place):
        return jnp.stack([piece(down_weight, lo, place) for lo in range(2)])

    def trade(part):
        return lambda place: lax.ppermute(part(place ^ 1), "hi", [(0, 1), (1, 0)])

    place = near

    def beside(x, *trades):
        nonlocal place
        x, place, *sent = lax.optimization_barrier((x, place, *[t(place) for t in trades]))
        return x, *sent

    each = rows * group
    q_all = jnp.broadcast_to(queries.reshape(1, each, head), (n_ctx, each, head))
    q_all = lax.all_to_all(q_all, ctx, 0, 0, tiled=True)
    own_gate = jnp.stack([gate_0(near), gate_1(near)])
    own_up = jnp.stack([up_0(near), up_1(near)])
    own_gate, own_up, gate_y0, q_all, place = lax.optimization_barrier(
        (own_gate, own_up, trade(gate_0)(place), q_all, place)
    )
    vmem = pl.BlockSpec(memory_space=pltpu.VMEM)
    smem = pl.BlockSpec(memory_space=pltpu.SMEM)
    params = pltpu.CompilerParams(vmem_limit_bytes=40 * 2**20)
    small = pltpu.CompilerParams(vmem_limit_bytes=24 * 2**20)
    partial = pl.pallas_call(
        functools.partial(attend_kernel, tokens=tokens, group=group, head=head, scale=1.0 / math.sqrt(head)),
        out_shape=jax.ShapeDtypeStruct((n_ctx, each + 8, head), BF16),
        in_specs=[smem] + [vmem] * 5,
        out_specs=vmem,
        compiler_params=params,
        cost_estimate=pl.CostEstimate(
            flops=4 * tokens * width * stretch, bytes_accessed=2**21, transcendentals=tokens * group * stretch
        ),
        name="attend",
    )(lengths, q_all, cache_keys[0], cache_values[0], seg_keys, seg_values)
    parts = lax.all_to_all(partial, ctx, 0, 0, tiled=True)
    parts, up_y1 = beside(parts, trade(up_1))
    attention, copies = pl.pallas_call(
        merge_kernel,
        out_shape=(jax.ShapeDtypeStruct((each, head), BF16), jax.ShapeDtypeStruct((n_ctx, each, head), BF16)),
        in_specs=[vmem],
        out_specs=(vmem, vmem),
        compiler_params=small,
        name="merge",
    )(parts)
    attention = attention.reshape(rows, width)
    heads_all = lax.all_to_all(copies, ctx, 0, 0, tiled=True)
    heads_all, gate_y1 = beside(heads_all, trade(gate_1))
    mixed = pl.pallas_call(
        out_kernel,
        out_shape=jax.ShapeDtypeStruct((n_tp, trows, feats), BF16),
        in_specs=[vmem] * 2,
        out_specs=vmem,
        scratch_shapes=[pltpu.VMEM((tokens * group, head), F32)],
        compiler_params=small,
        name="out",
    )(heads_all, out_weight)
    mixed = lax.all_to_all(mixed, "tp", 0, 0, tiled=True)
    own, stream = pl.pallas_call(
        stream_kernel,
        out_shape=(
            jax.ShapeDtypeStruct((trows, feats), BF16),
            jax.ShapeDtypeStruct((2 * n_tp, trows, feats), BF16),
        ),
        in_specs=[vmem] * 2,
        out_specs=(vmem, vmem),
        compiler_params=small,
        name="stream",
    )(mixed, residual_stream)
    stream = lax.all_to_all(stream, ("hi", "tp"), 0, 0, tiled=True)
    stream, up_y0 = beside(stream, trade(up_0))

    half = -(-(units + 3) // 128) * 128
    block = tokens // n_far
    send, keep = pl.pallas_call(
        project_kernel,
        out_shape=(
            jax.ShapeDtypeStruct((tokens, 2 * half), BF16),
            jax.ShapeDtypeStruct((tokens, 2 * half), F32),
        ),
        in_specs=[vmem] * 7,
        out_specs=(vmem, vmem),
        compiler_params=small,
        name="project",
    )(stream, own_gate, gate_y0, gate_y1, own_up, up_y0, up_y1)
    got = lax.ppermute(send, "lo", [(0, 1), (1, 0)])
    sums = pl.pallas_call(
        functools.partial(join_kernel, units=units),
        out_shape=jax.ShapeDtypeStruct((n_far, block, 2 * half), BF16),
        in_specs=[vmem] * 2,
        out_specs=vmem,
        compiler_params=small,
        name="join",
    )(keep, got)
    sums, down_y = beside(lax.all_to_all(sums, "far", 0, 0, tiled=True), trade(down_chunk))
    hidden = pl.pallas_call(
        hidden_kernel,
        out_shape=jax.ShapeDtypeStruct((2 * n_far, block, units), BF16),
        in_specs=[vmem],
        out_specs=vmem,
        compiler_params=small,
        name="hidden",
    )(sums)
    hidden = lax.all_to_all(hidden, ("far", "lo"), 0, 0, tiled=True)
    lowered = pl.pallas_call(
        down_kernel,
        out_shape=jax.ShapeDtypeStruct((2 * n_tp, trows, feats), BF16),
        in_specs=[vmem] * 3,
        out_specs=vmem,
        compiler_params=small,
        name="down",
    )(hidden, down_chunk(near), down_y)
    lowered = lax.all_to_all(lowered, ("hi", "tp"), 0, 0, tiled=True)
    layer_out = pl.pallas_call(
        last_kernel,
        out_shape=jax.ShapeDtypeStruct((trows, feats), BF16),
        in_specs=[vmem] * 2,
        out_specs=vmem,
        compiler_params=small,
        name="last",
    )(lowered, own)
    return (attention, layer_out)


def solution(mesh):
    fine = jax.sharding.Mesh(mesh.devices.reshape(-1, 2, 2, mesh.shape["tp"]), ("far", "lo", "hi", "tp"))
    ctx = ("far", "lo", "hi")
    return jax.shard_map(
        per_device,
        mesh=fine,
        in_specs=(
            P(ctx, "tp"),
            P("tp", ctx, None),
            P("tp", ctx, None),
            P(ctx, "tp"),
            P(ctx, "tp"),
            P(ctx),
            P("tp", ctx),
            P("tp", ctx),
            P(ctx),
            P(ctx, "tp"),
            P(ctx, "tp"),
            P("tp", ctx),
        ),
        out_specs=(P(ctx, "tp"), P("tp", ctx)),
        check_vma=False,
    )
```

```python
import functools
import math

import jax
import jax.numpy as jnp
from jax import lax
from jax.experimental import pallas as pl
from jax.experimental.pallas import tpu as pltpu
from jax.sharding import PartitionSpec as P

D = 8192
F32 = jnp.float32
BF16 = jnp.bfloat16
LOW = float("-inf")


def three_parts(x):
    one = x.astype(BF16).astype(F32)
    rest = x - one
    two = rest.astype(BF16).astype(F32)
    return one, two, (rest - two).astype(BF16).astype(F32)


def attend_kernel(lengths, q_ref, k_ref, v_ref, sk_ref, sv_ref, out_ref, *, tokens, group, head, scale):
    length = lengths[0]
    rows = tokens * group
    own = sk_ref.shape[0]
    first = lax.axis_index(("far", "lo", "hi")) * own
    query = q_ref[...].reshape(rows, head)
    unit = scale / math.log(2.0)

    def scores(keys):
        return lax.dot_general(keys, query, (((1,), (1,)), ((), ())), preferred_element_type=F32)

    def weigh(values, w):
        return lax.dot_general(values, w.astype(BF16), (((0,), (0,)), ((), ())), preferred_element_type=F32)

    own_s = scores(sk_ref[...])
    token = lax.broadcasted_iota(jnp.int32, (own, rows), 1) // group
    seen = first + lax.broadcasted_iota(jnp.int32, (own, rows), 0) <= token
    own_s = jnp.where(seen, own_s, LOW)
    s = scores(k_ref[...])
    s = jnp.where(lax.broadcasted_iota(jnp.int32, s.shape, 0) < length, s, LOW)
    top = jnp.maximum(jnp.max(own_s, axis=0, keepdims=True), jnp.max(s, axis=0, keepdims=True))
    own_w = jnp.exp2((own_s - top) * unit)
    w = jnp.exp2((s - top) * unit)
    total = jnp.sum(own_w, axis=0, keepdims=True) + jnp.sum(w, axis=0, keepdims=True)
    numer = weigh(sv_ref[...], own_w) + weigh(v_ref[...], w)
    blocks = out_ref.shape[0]
    each = rows // blocks
    out_ref[:, :each, :] = (numer / total).T.astype(BF16).reshape(blocks, each, head)
    stats = jnp.concatenate([*three_parts(top * unit), *three_parts(total), jnp.zeros((2, rows), F32)], axis=0)
    stats = jnp.concatenate([stats, jnp.zeros((8, rows), F32)], axis=0)
    spare = jnp.zeros((out_ref.shape[1] - each, head - each), F32)
    for i in range(blocks):
        tail = stats[: out_ref.shape[1] - each, i * each : (i + 1) * each]
        out_ref[i, each:, :] = jnp.concatenate([tail, spare], axis=1).astype(BF16)


def merge_kernel(in_ref, out_ref, copies_ref):
    blocks, rows, head = copies_ref.shape
    stat = [in_ref[:, rows + i, :].astype(F32) for i in range(6)]
    top = stat[0] + stat[1] + stat[2]
    total = stat[3] + stat[4] + stat[5]
    w = jnp.exp2(top - jnp.max(top, axis=0, keepdims=True)) * total
    w = (w / jnp.sum(w, axis=0, keepdims=True)).T
    out = jnp.zeros((rows, head), F32)
    for i in range(blocks):
        out = out + in_ref[i, :rows, :].astype(F32) * w[:rows, i : i + 1]
    out = out.astype(BF16)
    out_ref[...] = out
    for i in range(blocks):
        copies_ref[i] = out


def out_kernel(h_ref, w_ref, out_ref, wide_ref):
    blocks, rows, _ = out_ref.shape
    tokens = blocks * rows
    head = h_ref.shape[2]
    group = w_ref.shape[0] // head
    wide_ref[...] = h_ref[...].astype(F32).reshape(tokens * group, head)
    y = 0.0
    for g in range(group):
        x = wide_ref[pl.ds(g, tokens, stride=group), :].astype(BF16)
        y = y + jnp.dot(x, w_ref[g * head : (g + 1) * head, :], preferred_element_type=F32)
    for i in range(blocks):
        out_ref[i] = y[i * rows : (i + 1) * rows].astype(BF16)


def stream_kernel(in_ref, residual_ref, own_ref, copies_ref):
    own = jnp.sum(in_ref[...].astype(F32), axis=0) + residual_ref[...].astype(F32)
    own = own.astype(BF16)
    own_ref[...] = own
    for i in range(copies_ref.shape[0]):
        copies_ref[i] = own


def last_kernel(in_ref, own_ref, out_ref):
    out_ref[...] = (own_ref[...].astype(F32) + jnp.sum(in_ref[...].astype(F32), axis=0)).astype(BF16)


def project_kernel(
    x_ref, gate_ref, gate_y0_ref, gate_y1_ref, up_ref, up_y0_ref, up_y1_ref, send_g_ref, send_u_ref, keep_ref
):
    units = gate_ref.shape[1]
    each = x_ref.shape[0] // 2
    half = keep_ref.shape[1] // 2
    lo, hi = lax.axis_index("lo"), lax.axis_index("hi")
    own, other = (
        jnp.concatenate([x_ref[at * each + i].astype(F32) for i in range(each)], axis=0) for at in (hi, 1 - hi)
    )
    squares = jnp.sum(own * own, axis=1, keepdims=True) + jnp.sum(other * other, axis=1, keepdims=True)
    parts = three_parts(squares)
    own, other = own.astype(BF16), other.astype(BF16)

    def product(w, w_y):
        y = lax.dot_general(own, w, (((1,), (1,)), ((), ())), preferred_element_type=F32)
        return y + lax.dot_general(other, w_y, (((1,), (1,)), ((), ())), preferred_element_type=F32)

    tokens = squares.shape[0]
    spare = half - units
    keep_refs = (keep_ref.at[:, :half], keep_ref.at[:, half:])
    for at, (g_ref, u_ref) in ((1 - lo, (send_g_ref, send_u_ref)), (lo, keep_refs)):
        gate = product(gate_ref[at], jnp.where(at == 0, gate_y0_ref[...], gate_y1_ref[...]))
        up = product(up_ref[at], jnp.where(at == 0, up_y0_ref[...], up_y1_ref[...]))
        g_ref[...] = jnp.concatenate([gate, *parts, jnp.zeros((tokens, spare - 3), F32)], axis=1).astype(g_ref.dtype)
        u_ref[...] = jnp.concatenate([up, jnp.zeros((tokens, spare), F32)], axis=1).astype(u_ref.dtype)


def join_kernel(keep_ref, got_g_ref, got_u_ref, out_ref, *, units):
    total = keep_ref[...] + jnp.concatenate([got_g_ref[...], got_u_ref[...]], axis=1).astype(F32)
    cut = units // 128 * 128
    at = units - cut
    tail = total[:, cut : cut + 128]
    one, two, three = three_parts(jnp.sum(tail[:, at : at + 3], axis=1, keepdims=True))
    column = lax.broadcasted_iota(jnp.int32, tail.shape, 1) - at
    tail = jnp.where(column == 0, one, jnp.where(column == 1, two, jnp.where(column == 2, three, tail)))
    blocks, rows, _ = out_ref.shape
    for i in range(blocks):
        mine = slice(i * rows, (i + 1) * rows)
        out_ref[i] = total[mine].astype(BF16)
        out_ref[i, :, cut : cut + 128] = tail[mine].astype(BF16)


def hidden_kernel(in_ref, out_ref):
    blocks, _, units = out_ref.shape
    half = in_ref.shape[2] // 2
    sums = jnp.sum(in_ref[...].astype(F32), axis=0)
    power = jnp.sum(sums[:, units : units + 3], axis=1, keepdims=True) / D
    inv = lax.rsqrt(power + 1e-06)
    gate, upper = sums[:, :units] * inv, sums[:, half : half + units] * inv
    out = (gate / (1.0 + jnp.exp(-gate)) * upper).astype(BF16)
    for i in range(blocks):
        out_ref[i] = out


def down_kernel(h_ref, w_ref, wy_ref, out_ref):
    rows = out_ref.shape[1]
    each = out_ref.shape[0] // 2
    hi = lax.axis_index("hi")
    h = [jnp.concatenate([h_ref[i] for i in range(lo, h_ref.shape[0], 2)], axis=0) for lo in range(2)]
    for at, ref in ((hi, w_ref), (1 - hi, wy_ref)):
        y = jnp.dot(h[0], ref[0], preferred_element_type=F32) + jnp.dot(h[1], ref[1], preferred_element_type=F32)
        for k in range(each):
            out_ref[at * each + k] = y[k * rows : (k + 1) * rows].astype(BF16)


def per_device(
    queries,
    cache_keys,
    cache_values,
    seg_keys,
    seg_values,
    lengths,
    residual_stream,
    out_weight,
    norm_gain,
    gate_weight,
    up_weight,
    down_weight,
):
    rows, width = queries.shape
    _, stretch, head = cache_keys.shape
    group = width // head
    near_axes = ("lo", "hi")
    n_far, n_near, n_tp = lax.axis_size("far"), lax.axis_size(near_axes), lax.axis_size("tp")
    n_ctx = n_far * n_near
    ctx = ("far", *near_axes)
    tokens = rows * n_ctx
    trows = residual_stream.shape[0]
    feats = residual_stream.shape[1]
    units = gate_weight.shape[1] // n_near

    near = lax.axis_index(near_axes)

    def piece(w, lo, place):
        return lax.dynamic_slice_in_dim(w, (2 * lo + (place & 1)) * units, units, 0)

    def scaled(w, lo, place):
        return (piece(w.T, lo, place).astype(F32) * norm_gain).astype(BF16)

    def gate_0(place):
        return scaled(gate_weight, 0, place)

    def gate_1(place):
        return scaled(gate_weight, 1, place)

    def up_0(place):
        return scaled(up_weight, 0, place)

    def up_1(place):
        return scaled(up_weight, 1, place)

    def down_chunk(place):
        return jnp.stack([piece(down_weight, lo, place) for lo in range(2)])

    def trade(part):
        return lambda place: lax.ppermute(part(place ^ 1), "hi", [(0, 1), (1, 0)])

    place = near

    def beside(x, *trades):
        nonlocal place
        x, place, *sent = lax.optimization_barrier((x, place, *[t(place) for t in trades]))
        return x, *sent

    each = rows * group
    q_all = jnp.broadcast_to(queries.reshape(1, each, head), (n_ctx, each, head))
    q_all = lax.all_to_all(q_all, ctx, 0, 0, tiled=True)
    own_gate = jnp.stack([gate_0(near), gate_1(near)])
    own_up = jnp.stack([up_0(near), up_1(near)])
    own_gate, own_up, gate_y0, q_all, place = lax.optimization_barrier(
        (own_gate, own_up, trade(gate_0)(place), q_all, place)
    )
    vmem = pl.BlockSpec(memory_space=pltpu.VMEM)
    smem = pl.BlockSpec(memory_space=pltpu.SMEM)
    params = pltpu.CompilerParams(vmem_limit_bytes=40 * 2**20)
    small = pltpu.CompilerParams(vmem_limit_bytes=24 * 2**20)
    partial = pl.pallas_call(
        functools.partial(attend_kernel, tokens=tokens, group=group, head=head, scale=1.0 / math.sqrt(head)),
        out_shape=jax.ShapeDtypeStruct((n_ctx, each + 8, head), BF16),
        in_specs=[smem] + [vmem] * 5,
        out_specs=vmem,
        compiler_params=params,
        cost_estimate=pl.CostEstimate(
            flops=4 * tokens * width * stretch, bytes_accessed=2**21, transcendentals=tokens * group * stretch
        ),
        name="attend",
    )(lengths, q_all, cache_keys[0], cache_values[0], seg_keys, seg_values)
    parts = lax.all_to_all(partial, ctx, 0, 0, tiled=True)
    parts, up_y1 = beside(parts, trade(up_1))
    attention, copies = pl.pallas_call(
        merge_kernel,
        out_shape=(jax.ShapeDtypeStruct((each, head), BF16), jax.ShapeDtypeStruct((n_ctx, each, head), BF16)),
        in_specs=[vmem],
        out_specs=(vmem, vmem),
        compiler_params=small,
        name="merge",
    )(parts)
    attention = attention.reshape(rows, width)
    heads_all = lax.all_to_all(copies, ctx, 0, 0, tiled=True)
    heads_all, gate_y1 = beside(heads_all, trade(gate_1))
    mixed = pl.pallas_call(
        out_kernel,
        out_shape=jax.ShapeDtypeStruct((n_tp, trows, feats), BF16),
        in_specs=[vmem] * 2,
        out_specs=vmem,
        scratch_shapes=[pltpu.VMEM((tokens * group, head), F32)],
        compiler_params=small,
        name="out",
    )(heads_all, out_weight)
    mixed = lax.all_to_all(mixed, "tp", 0, 0, tiled=True)
    own, stream = pl.pallas_call(
        stream_kernel,
        out_shape=(
            jax.ShapeDtypeStruct((trows, feats), BF16),
            jax.ShapeDtypeStruct((2 * n_tp, trows, feats), BF16),
        ),
        in_specs=[vmem] * 2,
        out_specs=(vmem, vmem),
        compiler_params=small,
        name="stream",
    )(mixed, residual_stream)
    stream = lax.all_to_all(stream, ("hi", "tp"), 0, 0, tiled=True)
    stream, up_y0 = beside(stream, trade(up_0))

    half = -(-(units + 3) // 128) * 128
    block = tokens // n_far
    send_g, send_u, keep = pl.pallas_call(
        project_kernel,
        out_shape=(
            jax.ShapeDtypeStruct((tokens, half), BF16),
            jax.ShapeDtypeStruct((tokens, half), BF16),
            jax.ShapeDtypeStruct((tokens, 2 * half), F32),
        ),
        in_specs=[vmem] * 7,
        out_specs=(vmem, vmem, vmem),
        compiler_params=small,
        name="project",
    )(stream, own_gate, gate_y0, gate_y1, own_up, up_y0, up_y1)
    n_z = 2 * n_far
    got_g = lax.ppermute(send_g, ("far", "lo"), [(z, z ^ 1) for z in range(n_z)])
    got_u = lax.ppermute(send_u, ("far", "lo"), [(z, (z + 2 * (z % 2) - 1) % n_z) for z in range(n_z)])
    sums = pl.pallas_call(
        functools.partial(join_kernel, units=units),
        out_shape=jax.ShapeDtypeStruct((n_far, block, 2 * half), BF16),
        in_specs=[vmem] * 3,
        out_specs=vmem,
        compiler_params=small,
        name="join",
    )(keep, got_g, got_u)
    sums, down_y = beside(lax.all_to_all(sums, "far", 0, 0, tiled=True), trade(down_chunk))
    hidden = pl.pallas_call(
        hidden_kernel,
        out_shape=jax.ShapeDtypeStruct((2 * n_far, block, units), BF16),
        in_specs=[vmem],
        out_specs=vmem,
        compiler_params=small,
        name="hidden",
    )(sums)
    hidden = lax.all_to_all(hidden, ("far", "lo"), 0, 0, tiled=True)
    lowered = pl.pallas_call(
        down_kernel,
        out_shape=jax.ShapeDtypeStruct((2 * n_tp, trows, feats), BF16),
        in_specs=[vmem] * 3,
        out_specs=vmem,
        compiler_params=small,
        name="down",
    )(hidden, down_chunk(near), down_y)
    lowered = lax.all_to_all(lowered, ("hi", "tp"), 0, 0, tiled=True)
    layer_out = pl.pallas_call(
        last_kernel,
        out_shape=jax.ShapeDtypeStruct((trows, feats), BF16),
        in_specs=[vmem] * 2,
        out_specs=vmem,
        compiler_params=small,
        name="last",
    )(lowered, own)
    return (attention, layer_out)


def solution(mesh):
    fine = jax.sharding.Mesh(mesh.devices.reshape(-1, 2, 2, mesh.shape["tp"]), ("far", "lo", "hi", "tp"))
    ctx = ("far", "lo", "hi")
    return jax.shard_map(
        per_device,
        mesh=fine,
        in_specs=(
            P(ctx, "tp"),
            P("tp", ctx, None),
            P("tp", ctx, None),
            P(ctx, "tp"),
            P(ctx, "tp"),
            P(ctx),
            P("tp", ctx),
            P("tp", ctx),
            P(ctx),
            P(ctx, "tp"),
            P(ctx, "tp"),
            P("tp", ctx),
        ),
        out_specs=(P(ctx, "tp"), P("tp", ctx)),
        check_vma=False,
    )
```

```python
import functools
import math

import jax
import jax.numpy as jnp
from jax import lax
from jax.experimental import pallas as pl
from jax.experimental.pallas import tpu as pltpu
from jax.sharding import PartitionSpec as P

D = 8192
F32 = jnp.float32
BF16 = jnp.bfloat16
LOW = float("-inf")


def three_parts(x):
    one = x.astype(BF16).astype(F32)
    rest = x - one
    two = rest.astype(BF16).astype(F32)
    return one, two, (rest - two).astype(BF16).astype(F32)


def attend_kernel(lengths, q_ref, k_ref, v_ref, sk_ref, sv_ref, out_ref, *, tokens, group, head, scale):
    length = lengths[0]
    rows = tokens * group
    own = sk_ref.shape[0]
    first = lax.axis_index(("far", "lo", "hi")) * own
    query = q_ref[...].reshape(rows, head)
    unit = scale / math.log(2.0)

    def scores(keys):
        return lax.dot_general(keys, query, (((1,), (1,)), ((), ())), preferred_element_type=F32)

    def weigh(values, w):
        return lax.dot_general(values, w.astype(BF16), (((0,), (0,)), ((), ())), preferred_element_type=F32)

    own_s = scores(sk_ref[...])
    token = lax.broadcasted_iota(jnp.int32, (own, rows), 1) // group
    seen = first + lax.broadcasted_iota(jnp.int32, (own, rows), 0) <= token
    own_s = jnp.where(seen, own_s, LOW)
    s = scores(k_ref[...])
    s = jnp.where(lax.broadcasted_iota(jnp.int32, s.shape, 0) < length, s, LOW)
    top = jnp.maximum(jnp.max(own_s, axis=0, keepdims=True), jnp.max(s, axis=0, keepdims=True))
    own_w = jnp.exp2((own_s - top) * unit)
    w = jnp.exp2((s - top) * unit)
    total = jnp.sum(own_w, axis=0, keepdims=True) + jnp.sum(w, axis=0, keepdims=True)
    numer = weigh(sv_ref[...], own_w) + weigh(v_ref[...], w)
    blocks = out_ref.shape[0]
    each = rows // blocks
    out_ref[:, :each, :] = (numer / total).T.astype(BF16).reshape(blocks, each, head)
    stats = jnp.concatenate([*three_parts(top * unit), *three_parts(total), jnp.zeros((2, rows), F32)], axis=0)
    stats = jnp.concatenate([stats, jnp.zeros((8, rows), F32)], axis=0)
    spare = jnp.zeros((out_ref.shape[1] - each, head - each), F32)
    for i in range(blocks):
        tail = stats[: out_ref.shape[1] - each, i * each : (i + 1) * each]
        out_ref[i, each:, :] = jnp.concatenate([tail, spare], axis=1).astype(BF16)


def merge_kernel(in_ref, out_ref, copies_ref, wide_ref):
    blocks, rows, head = copies_ref.shape
    stat = [in_ref[:, rows + i, :].astype(F32) for i in range(6)]
    top = stat[0] + stat[1] + stat[2]
    total = stat[3] + stat[4] + stat[5]
    w = jnp.exp2(top - jnp.max(top, axis=0, keepdims=True)) * total
    w = (w / jnp.sum(w, axis=0, keepdims=True)).T
    out = jnp.zeros((rows, head), F32)
    for i in range(blocks):
        out = out + in_ref[i, :rows, :].astype(F32) * w[:rows, i : i + 1]
    wide_ref[...] = out
    tokens = out_ref.shape[0]
    group = rows // tokens
    for g in range(group):
        out_ref[:, g * head : (g + 1) * head] = wide_ref[pl.ds(g, tokens, stride=group), :].astype(BF16)
    out = out.astype(BF16)
    for i in range(blocks):
        copies_ref[i] = out


def out_kernel(h_ref, w_ref, out_ref, wide_ref):
    blocks, rows, _ = out_ref.shape
    tokens = blocks * rows
    head = h_ref.shape[2]
    group = w_ref.shape[0] // head
    wide_ref[...] = h_ref[...].astype(F32).reshape(tokens * group, head)
    y = 0.0
    for g in range(group):
        x = wide_ref[pl.ds(g, tokens, stride=group), :].astype(BF16)
        y = y + jnp.dot(x, w_ref[g * head : (g + 1) * head, :], preferred_element_type=F32)
    for i in range(blocks):
        out_ref[i] = y[i * rows : (i + 1) * rows].astype(BF16)


def stream_kernel(in_ref, residual_ref, own_ref, copies_ref):
    own = jnp.sum(in_ref[...].astype(F32), axis=0) + residual_ref[...].astype(F32)
    own = own.astype(BF16)
    own_ref[...] = own
    for i in range(copies_ref.shape[0]):
        copies_ref[i] = own


def last_kernel(in_ref, own_ref, out_ref):
    out_ref[...] = (own_ref[...].astype(F32) + jnp.sum(in_ref[...].astype(F32), axis=0)).astype(BF16)


def project_kernel(
    x_ref, gate_ref, gate_y0_ref, gate_y1_ref, up_ref, up_y0_ref, up_y1_ref, send_g_ref, send_u_ref, keep_ref
):
    units = gate_ref.shape[1]
    each = x_ref.shape[0] // 2
    half = keep_ref.shape[1] // 2
    lo, hi = lax.axis_index("lo"), lax.axis_index("hi")
    own, other = (
        jnp.concatenate([x_ref[at * each + i].astype(F32) for i in range(each)], axis=0) for at in (hi, 1 - hi)
    )
    squares = jnp.sum(own * own, axis=1, keepdims=True) + jnp.sum(other * other, axis=1, keepdims=True)
    parts = three_parts(squares)
    own, other = own.astype(BF16), other.astype(BF16)

    def product(w, w_y):
        y = lax.dot_general(own, w, (((1,), (1,)), ((), ())), preferred_element_type=F32)
        return y + lax.dot_general(other, w_y, (((1,), (1,)), ((), ())), preferred_element_type=F32)

    tokens = squares.shape[0]
    spare = half - units
    keep_refs = (keep_ref.at[:, :half], keep_ref.at[:, half:])
    for at, (g_ref, u_ref) in ((1 - lo, (send_g_ref, send_u_ref)), (lo, keep_refs)):
        gate = product(gate_ref[at], jnp.where(at == 0, gate_y0_ref[...], gate_y1_ref[...]))
        up = product(up_ref[at], jnp.where(at == 0, up_y0_ref[...], up_y1_ref[...]))
        g_ref[...] = jnp.concatenate([gate, *parts, jnp.zeros((tokens, spare - 3), F32)], axis=1).astype(g_ref.dtype)
        u_ref[...] = jnp.concatenate([up, jnp.zeros((tokens, spare), F32)], axis=1).astype(u_ref.dtype)


def join_kernel(keep_ref, got_g_ref, got_u_ref, out_ref, *, units):
    total = keep_ref[...] + jnp.concatenate([got_g_ref[...], got_u_ref[...]], axis=1).astype(F32)
    cut = units // 128 * 128
    at = units - cut
    tail = total[:, cut : cut + 128]
    one, two, three = three_parts(jnp.sum(tail[:, at : at + 3], axis=1, keepdims=True))
    column = lax.broadcasted_iota(jnp.int32, tail.shape, 1) - at
    tail = jnp.where(column == 0, one, jnp.where(column == 1, two, jnp.where(column == 2, three, tail)))
    blocks, rows, _ = out_ref.shape
    for i in range(blocks):
        mine = slice(i * rows, (i + 1) * rows)
        out_ref[i] = total[mine].astype(BF16)
        out_ref[i, :, cut : cut + 128] = tail[mine].astype(BF16)


def hidden_kernel(in_ref, out_ref):
    blocks, _, units = out_ref.shape
    half = in_ref.shape[2] // 2
    sums = jnp.sum(in_ref[...].astype(F32), axis=0)
    power = jnp.sum(sums[:, units : units + 3], axis=1, keepdims=True) / D
    inv = lax.rsqrt(power + 1e-06)
    gate, upper = sums[:, :units] * inv, sums[:, half : half + units] * inv
    out = (gate / (1.0 + jnp.exp(-gate)) * upper).astype(BF16)
    for i in range(blocks):
        out_ref[i] = out


def down_kernel(h_ref, w_ref, wy_ref, out_ref):
    rows = out_ref.shape[1]
    each = out_ref.shape[0] // 2
    hi = lax.axis_index("hi")
    h = [jnp.concatenate([h_ref[i] for i in range(lo, h_ref.shape[0], 2)], axis=0) for lo in range(2)]
    for at, ref in ((hi, w_ref), (1 - hi, wy_ref)):
        y = jnp.dot(h[0], ref[0], preferred_element_type=F32) + jnp.dot(h[1], ref[1], preferred_element_type=F32)
        for k in range(each):
            out_ref[at * each + k] = y[k * rows : (k + 1) * rows].astype(BF16)


def per_device(
    queries,
    cache_keys,
    cache_values,
    seg_keys,
    seg_values,
    lengths,
    residual_stream,
    out_weight,
    norm_gain,
    gate_weight,
    up_weight,
    down_weight,
):
    rows, width = queries.shape
    _, stretch, head = cache_keys.shape
    group = width // head
    near_axes = ("lo", "hi")
    n_far, n_near, n_tp = lax.axis_size("far"), lax.axis_size(near_axes), lax.axis_size("tp")
    n_ctx = n_far * n_near
    ctx = ("far", *near_axes)
    tokens = rows * n_ctx
    trows = residual_stream.shape[0]
    feats = residual_stream.shape[1]
    units = gate_weight.shape[1] // n_near

    near = lax.axis_index(near_axes)

    def piece(w, lo, place):
        return lax.dynamic_slice_in_dim(w, (2 * lo + (place & 1)) * units, units, 0)

    def scaled(w, lo, place):
        return (piece(w.T, lo, place).astype(F32) * norm_gain).astype(BF16)

    def gate_0(place):
        return scaled(gate_weight, 0, place)

    def gate_1(place):
        return scaled(gate_weight, 1, place)

    def up_0(place):
        return scaled(up_weight, 0, place)

    def up_1(place):
        return scaled(up_weight, 1, place)

    def down_chunk(place):
        return jnp.stack([piece(down_weight, lo, place) for lo in range(2)])

    def trade(part):
        return lambda place: lax.ppermute(part(place ^ 1), "hi", [(0, 1), (1, 0)])

    place = near

    def beside(x, *trades):
        nonlocal place
        x, place, *sent = lax.optimization_barrier((x, place, *[t(place) for t in trades]))
        return x, *sent

    each = rows * group
    q_all = jnp.broadcast_to(queries.reshape(1, each, head), (n_ctx, each, head))
    q_all = lax.all_to_all(q_all, ctx, 0, 0, tiled=True)
    own_gate = jnp.stack([gate_0(near), gate_1(near)])
    own_up = jnp.stack([up_0(near), up_1(near)])
    own_gate, own_up, gate_y0, q_all, place = lax.optimization_barrier(
        (own_gate, own_up, trade(gate_0)(place), q_all, place)
    )
    vmem = pl.BlockSpec(memory_space=pltpu.VMEM)
    smem = pl.BlockSpec(memory_space=pltpu.SMEM)
    params = pltpu.CompilerParams(vmem_limit_bytes=40 * 2**20)
    small = pltpu.CompilerParams(vmem_limit_bytes=24 * 2**20)
    partial = pl.pallas_call(
        functools.partial(attend_kernel, tokens=tokens, group=group, head=head, scale=1.0 / math.sqrt(head)),
        out_shape=jax.ShapeDtypeStruct((n_ctx, each + 8, head), BF16),
        in_specs=[smem] + [vmem] * 5,
        out_specs=vmem,
        compiler_params=params,
        cost_estimate=pl.CostEstimate(
            flops=4 * tokens * width * stretch, bytes_accessed=2**21, transcendentals=tokens * group * stretch
        ),
        name="attend",
    )(lengths, q_all, cache_keys[0], cache_values[0], seg_keys, seg_values)
    parts = lax.all_to_all(partial, ctx, 0, 0, tiled=True)
    parts, up_y1 = beside(parts, trade(up_1))
    attention, copies = pl.pallas_call(
        merge_kernel,
        out_shape=(jax.ShapeDtypeStruct((rows, width), BF16), jax.ShapeDtypeStruct((n_ctx, each, head), BF16)),
        in_specs=[vmem],
        out_specs=(vmem, vmem),
        scratch_shapes=[pltpu.VMEM((each, head), F32)],
        compiler_params=small,
        name="merge",
    )(parts)
    heads_all = lax.all_to_all(copies, ctx, 0, 0, tiled=True)
    heads_all, gate_y1 = beside(heads_all, trade(gate_1))
    mixed = pl.pallas_call(
        out_kernel,
        out_shape=jax.ShapeDtypeStruct((n_tp, trows, feats), BF16),
        in_specs=[vmem] * 2,
        out_specs=vmem,
        scratch_shapes=[pltpu.VMEM((tokens * group, head), F32)],
        compiler_params=small,
        name="out",
    )(heads_all, out_weight)
    mixed = lax.all_to_all(mixed, "tp", 0, 0, tiled=True)
    own, stream = pl.pallas_call(
        stream_kernel,
        out_shape=(
            jax.ShapeDtypeStruct((trows, feats), BF16),
            jax.ShapeDtypeStruct((2 * n_tp, trows, feats), BF16),
        ),
        in_specs=[vmem] * 2,
        out_specs=(vmem, vmem),
        compiler_params=small,
        name="stream",
    )(mixed, residual_stream)
    stream = lax.all_to_all(stream, ("hi", "tp"), 0, 0, tiled=True)
    stream, up_y0 = beside(stream, trade(up_0))

    half = -(-(units + 3) // 128) * 128
    block = tokens // n_far
    send_g, send_u, keep = pl.pallas_call(
        project_kernel,
        out_shape=(
            jax.ShapeDtypeStruct((tokens, half), BF16),
            jax.ShapeDtypeStruct((tokens, half), BF16),
            jax.ShapeDtypeStruct((tokens, 2 * half), F32),
        ),
        in_specs=[vmem] * 7,
        out_specs=(vmem, vmem, vmem),
        compiler_params=small,
        name="project",
    )(stream, own_gate, gate_y0, gate_y1, own_up, up_y0, up_y1)
    n_z = 2 * n_far
    got_g = lax.ppermute(send_g, ("far", "lo"), [(z, z ^ 1) for z in range(n_z)])
    got_u = lax.ppermute(send_u, ("far", "lo"), [(z, (z + 2 * (z % 2) - 1) % n_z) for z in range(n_z)])
    sums = pl.pallas_call(
        functools.partial(join_kernel, units=units),
        out_shape=jax.ShapeDtypeStruct((n_far, block, 2 * half), BF16),
        in_specs=[vmem] * 3,
        out_specs=vmem,
        compiler_params=small,
        name="join",
    )(keep, got_g, got_u)
    sums, down_y, own_down = beside(
        lax.all_to_all(sums, "far", 0, 0, tiled=True), trade(down_chunk), lambda place: down_chunk(place)
    )
    hidden = pl.pallas_call(
        hidden_kernel,
        out_shape=jax.ShapeDtypeStruct((2 * n_far, block, units), BF16),
        in_specs=[vmem],
        out_specs=vmem,
        compiler_params=small,
        name="hidden",
    )(sums)
    hidden = lax.all_to_all(hidden, ("far", "lo"), 0, 0, tiled=True)
    lowered = pl.pallas_call(
        down_kernel,
        out_shape=jax.ShapeDtypeStruct((2 * n_tp, trows, feats), BF16),
        in_specs=[vmem] * 3,
        out_specs=vmem,
        compiler_params=small,
        name="down",
    )(hidden, own_down, down_y)
    lowered = lax.all_to_all(lowered, ("hi", "tp"), 0, 0, tiled=True)
    layer_out = pl.pallas_call(
        last_kernel,
        out_shape=jax.ShapeDtypeStruct((trows, feats), BF16),
        in_specs=[vmem] * 2,
        out_specs=vmem,
        compiler_params=small,
        name="last",
    )(lowered, own)
    return (attention, layer_out)


def solution(mesh):
    fine = jax.sharding.Mesh(mesh.devices.reshape(-1, 2, 2, mesh.shape["tp"]), ("far", "lo", "hi", "tp"))
    ctx = ("far", "lo", "hi")
    return jax.shard_map(
        per_device,
        mesh=fine,
        in_specs=(
            P(ctx, "tp"),
            P("tp", ctx, None),
            P("tp", ctx, None),
            P(ctx, "tp"),
            P(ctx, "tp"),
            P(ctx),
            P("tp", ctx),
            P("tp", ctx),
            P(ctx),
            P(ctx, "tp"),
            P(ctx, "tp"),
            P("tp", ctx),
        ),
        out_specs=(P(ctx, "tp"), P("tp", ctx)),
        check_vma=False,
    )
```
